32 devices in a mesh: seq: 32 (over z, y, x, core).
Axes of the slice: x: 2, y: 2, z: 4, core: 2. Of those that a mesh axis runs over, the one named last changes fastest.
Arguments:
- inputs: bfloat16 [16384, 768], P('seq'), may hold values from -6 to 6
- segment_ids: int32 [32, 512], P('seq'), may hold values from 0 to 3, never falling along the last dimension, each value on 1 to 256 neighbouring positions
- routes: int32 [16384, 1], P('seq'), may hold values from 0 to 31
- cotangent: bfloat16 [16384, 768], P('seq'), may hold values from -6 to 6
- gain_attn: float32 [768], P('seq'), may hold values from 0.1 to 1.9
- gain_ffn: float32 [768], P('seq'), may hold values from 0.1 to 1.9
- bias_table: float32 [384], P('seq'), may hold values from -4 to 4
- w_query: float32 [768, 768], P('seq'), may hold values from -0.21875 to 0.21875
- w_key: float32 [768, 768], P('seq'), may hold values from -0.21875 to 0.21875
- w_value: float32 [768, 768], P('seq'), may hold values from -0.21875 to 0.21875
- w_output: float32 [768, 768], P('seq'), may hold values from -2.5 to 2.5
- w_router: float32 [768, 32], P('seq'), may hold values from -0.108 to 0.108
- w_in: float32 [32, 768, 3072], P('seq'), may hold values from -0.21875 to 0.21875
- w_out: float32 [32, 3072, 768], P('seq'), may hold values from -3.4641016 to 3.4641016
Outputs:
- outputs: bfloat16 [16384, 768], P('seq')
- grad_inputs: bfloat16 [16384, 768], P('seq')
- grad_gain_attn: float32 [768], P('seq')
- grad_gain_ffn: float32 [768], P('seq')
- grad_bias_table: float32 [384], P('seq')
- grad_w_query: float32 [768, 768], P('seq')
- grad_w_key: float32 [768, 768], P('seq')
- grad_w_value: float32 [768, 768], P('seq')
- grad_w_output: float32 [768, 768], P('seq')
- grad_w_router: float32 [768, 32], P('seq')
- grad_w_in: float32 [32, 768, 3072], P('seq')
- grad_w_out: float32 [32, 3072, 768], P('seq')
The draws below stay inside these ranges and needn't reach their ends.
Inputs may be any that keep to these rules, and one draw needn't show every extreme that they name: `segment_ids`: along each packed row of 512 positions the ids never fall.
All inputs are finite; a program needn't handle non-finite values.
Results may differ from the reference program's by a relative error of at most 0.017.
The reference program's roundings to bfloat16 on the way count: a program that leaves them out, or rounds other values in their place, can miss the bound.
Values may be sent and summed in bfloat16 or wider, within the bound.
No kernel may reach another device: no remote copies, remote signals or barrier semaphores. Data moves between devices by JAX's collectives and lax.ppermute only.
A program may use at most 256 MiB of HBM per device.

```python
import math
import jax
import jax.numpy as jnp
import numpy as np
from jax import lax

D = 768
HEADS = 12
HEAD_DIM = 64
FF = 3072
BUCKETS = 32
SEQLEN = 512
SEQ_DEV = 1
EXPERTS = 32
TOK_DEV = 512
ROWS = 32
TOKENS = 16384
CAP = 20
N_SEQ = 32


def with_spikes(values, key, source, target, parts, factor):
    owner, partner = [(jnp.arange(values.shape[axis_at]) // (values.shape[axis_at] // parts)).reshape([-1 if axis == axis_at else 1 for axis in range(values.ndim)]) for axis_at in (source, target)]
    chosen = jax.random.permutation(key, parts)[partner]
    strong = (owner == chosen) | (owner == (partner + parts // 2) % parts)
    return jnp.where(strong, factor * values, values)


def block_scale(own_key, extent, shards, smallest, high):
    factor_of, own = 1.0, jax.random.fold_in(own_key, 6)
    for axis_at, blocks in shards:
        steps = jnp.exp(jax.random.uniform(jax.random.fold_in(own, axis_at), (blocks,), jnp.float32, smallest / len(shards), high / len(shards)))
        factor_of = factor_of * jnp.repeat(steps, extent[axis_at] // blocks).reshape([-1 if axis == axis_at else 1 for axis in range(len(extent))])
    return factor_of


def distinct(rng, rows, count, top, lift):
    ranking = jax.random.permutation(jax.random.fold_in(rng, 1), count)
    boost = ranking
    for power in range(3):
        boost = boost * boost // count
    boost = boost * lift // count
    tickets = jax.random.randint(jax.random.fold_in(rng, 2), (rows, count), 0, 4096) + boost
    holders = jax.random.permutation(jax.random.fold_in(rng, 3), rows)[jnp.arange(count) % rows]
    tickets = jnp.where(jnp.arange(rows)[:, None] == holders[None, :], 1 << 14, tickets)
    priority = tickets * count + jnp.arange(count)
    return lax.top_k(priority.astype(jnp.int32), top)[1].astype(jnp.int32)


def split_up(count, total, reach, lean):
    portions = [(1 << 20) // math.isqrt(grade ** lean) + 1 for grade in range(2, count + 1)]
    rest, counts = total - reach - (count - 1), [1] * (count - 1)
    while rest > 0:
        movable = [i for i in range(count - 1) if counts[i] < reach]
        pool, budget = sum([portions[i] for i in movable]), rest
        for i in movable:
            extra = min(reach - counts[i], max(1, budget * portions[i] // pool), rest)
            counts[i] = counts[i] + extra
            rest = rest - extra
    return np.array([reach] + counts)


def uneven_parts(own_key, number_of, total, most, lean):
    if number_of == 2:
        one = jax.random.randint(own_key, (), max(1, total - most), min(most, total - 1) + 1)
        return jnp.stack([one, total - one])
    lengths = jnp.asarray(split_up(number_of, total, most, lean), jnp.int32)
    twos = (number_of - 1) // 2
    source_of, taker = lengths[1:1 + 2 * twos:2], lengths[2:2 + 2 * twos:2]
    slack = jnp.minimum(source_of - 1, most - taker)
    shifted = jax.random.randint(jax.random.fold_in(own_key, 1), (twos,), 0, 1 << 20) % (slack + 1)
    lengths = lengths.at[1:1 + 2 * twos:2].set(source_of - shifted).at[2:2 + 2 * twos:2].set(taker + shifted)
    return lengths[jax.random.permutation(jax.random.fold_in(own_key, 2), number_of)]


def scatter_about(stream_key, extent, width, limit, split=(), kind=jnp.bfloat16):
    drawn = jax.random.normal(stream_key, extent, jnp.float32) * width
    if len(split) > 0:
        drawn = block_scale(stream_key, extent, split, -0.22, 0.18) * drawn
    return jnp.clip(drawn, min=-limit, max=limit).astype(kind)


def noise_with(rng, extent, scale, most, split, heavy, held_as=jnp.bfloat16):
    drawn = scale * jax.random.normal(rng, extent, jnp.float32)
    if split:
        drawn = drawn * block_scale(rng, extent, split, -0.22, 0.18)
    return jnp.clip(with_spikes(drawn, jax.random.fold_in(rng, 3), *heavy), -most, most).astype(held_as)


def setup_inputs(seed: int = 0) -> dict:
    key_list = jax.random.split(jax.random.key(seed), 15)
    inputs = noise_with(key_list[0], (TOKENS, D), 1.0, 6.0, ((0, 32),), (0, 1, 32, 2.75))
    segment_ids = jax.vmap(lambda own: jnp.searchsorted(jnp.cumsum(uneven_parts(own, 4, SEQLEN, SEQLEN // 2, 0)), jnp.arange(SEQLEN), side="right"))(jax.random.split(key_list[1], ROWS)).reshape((ROWS, SEQLEN)).astype(jnp.int32)
    routes = distinct(key_list[2], TOKENS, EXPERTS, 1, 256)
    cotangent = scatter_about(key_list[3], (TOKENS, D), 1.0, 6.0, ((0, 32),))
    gain_attn = jnp.clip(1.0 + 0.18 * jax.random.normal(key_list[4], (D,), jnp.float32), 0.1, 1.9)
    gain_ffn = jnp.clip(1.0 + 0.18 * jax.random.normal(key_list[5], (D,), jnp.float32), 0.1, 1.9)
    bias_table = scatter_about(key_list[6], (BUCKETS * HEADS,), 1.0, 4.0, ((0, 32),), jnp.float32)
    w_query = scatter_about(key_list[7], (D, D), D ** -0.5, 0.21875, ((0, 32),), jnp.float32)
    w_key = scatter_about(key_list[8], (D, D), D ** -0.5, 0.21875, ((0, 32),), jnp.float32)
    w_value = scatter_about(key_list[9], (D, D), D ** -0.5, 0.21875, ((0, 32),), jnp.float32)
    w_output = scatter_about(key_list[10], (D, D), (max(1, 4 * D // SEQLEN)) ** -0.5, 2.5, ((0, 32),), jnp.float32)
    w_router = scatter_about(key_list[11], (D, EXPERTS), 0.018, 0.108, ((0, 32),), jnp.float32)
    w_in = scatter_about(key_list[12], (EXPERTS, D, FF), D ** -0.5, 0.21875, ((0, 32),), jnp.float32)
    w_out = scatter_about(key_list[13], (EXPERTS, FF, D), (EXPERTS * FF ** -0.5), 3.4641016, ((0, 32),), jnp.float32)
    return dict(inputs=inputs, segment_ids=segment_ids, routes=routes, cotangent=cotangent, gain_attn=gain_attn, gain_ffn=gain_ffn, bias_table=bias_table, w_query=w_query, w_key=w_key, w_value=w_value, w_output=w_output, w_router=w_router, w_in=w_in, w_out=w_out)


epsilon = 1e-06
bucket_edges = (1, 2, 3, 4, 5, 6, 7, 8, 12, 16, 23, 32, 46, 64, 91)
highest = lax.Precision.HIGHEST
gelu_coef = 0.7978845608028654
cubic_coef = 0.044715

@jax.custom_vjp
def low(v):
    return lax.optimization_barrier(v.astype(jnp.bfloat16)).astype(jnp.float32)

@jax.custom_vjp
def low_back(v):
    return v

def low_keep(v):
    return (low(v), None)

def low_pass(kept, grad):
    return (grad,)

def back_keep(v):
    return (v, None)

def back_low(kept, grad):
    return (low(grad),)
low.defvjp(low_keep, low_pass)
low_back.defvjp(back_keep, back_low)

def gelu_tanh(values):
    return 0.5 * values * (1.0 + jnp.tanh(gelu_coef * (values + cubic_coef * values * values * values)))

def exact_dot(left, right):
    return jnp.dot(left, right, precision=highest, preferred_element_type=jnp.float32)

def rms_norm(values, gain_vec):
    return values * lax.rsqrt(lax.optimization_barrier(jnp.mean(values * values, axis=-1, keepdims=True)) + epsilon) * gain_vec

def relative_buckets(length):
    places = jnp.arange(length, dtype=jnp.int32)
    offset = places[None, :] - places[:, None]
    magnitude = jnp.abs(offset)
    bucket = jnp.zeros((length, length), jnp.int32)
    for edge_value in bucket_edges:
        bucket = bucket + (magnitude >= edge_value).astype(jnp.int32)
    return (bucket + BUCKETS // 2 * (offset > 0).astype(jnp.int32)).astype(jnp.int32)

def reference(inputs, segment_ids, routes, cotangent, gain_attn, gain_ffn, bias_table, w_query, w_key, w_value, w_output, w_router, w_in, w_out):
    score_scale = HEAD_DIM ** (-0.5)
    bucket = relative_buckets(SEQLEN)
    route_ids = routes[:, 0].astype(jnp.int32)
    grouped = route_ids.reshape(N_SEQ, TOK_DEV)
    chosen = (grouped[:, :, None] == jnp.arange(EXPERTS, dtype=jnp.int32)[None, None, :]).astype(jnp.int32)
    running = jnp.cumsum(chosen, axis=1, dtype=jnp.int32)
    position = (lax.optimization_barrier(jnp.sum(running * chosen, axis=2, dtype=jnp.int32)) - 1).astype(jnp.int32)
    group_ids = jnp.arange(N_SEQ, dtype=jnp.int32)[:, None]
    slot_count = EXPERTS * N_SEQ * CAP
    slot_place = (grouped * (N_SEQ * CAP) + group_ids * CAP + position).astype(jnp.int32)
    target = jnp.where(position < CAP, slot_place, jnp.int32(slot_count)).reshape(TOKENS).astype(jnp.int32)
    source = jnp.full((slot_count + 1,), TOKENS, jnp.int32).at[target].set(jnp.arange(TOKENS, dtype=jnp.int32))[:slot_count]

    def forward(tokens_in, gain_one, gain_two, table, query_w, key_w, value_w, output_w, router_w, inner_w, outer_w):
        gain_one = low(gain_one)
        gain_two = low(gain_two)
        query_w = low(query_w)
        key_w = low(key_w)
        value_w = low(value_w)
        output_w = low(output_w)
        router_w = low(router_w)
        table_low = low(table).reshape(BUCKETS, HEADS)
        score_bias = jnp.transpose(table_low[bucket], (2, 0, 1))

        def attend(pieces):
            block_tokens, block_segments = pieces
            normed = low(rms_norm(block_tokens, gain_one))
            query = low_back(low(exact_dot(normed, query_w))).reshape(SEQ_DEV, SEQLEN, HEADS, HEAD_DIM)
            key_rows = low_back(low(exact_dot(normed, key_w))).reshape(SEQ_DEV, SEQLEN, HEADS, HEAD_DIM)
            value_rows = low_back(low(exact_dot(normed, value_w))).reshape(SEQ_DEV, SEQLEN, HEADS, HEAD_DIM)
            scores = jnp.einsum('sqhd,skhd->shqk', query, key_rows, precision=highest) * score_scale + score_bias[None]
            same_doc = block_segments[:, :, None] == block_segments[:, None, :]
            scores = low_back(jnp.where(same_doc[:, None], scores, -1000000000.0))
            attn_probs = jax.nn.softmax(scores, axis=-1)
            mixed = jnp.einsum('shqk,skhd->sqhd', low(attn_probs), value_rows, precision=highest).reshape(TOK_DEV, D)
            mixed = low_back(low(mixed))
            return block_tokens + low_back(exact_dot(mixed, output_w))
        after_attn = lax.map(jax.checkpoint(attend), (tokens_in.reshape(N_SEQ, TOK_DEV, D), segment_ids.reshape(N_SEQ, SEQ_DEV, SEQLEN)))
        after_attn = after_attn.reshape(TOKENS, D)
        normed_two = low(rms_norm(after_attn, gain_two))
        logits = low_back(exact_dot(normed_two, router_w))
        router_probs = jax.nn.softmax(logits, axis=-1)
        gate_prob = jnp.take_along_axis(router_probs, routes.astype(jnp.int32), axis=1)[:, 0]
        padded = jnp.concatenate([normed_two, jnp.zeros((1, D), jnp.float32)], axis=0)
        expert_in = low_back(padded[source]).reshape(EXPERTS, N_SEQ * CAP, D)

        def expert(pieces):
            rows_in, inner, outer = pieces
            pre_act = low_back(exact_dot(rows_in, low(inner)))
            hidden = low(gelu_tanh(pre_act))
            return low_back(low(exact_dot(hidden, low(outer))))
        expert_out = lax.map(jax.checkpoint(expert), (expert_in, inner_w, outer_w)).reshape(slot_count, D)
        expert_out = jnp.concatenate([expert_out, jnp.zeros((1, D), jnp.float32)], axis=0)
        return after_attn + gate_prob[:, None] * expert_out[target]
    primals = (inputs.astype(jnp.float32), gain_attn, gain_ffn, bias_table, w_query, w_key, w_value, w_output, w_router, w_in, w_out)
    result, pullback = jax.vjp(forward, *primals)
    gradients = pullback(cotangent.astype(jnp.float32))
    return (result.astype(jnp.bfloat16), gradients[0].astype(jnp.bfloat16), gradients[1], gradients[2], gradients[3], gradients[4], gradients[5], gradients[6], gradients[7], gradients[8], gradients[9], gradients[10])
```

```python
import functools

import jax
import jax.numpy as jnp
import numpy as np
from jax import lax
from jax.experimental import pallas as pl
from jax.experimental.pallas import tpu as pltpu
from jax.sharding import PartitionSpec as P

HEADS = 12
HEAD_DIM = 64
BUCKETS = 32
GROUPS = 3
LANES = 128

epsilon = 1e-06
bucket_edges = (1, 2, 3, 4, 5, 6, 7, 8, 12, 16, 23, 32, 46, 64, 91)
gelu_coef = 0.7978845608028654
cubic_coef = 0.044715

f32 = jnp.float32
bf16 = jnp.bfloat16


def bit_groups(count):
    bits = count.bit_length() - 1
    groups, low = [(0, 1)], 1
    while low < bits:
        width = min(2, bits - low)
        groups.append((low, width))
        low += width
    return groups


def relative_order(count):
    order = [0]
    for low, width in bit_groups(count):
        order = [base + (m << low) for base in order for m in range(1 << width)]
    return order


def swap(values, distance, count):
    return lax.ppermute(values, "seq", [(i, i ^ distance) for i in range(count)])


def gather_relative(shard, count):
    held = shard
    for low, width in reversed(bit_groups(count)[1:]):
        held = jnp.concatenate(
            [held] + [swap(held, m << low, count) for m in range(1, 1 << width)], axis=0
        )
    return held, swap(held, 1, count)


def scatter_relative(keep, send, count):
    total = keep + swap(send, 1, count).astype(f32)
    for low, width in bit_groups(count)[1:]:
        part = total.shape[0] >> width
        pieces = [total[m * part : (m + 1) * part] for m in range(1 << width)]
        total = pieces[0]
        for m in range(1, 1 << width):
            total = total + swap(pieces[m].astype(bf16), m << low, count).astype(f32)
    return total


def mm(left, right):
    return jnp.dot(left, right, preferred_element_type=f32)


def mm_nt(left, right):
    return lax.dot_general(left, right, (((1,), (1,)), ((), ())), preferred_element_type=f32)


def mm_tn(left, right):
    return lax.dot_general(left, right, (((0,), (0,)), ((), ())), preferred_element_type=f32)


def split_two(values):
    high = values.astype(bf16)
    return high, (values - high.astype(f32)).astype(bf16)


def kernel_call(body, outs, scratch=(), grid=None, in_specs=None, out_specs=None, flops=0, nbytes=0, vmem=48):
    extra = {}
    if grid is not None:
        extra = dict(grid=grid, in_specs=in_specs, out_specs=out_specs)
    return pl.pallas_call(
        body,
        out_shape=[jax.ShapeDtypeStruct(s, d) for s, d in outs],
        scratch_shapes=list(scratch),
        compiler_params=pltpu.CompilerParams(vmem_limit_bytes=vmem * 1024 * 1024),
        cost_estimate=pl.CostEstimate(flops=flops, bytes_accessed=nbytes, transcendentals=0),
        **extra,
    )


def to_slab(values, stage, out_ref):
    slots, width = values.shape
    blocks = width // LANES
    for c in range(blocks):
        stage[pl.ds(c, slots, stride=blocks), :] = values[:, c * LANES : (c + 1) * LANES]
    out_ref[...] = stage[...].astype(out_ref.dtype)


def from_slab(in_ref, stage, slots, put):
    stage[...] = in_ref[...].astype(f32)
    blocks = in_ref.shape[0] // slots
    for c in range(blocks):
        put(c, stage[pl.ds(c, slots, stride=blocks), :])


def to_column(row, width=LANES):
    return jnp.transpose(jnp.broadcast_to(row, (width, row.shape[1])))


def inverse_rms(values):
    return lax.rsqrt(jnp.mean(values * values, axis=-1, keepdims=True) + epsilon)


def buckets_of(offset):
    magnitude = jnp.abs(offset)
    bucket = jnp.zeros(offset.shape, jnp.int32)
    for edge in bucket_edges:
        bucket = bucket + (magnitude >= edge).astype(jnp.int32)
    return bucket + BUCKETS // 2 * (offset > 0).astype(jnp.int32)


def prepare_kernel(
    rows_local, entries, experts, capacity,
    me_ref, rel_ref, off_ref, x_ref, seg_ref, routes_ref, cot_ref,
    perm_ref, xperm_ref, segcol_ref, hmask_ref, umask_ref, dt_ref, dm_ref, cot_send_ref,
    stage,
):
    tokens, width = x_ref.shape
    slots = dm_ref.shape[0]
    me = me_ref[0]
    device_row = rel_ref[...] ^ me
    off_row = off_ref[...]
    true_row = device_row * rows_local + off_row
    perm = (lax.broadcasted_iota(jnp.int32, (width, width), 0) == true_row).astype(f32).astype(bf16)
    perm_ref[...] = perm
    xperm_ref[...] = mm(x_ref[...], perm).astype(bf16)
    segcol_ref[...] = to_column(seg_ref[...].astype(f32))
    flat = device_row * entries + off_row
    bucket_row = ((flat.astype(f32) + 0.5) * (1.0 / HEADS)).astype(jnp.int32)
    head_row = jnp.where(off_row < entries, flat - bucket_row * HEADS, -1)
    bucket_col = to_column(bucket_row.astype(f32))
    head_col = to_column(head_row.astype(f32))
    lane = lax.broadcasted_iota(jnp.int32, (width, LANES), 1).astype(f32)
    hmask_ref[...] = (head_col == lane).astype(f32).astype(bf16)
    umask_ref[...] = (bucket_col == lane).astype(f32).astype(bf16)
    routes = routes_ref[...]
    labels = lax.broadcasted_iota(jnp.int32, (tokens, experts), 1)
    picked = (routes == labels).astype(f32)
    earlier = (
        lax.broadcasted_iota(jnp.int32, (tokens, tokens), 1)
        <= lax.broadcasted_iota(jnp.int32, (tokens, tokens), 0)
    ).astype(f32).astype(bf16)
    counts = mm(earlier, picked.astype(bf16))
    position = jnp.sum(counts * picked, axis=1, keepdims=True) - 1.0
    slot_col = jnp.where(
        position < capacity, routes.astype(f32) * capacity + position, -1.0
    )
    slot_lane = lax.broadcasted_iota(jnp.int32, (tokens, slots), 1).astype(f32)
    dt_ref[...] = (slot_col == slot_lane).astype(f32).astype(bf16)
    slot_row = jnp.transpose(jnp.broadcast_to(slot_col, (tokens, LANES)))[0:1, :]
    slot_sub = lax.broadcasted_iota(jnp.int32, (slots, tokens), 0).astype(f32)
    dispatch = (slot_sub == slot_row).astype(f32).astype(bf16)
    dm_ref[...] = dispatch
    to_slab(mm(dispatch, cot_ref[...]), stage, cot_send_ref)


def strips_of(vec, heads):
    out = []
    for h in heads:
        spread = jnp.broadcast_to(vec[h : h + 1, :], (LANES, 4 * LANES))
        rolled = pltpu.roll(spread, 3 * LANES + 1, 1, stride=1, stride_axis=0)
        out.append(rolled[:, : 3 * LANES])
    return out


def attend_forward_kernel(group, *refs):
    first = group == 0
    if first:
        (xperm_ref, own_ref, oth_ref, hmask_ref, umask_ref, segrow_ref, segcol_ref,
         qkv_ref, probs_ref, mixed_ref, normed_ref, gain_ref, vec_ref) = refs
    else:
        (normed_ref, vec_ref, own_ref, oth_ref, segrow_ref, segcol_ref,
         qkv_ref, probs_ref, mixed_ref) = refs
    half = own_ref.shape[0]
    tokens = segcol_ref.shape[0]
    per_group = HEADS // GROUPS
    span = per_group * HEAD_DIM
    if first:
        packed = jnp.concatenate(
            [own_ref[:, 3 * span :].astype(f32), oth_ref[:, 3 * span :].astype(f32)], axis=0
        )
        packed_row = jnp.transpose(packed)
        gain = packed_row[0:1, :]
        gain_ref[...] = jnp.broadcast_to(gain, gain_ref.shape)
        table_col = packed[:, 1:2]
        spread = (table_col * hmask_ref[...].astype(f32)).astype(bf16)
        table = mm_tn(spread, umask_ref[...])[:16]
        offset = lax.broadcasted_iota(jnp.int32, (LANES, 4 * LANES), 1) - 255
        onehot = (
            lax.broadcasted_iota(jnp.int32, (LANES, 4 * LANES), 0) == buckets_of(offset)
        ).astype(f32).astype(bf16)
        vec_ref[...] = mm(table.astype(bf16), onehot)
        x = xperm_ref[...].astype(f32)
        normed_ref[...] = (x * inverse_rms(x) * gain).astype(bf16)
    normed = normed_ref[...]
    weights_own = own_ref[:, : 3 * span] if first else own_ref[...]
    weights_oth = oth_ref[:, : 3 * span] if first else oth_ref[...]
    qkv = mm(normed[:, :half], weights_own) + mm(normed[:, half:], weights_oth)
    scale = HEAD_DIM ** (-0.5)
    qkv_ref[:, :span] = (qkv[:, :span].astype(bf16) * scale).astype(bf16)
    qkv_ref[:, span:] = qkv[:, span:].astype(bf16)
    vec = vec_ref[...]
    low_half = lax.broadcasted_iota(jnp.int32, (LANES, LANES), 1) < HEAD_DIM
    blocks = tokens // LANES
    for pair in range(span // LANES):
        cols = slice(pair * LANES, (pair + 1) * LANES)
        keys = qkv_ref[:, span + pair * LANES : span + (pair + 1) * LANES]
        vals = qkv_ref[:, 2 * span + pair * LANES : 2 * span + (pair + 1) * LANES]
        heads = [group * per_group + pair * 2 + k for k in range(2)]
        strips = strips_of(vec, heads)
        for i in range(blocks):
            rows = slice(i * LANES, (i + 1) * LANES)
            query = qkv_ref[rows, cols]
            same = segcol_ref[rows, 0:1] == segrow_ref[...].astype(f32)
            mixed = []
            for k in range(2):
                keep = low_half if k == 0 else jnp.logical_not(low_half)
                masked = jnp.where(keep, query, jnp.zeros_like(query))
                scores = mm_nt(masked, keys)
                h = heads[k]
                left = vec[h : h + 1, 0:1]
                right = vec[h : h + 1, 510:511]
                bias = []
                for j in range(blocks):
                    if j < i - 1:
                        bias.append(jnp.broadcast_to(left, (LANES, LANES)))
                    elif j > i + 1:
                        bias.append(jnp.broadcast_to(right, (LANES, LANES)))
                    else:
                        at = (j - i + 1) * LANES
                        bias.append(strips[k][:, at : at + LANES])
                scores = scores + jnp.concatenate(bias, axis=1)
                scores = jnp.where(same, scores, -1000000000.0)
                top = jnp.max(scores, axis=-1, keepdims=True)
                weights = jnp.exp(scores - top)
                total = jnp.sum(weights, axis=-1, keepdims=True)
                probs = (weights * (1.0 / total)).astype(bf16)
                probs_ref[pair * 2 + k, rows, :] = probs
                mixed.append(mm(probs, vals))
            mixed_ref[rows, cols] = jnp.where(low_half, mixed[0], mixed[1]).astype(bf16)


def restore_kernel(own_ref, oth_ref, perm_ref, wo_ref, router_ref, gain_ref, experts):
    half = own_ref.shape[0]
    width = wo_ref.shape[1]
    perm = perm_ref[...]
    true = mm(perm[:, :half], own_ref[...]) + mm(perm[:, half:], oth_ref[...])
    wo_ref[...] = true[:, :width].astype(bf16)
    router_ref[...] = true[:, width:].astype(bf16)
    block = (experts // LANES) * LANES
    lanes = jnp.transpose(true[:, width + block : width + block + LANES])
    gain_ref[...] = jnp.broadcast_to(lanes[experts - block : experts - block + 1, :], gain_ref.shape)


def after_kernel(x_ref, m0, m1, m2, wo_ref, gain_ref, dm_ref, after_ref, low_ref, send_ref, stage):
    span = m0.shape[1]
    after = x_ref[...].astype(f32)
    for c, m in enumerate((m0, m1, m2)):
        after = after + mm(m[...], wo_ref[c * span : (c + 1) * span, :])
    after_ref[...] = after
    low = (after * inverse_rms(after) * gain_ref[0:1, :]).astype(bf16)
    low_ref[...] = low
    to_slab(mm(dm_ref[...], low), stage, send_ref)


def transpose_kernel(m0, m1, m2, perm_ref, normed_ref, mixed_t_ref, normed_t_ref):
    span = m0.shape[1]
    total = None
    for c, m in enumerate((m0, m1, m2)):
        part = mm(m[...], perm_ref[c * span : (c + 1) * span, :])
        total = part if total is None else total + part
    mixed_t_ref[...] = jnp.transpose(total).astype(bf16)
    normed_t_ref[...] = jnp.transpose(normed_ref[...].astype(f32)).astype(bf16)


def early_expert_kernel(recv_ref, win_ref, wout_ref, cot_ref, win_low_ref, wout_low_ref, g_ref, stage):
    slots = cot_ref.shape[0]

    @pl.when(pl.program_id(0) == 0)
    def _():
        def put(c, values):
            cot_ref[:, c * LANES : (c + 1) * LANES] = values.astype(bf16)

        from_slab(recv_ref, stage, slots, put)

    win_low_ref[...] = win_ref[0].astype(bf16)
    wout = wout_ref[0].astype(bf16)
    wout_low_ref[...] = wout
    g_ref[...] = mm_nt(cot_ref[...], wout)


def expert_kernel(
    experts, steps,
    me_ref, recv_ref, cot_ref, win_ref, wout_ref, g_ref, router_ref,
    back_ref, prod_ref, hidden_ref, act_ref, x_ref, rows_ref, glog_ref,
    stage, acc_prod, acc_back, gate_ref,
):
    slots = cot_ref.shape[0]
    step = pl.program_id(0)
    wide = router_ref.shape[1]

    def router_probs():
        logits = mm(x_ref[...], router_ref[...])
        lane = lax.broadcasted_iota(jnp.int32, (slots, wide), 1)
        logits = jnp.where(lane < experts, logits, -jnp.inf)
        weights = jnp.exp(logits - jnp.max(logits, axis=-1, keepdims=True))
        probs = weights / jnp.sum(weights, axis=-1, keepdims=True)
        own = (lane == me_ref[0]).astype(f32)
        return probs, own, jnp.sum(probs * own, axis=-1, keepdims=True)

    @pl.when(step == 0)
    def _():
        def put(c, values):
            x_ref[:, c * LANES : (c + 1) * LANES] = values.astype(bf16)

        from_slab(recv_ref, stage, slots, put)
        _, _, gate = router_probs()
        gate_ref[...] = jnp.broadcast_to(gate, gate_ref.shape)
        rows_ref[...] = (gate * cot_ref[...].astype(f32)).astype(bf16)
        acc_prod[...] = jnp.zeros_like(acc_prod)
        acc_back[...] = jnp.zeros_like(acc_back)

    win = win_ref[...]
    pre = mm(x_ref[...], win)
    squared = pre * pre
    bent = jnp.tanh(gelu_coef * (pre + cubic_coef * squared * pre))
    rise = 0.5 * (1.0 + bent)
    hidden = (pre * rise).astype(bf16)
    slope = rise + 0.5 * pre * (1.0 - bent * bent) * gelu_coef * (1.0 + 3.0 * cubic_coef * squared)
    act = (gate_ref[:, 0:1] * g_ref[...] * slope).astype(bf16)
    hidden_ref[...] = hidden
    act_ref[...] = act
    acc_prod[...] += mm(hidden, wout_ref[...])
    acc_back[...] += mm_nt(act, win)

    @pl.when(step == steps - 1)
    def _():
        probs, own, gate = router_probs()
        produced = acc_prod[...].astype(bf16).astype(f32)
        grad_gate = jnp.sum(cot_ref[...].astype(f32) * produced, axis=-1, keepdims=True)
        grad_logits = (probs * (own - gate) * grad_gate).astype(bf16)
        glog_ref[...] = grad_logits
        back = acc_back[...].astype(bf16).astype(f32) + mm_nt(grad_logits, router_ref[...])
        to_slab(back, stage, back_ref)
        to_slab(produced, stage, prod_ref)


def expert_weights_kernel(
    x_ref, rows_ref, glog_ref, perm_ref, hidden_ref, act_ref, gin_ref, gout_ref, grouter_ref, xt
):
    @pl.when(pl.program_id(0) == 0)
    def _():
        xt[...] = jnp.transpose(x_ref[...].astype(f32)).astype(bf16)
        moved = mm(x_ref[...], perm_ref[...]).astype(bf16)
        grouter_ref[...] = mm_tn(moved, glog_ref[...])

    gout_ref[0] = mm_tn(hidden_ref[...], rows_ref[...])
    gin_ref[0] = mm(xt[...], act_ref[...])


def output_kernel(experts, recv_ref, dt_ref, after_ref, low_ref, router_ref, routes_ref, out_ref, stage, rows):
    def put(c, values):
        rows[:, c * LANES : (c + 1) * LANES] = values.astype(bf16)

    from_slab(recv_ref, stage, dt_ref.shape[1], put)
    produced = mm(dt_ref[...], rows[...])
    logits = mm(low_ref[...], router_ref[...])
    lane = lax.broadcasted_iota(jnp.int32, logits.shape, 1)
    logits = jnp.where(lane < experts, logits, -jnp.inf)
    weights = jnp.exp(logits - jnp.max(logits, axis=-1, keepdims=True))
    own = (lane == routes_ref[...]).astype(f32)
    gate = jnp.sum(weights * own, axis=-1, keepdims=True) / jnp.sum(weights, axis=-1, keepdims=True)
    out_ref[...] = (after_ref[...] + gate * produced).astype(bf16)


def norm_two_kernel(
    experts,
    recv_ref, dt_ref, after_ref, gain_ref, cot_ref, wo_ref, mixed_t_ref, perm_ref, grouter_ref,
    grad_after_ref, grad_mixed_ref, keep_ref, send_ref,
    stage, rows,
):
    def put(c, values):
        rows[:, c * LANES : (c + 1) * LANES] = values.astype(bf16)

    from_slab(recv_ref, stage, dt_ref.shape[1], put)
    grad = mm(dt_ref[...], rows[...])
    after = after_ref[...]
    inverse = inverse_rms(after)
    unit = after * inverse
    scaled = grad * gain_ref[0:1, :]
    back = inverse * (scaled - unit * jnp.mean(scaled * unit, axis=-1, keepdims=True))
    grad_after = cot_ref[...].astype(f32) + back
    grad_after_ref[...] = grad_after
    low = grad_after.astype(bf16)
    grad_mixed_ref[...] = mm_nt(low, wo_ref[...]).astype(bf16)
    half = keep_ref.shape[0]
    width = low.shape[1]
    keep_ref[:, :width] = mm(mixed_t_ref[:half, :], low)
    send_ref[:, :width] = mm(mixed_t_ref[half:, :], low).astype(bf16)
    gain_row = jnp.sum(grad * unit, axis=0, keepdims=True)
    high, rest = split_two(jnp.broadcast_to(gain_row, (8, width)))
    gain_row = (mm(high, perm_ref[...]) + mm(rest, perm_ref[...]))[0:1, :]
    grouter = grouter_ref[...]
    lane = lax.broadcasted_iota(jnp.int32, grouter.shape, 1)
    packed = jnp.where(
        lane < experts, grouter, jnp.where(lane == experts, to_column(gain_row, grouter.shape[1]), 0.0)
    )
    keep_ref[:, width:] = packed[:half]
    send_ref[:, width:] = packed[half:].astype(bf16)


def unskew(skewed):
    span = 4 * LANES
    total = None
    for g in range(LANES // 8):
        moved = pltpu.roll(skewed[8 * g : 8 * g + 8, :], (LANES - 1 - 8 * g) % span, 1)
        total = moved if total is None else total + moved
    turned = jnp.concatenate([total[7 - s : 8 - s, :] for s in range(8)], axis=0)
    turned = pltpu.roll(turned, span - 7, 1, stride=1, stride_axis=0)
    return jnp.sum(turned, axis=0, keepdims=True)


def attend_backward_kernel(
    qkv_ref, probs_ref, gm_ref, normed_t_ref,
    dqkv_ref, keep_ref, send_ref, dvec_ref,
    ds_ref,
):
    tokens = qkv_ref.shape[0]
    span = gm_ref.shape[1]
    blocks = tokens // LANES
    scale = HEAD_DIM ** (-0.5)
    low_half = lax.broadcasted_iota(jnp.int32, (LANES, LANES), 1) < HEAD_DIM
    lane = lax.broadcasted_iota(jnp.int32, (1, 4 * LANES), 1)
    for pair in range(span // LANES):
        cols = slice(pair * LANES, (pair + 1) * LANES)
        keys = qkv_ref[:, span + pair * LANES : span + (pair + 1) * LANES]
        vals = qkv_ref[:, 2 * span + pair * LANES : 2 * span + (pair + 1) * LANES]
        query_t = jnp.transpose(qkv_ref[:, cols].astype(f32)).astype(bf16)
        grad_t = jnp.transpose(gm_ref[:, cols].astype(f32)).astype(bf16)
        dq = [[None, None] for _ in range(blocks)]
        dk_t, dv_t = [], []
        for k in range(2):
            head = pair * 2 + k
            keep = low_half if k == 0 else jnp.logical_not(low_half)
            strip = [None] * 3
            far_left = far_right = None
            for i in range(blocks):
                rows = slice(i * LANES, (i + 1) * LANES)
                grad = gm_ref[rows, cols]
                grad = jnp.where(keep, grad, jnp.zeros_like(grad))
                dp = mm_nt(grad, vals)
                probs = probs_ref[head, rows, :].astype(f32)
                delta = jnp.sum(probs * dp, axis=-1, keepdims=True)
                ds = (probs * (dp - delta)).astype(bf16)
                ds_ref[k, rows, :] = ds
                dq[i][k] = mm(ds, keys)
                wide = ds.astype(f32)
                for j in range(blocks):
                    piece = wide[:, j * LANES : (j + 1) * LANES]
                    if j < i - 1:
                        far_left = piece if far_left is None else far_left + piece
                    elif j > i + 1:
                        far_right = piece if far_right is None else far_right + piece
                    else:
                        at = j - i + 1
                        strip[at] = piece if strip[at] is None else strip[at] + piece
            part = slice(k * HEAD_DIM, (k + 1) * HEAD_DIM)
            dk_t.append(mm(query_t[part, :], ds_ref[k]))
            dv_t.append(mm(grad_t[part, :], probs_ref[head]))
            skewed = jnp.concatenate(strip + [jnp.zeros((LANES, LANES), f32)], axis=1)
            vec = unskew(skewed)
            left = jnp.sum(jnp.sum(far_left, axis=0, keepdims=True), axis=1, keepdims=True)
            right = jnp.sum(jnp.sum(far_right, axis=0, keepdims=True), axis=1, keepdims=True)
            vec = vec + jnp.where(lane == 0, left, 0.0) + jnp.where(lane == 510, right, 0.0)
            dvec_ref[head : head + 1, :] = vec
        for i in range(blocks):
            rows = slice(i * LANES, (i + 1) * LANES)
            dqkv_ref[rows, cols] = (jnp.where(low_half, dq[i][0], dq[i][1]) * scale).astype(bf16)
        dk = jnp.transpose(jnp.concatenate(dk_t, axis=0))
        dv = jnp.transpose(jnp.concatenate(dv_t, axis=0))
        dqkv_ref[:, span + pair * LANES : span + (pair + 1) * LANES] = dk.astype(bf16)
        dqkv_ref[:, 2 * span + pair * LANES : 2 * span + (pair + 1) * LANES] = dv.astype(bf16)
    half = keep_ref.shape[0]
    grads = dqkv_ref[...]
    send_ref[...] = mm(normed_t_ref[half:, :], grads).astype(bf16)
    keep_ref[...] = mm(normed_t_ref[:half, :], grads)


def last_kernel(
    xperm_ref, gain_ref, perm_ref, after_ref, hmask_ref, umask_ref,
    d0, own0, oth0, v0, d1, own1, oth1, v1, d2, own2, oth2, v2,
    out_ref, keep_ref, send_ref,
):
    groups = ((d0, own0, oth0, v0), (d1, own1, oth1, v1), (d2, own2, oth2, v2))
    wide = d1.shape[1]
    first = second = None
    for d, own, oth, _ in groups:
        grads = d[...]
        one = mm_nt(grads, own[:, :wide])
        two = mm_nt(grads, oth[:, :wide])
        first = one if first is None else first + one
        second = two if second is None else second + two
    grad = jnp.concatenate([first, second], axis=1)
    x = xperm_ref[...].astype(f32)
    inverse = inverse_rms(x)
    unit = x * inverse
    scaled = grad * gain_ref[0:1, :]
    back = inverse * (scaled - unit * jnp.mean(scaled * unit, axis=-1, keepdims=True))
    high, rest = split_two(back)
    perm = perm_ref[...]
    out_ref[...] = (after_ref[...] + (mm_nt(high, perm) + mm_nt(rest, perm))).astype(bf16)
    gain_col = to_column(jnp.sum(grad * unit, axis=0, keepdims=True))
    per_group = HEADS // GROUPS
    vec = jnp.concatenate(
        [g[3][:per_group, :] for g in groups] + [jnp.zeros((4, 4 * LANES), f32)], axis=0
    )
    offset = lax.broadcasted_iota(jnp.int32, (LANES, 4 * LANES), 1) - 255
    onehot = (
        lax.broadcasted_iota(jnp.int32, (LANES, 4 * LANES), 0) == buckets_of(offset)
    ).astype(f32).astype(bf16)

    def exact(values, right, product):
        one, low = split_two(values)
        two, three = split_two(values - one.astype(f32))
        return product(one, right) + (product(two, right) + product(three, right))

    table = exact(vec, onehot, mm_nt)
    heads = hmask_ref[:, :16]
    one, _ = split_two(table)
    two, _ = split_two(table - one.astype(f32))
    three = (table - one.astype(f32) - two.astype(f32)).astype(bf16)
    spread = mm(heads, one) + (mm(heads, two) + mm(heads, three))
    table_col = jnp.sum(spread * umask_ref[...].astype(f32), axis=1, keepdims=True)
    lane = lax.broadcasted_iota(jnp.int32, gain_col.shape, 1)
    packed = jnp.where(lane == 0, gain_col, jnp.where(lane == 1, table_col, 0.0))
    half = keep_ref.shape[0]
    keep_ref[...] = packed[:half]
    send_ref[...] = packed[half:].astype(bf16)


def shards(
    count,
    inputs,
    segment_ids,
    routes,
    cotangent,
    gain_attn,
    gain_ffn,
    bias_table,
    w_query,
    w_key,
    w_value,
    w_output,
    w_router,
    w_in,
    w_out,
):
    tokens, width = inputs.shape
    experts = w_router.shape[1]
    rows_local = w_query.shape[0]
    entries = bias_table.shape[0]
    hidden_units = w_in.shape[2]
    capacity = max(2, 5 * tokens // (4 * experts))
    slots = experts * capacity
    blocks = width // LANES
    span = width // GROUPS
    half = width // 2
    wide = -(-(experts + 1) // LANES) * LANES
    me = lax.axis_index("seq").astype(jnp.int32).reshape(1)
    smem = pl.BlockSpec(memory_space=pltpu.SMEM)
    vmem = pl.BlockSpec(memory_space=pltpu.VMEM)

    low = [w.astype(bf16) for w in (w_query, w_key, w_value)]
    small = jnp.concatenate(
        [
            gain_attn.astype(bf16)[:, None],
            jnp.pad(bias_table.astype(bf16), (0, rows_local - entries))[:, None],
            jnp.zeros((rows_local, LANES - 2), bf16),
        ],
        axis=1,
    )
    pieces = []
    for c in range(GROUPS):
        own = [w[:, c * span : (c + 1) * span] for w in low]
        pieces.append(jnp.concatenate(own + ([small] if c == 0 else []), axis=1))
    tail = jnp.concatenate(
        [
            w_output.astype(bf16),
            w_router.astype(bf16),
            gain_ffn.astype(bf16)[:, None],
            jnp.zeros((rows_local, wide - experts - 1), bf16),
        ],
        axis=1,
    )
    halves = [gather_relative(p, count) for p in pieces]
    own_tail, oth_tail = gather_relative(tail, count)

    order = np.asarray(relative_order(count), np.int32)
    rel_row = jnp.asarray(np.repeat(order, rows_local)[None, :])
    off_row = jnp.asarray(np.tile(np.arange(rows_local, dtype=np.int32), count)[None, :])
    slab = (slots * blocks, LANES)
    slab_stage = pltpu.VMEM(slab, f32)
    perm, xperm, segcol, hmask, umask, dt, dm, cot_send = pl.pallas_call(
        functools.partial(prepare_kernel, rows_local, entries, experts, capacity),
        out_shape=[
            jax.ShapeDtypeStruct(s, d)
            for s, d in (
                ((width, width), bf16),
                ((tokens, width), bf16),
                ((tokens, LANES), f32),
                ((width, LANES), bf16),
                ((width, LANES), bf16),
                ((tokens, slots), bf16),
                ((slots, tokens), bf16),
                (slab, bf16),
            )
        ],
        in_specs=[smem] + [vmem] * 6,
        scratch_shapes=[slab_stage],
        compiler_params=pltpu.CompilerParams(vmem_limit_bytes=48 * 1024 * 1024),
        cost_estimate=pl.CostEstimate(flops=4 * 10**9, bytes_accessed=10**7, transcendentals=0),
    )(me, rel_row, off_row, inputs, segment_ids, routes, cotangent)

    slab_split = (count, slots * blocks // count, LANES)

    def exchange(rows):
        return lax.all_to_all(
            rows.reshape(slab_split), "seq", split_axis=0, concat_axis=0, tiled=True
        ).reshape(slab)

    cot_recv = exchange(cot_send)

    per_group = HEADS // GROUPS
    group_outs = [
        ((tokens, 3 * span), bf16),
        ((per_group, tokens, tokens), bf16),
        ((tokens, span), bf16),
    ]
    fwd_cost = dict(flops=3 * 10**9, nbytes=8 * 10**6)
    qkv, probs, mixed = [None] * GROUPS, [None] * GROUPS, [None] * GROUPS
    qkv[0], probs[0], mixed[0], normed, gain_one, vec = kernel_call(
        functools.partial(attend_forward_kernel, 0),
        group_outs + [((tokens, width), bf16), ((8, width), f32), ((16, 4 * LANES), f32)],
        **fwd_cost,
    )(xperm, halves[0][0], halves[0][1], hmask, umask, segment_ids, segcol)
    for c in range(1, GROUPS):
        qkv[c], probs[c], mixed[c] = kernel_call(
            functools.partial(attend_forward_kernel, c), group_outs, **fwd_cost
        )(normed, vec, halves[c][0], halves[c][1], segment_ids, segcol)

    output_w, router_w, gain_two = kernel_call(
        functools.partial(restore_kernel, experts=experts),
        [((width, width), bf16), ((width, wide), bf16), ((8, width), f32)],
        flops=10**9,
        nbytes=4 * 10**6,
    )(own_tail, oth_tail, perm)
    after, low_two, row_send = kernel_call(
        after_kernel,
        [((tokens, width), f32), ((tokens, width), bf16), (slab, bf16)],
        scratch=[slab_stage],
        flops=2 * 10**9,
        nbytes=6 * 10**6,
    )(inputs, *mixed, output_w, gain_two, dm)
    row_recv = exchange(row_send)

    step_units = hidden_units // 6
    steps = hidden_units // step_units

    def whole(shape):
        return pl.BlockSpec(shape, lambda i: (0,) * len(shape))

    weight_in = pl.BlockSpec((1, width, step_units), lambda i: (0, 0, i))
    weight_out = pl.BlockSpec((1, step_units, width), lambda i: (0, i, 0))
    low_in = pl.BlockSpec((width, step_units), lambda i: (0, i))
    low_out = pl.BlockSpec((step_units, width), lambda i: (i, 0))
    slot_units = pl.BlockSpec((slots, step_units), lambda i: (0, i))
    cot_rows, win_low, wout_low, grad_hidden = kernel_call(
        early_expert_kernel,
        [
            ((slots, width), bf16),
            ((width, hidden_units), bf16),
            ((hidden_units, width), bf16),
            ((slots, hidden_units), f32),
        ],
        scratch=[slab_stage],
        grid=(steps,),
        in_specs=[whole(slab), weight_in, weight_out],
        out_specs=[whole((slots, width)), low_in, low_out, slot_units],
        flops=3 * 10**9,
        nbytes=36 * 10**6,
    )(cot_recv, w_in, w_out)
    mixed_t, normed_t = kernel_call(
        transpose_kernel,
        [((width, tokens), bf16), ((width, tokens), bf16)],
        flops=10**9,
        nbytes=4 * 10**6,
    )(*mixed, perm, normed)
    back_send, prod_send, hidden, act, x_rows, grad_rows, grad_logits = kernel_call(
        functools.partial(expert_kernel, experts, steps),
        [
            (slab, bf16),
            (slab, bf16),
            ((slots, hidden_units), bf16),
            ((slots, hidden_units), bf16),
            ((slots, width), bf16),
            ((slots, width), bf16),
            ((slots, wide), bf16),
        ],
        scratch=[
            slab_stage,
            pltpu.VMEM((slots, width), f32),
            pltpu.VMEM((slots, width), f32),
            pltpu.VMEM((slots, LANES), f32),
        ],
        grid=(steps,),
        in_specs=[
            smem,
            whole(slab),
            whole((slots, width)),
            low_in,
            low_out,
            slot_units,
            whole((width, wide)),
        ],
        out_specs=[
            whole(slab),
            whole(slab),
            slot_units,
            slot_units,
            whole((slots, width)),
            whole((slots, width)),
            whole((slots, wide)),
        ],
        flops=10 * 10**9,
        nbytes=30 * 10**6,
    )(me, row_recv, cot_rows, win_low, wout_low, grad_hidden, router_w)
    back_recv = exchange(back_send)
    prod_send, back_recv_first = lax.optimization_barrier((prod_send, back_recv))
    prod_recv = exchange(prod_send)
    grad_inner, grad_outer, grad_router = kernel_call(
        expert_weights_kernel,
        [
            ((1, width, hidden_units), f32),
            ((1, hidden_units, width), f32),
            ((width, wide), f32),
        ],
        scratch=[pltpu.VMEM((width, slots), bf16)],
        grid=(steps,),
        in_specs=[
            whole((slots, width)),
            whole((slots, width)),
            whole((slots, wide)),
            whole((width, width)),
            slot_units,
            slot_units,
        ],
        out_specs=[weight_in, weight_out, whole((width, wide))],
        flops=7 * 10**9,
        nbytes=30 * 10**6,
    )(x_rows, grad_rows, grad_logits, perm, hidden, act)

    row_scratch = pltpu.VMEM((slots, width), bf16)
    grad_after, grad_mixed, keep_o, send_o = kernel_call(
        functools.partial(norm_two_kernel, experts),
        [
            ((tokens, width), f32),
            ((tokens, width), bf16),
            ((half, width + wide), f32),
            ((half, width + wide), bf16),
        ],
        scratch=[slab_stage, row_scratch],
        flops=2 * 10**9,
        nbytes=10 * 10**6,
    )(back_recv_first, dt, after, gain_two, cotangent, output_w, mixed_t, perm, grad_router)
    sum_o = scatter_relative(keep_o, send_o, count)

    output = kernel_call(
        functools.partial(output_kernel, experts),
        [((tokens, width), bf16)],
        scratch=[slab_stage, row_scratch],
        flops=10**9,
        nbytes=5 * 10**6,
    )(prod_recv, dt, after, low_two, router_w, routes)[0]

    grads, sums = [], []
    for c in range(GROUPS):
        dqkv, keep, send, dvec = kernel_call(
            attend_backward_kernel,
            [
                ((tokens, 3 * span), bf16),
                ((half, 3 * span), f32),
                ((half, 3 * span), bf16),
                ((8, 4 * LANES), f32),
            ],
            scratch=[pltpu.VMEM((2, tokens, tokens), bf16)],
            flops=4 * 10**9,
            nbytes=8 * 10**6,
        )(qkv[c], probs[c], grad_mixed[:, c * span : (c + 1) * span], normed_t)
        sums.append(scatter_relative(keep, send, count))
        grads += [dqkv, halves[c][0], halves[c][1], dvec]
    grad_inputs, keep, send = kernel_call(
        last_kernel,
        [((tokens, width), bf16), ((half, LANES), f32), ((half, LANES), bf16)],
        flops=4 * 10**9,
        nbytes=10 * 10**6,
    )(xperm, gain_one, perm, grad_after, hmask, umask, *grads)
    sum_small = scatter_relative(keep, send, count)

    def weight(k):
        return jnp.concatenate([s[:, k * span : (k + 1) * span] for s in sums], axis=1)

    return (
        output,
        grad_inputs,
        sum_small[:, 0],
        sum_o[:, width + experts],
        sum_small[:entries, 1],
        weight(0),
        weight(1),
        weight(2),
        sum_o[:, :width],
        sum_o[:, width : width + experts],
        grad_inner,
        grad_outer,
    )


def solution(mesh):
    row, flat, cube = P("seq", None), P("seq"), P("seq", None, None)
    in_specs = (row,) * 4 + (flat,) * 3 + (row,) * 5 + (cube,) * 2
    out_specs = (row,) * 2 + (flat,) * 3 + (row,) * 5 + (cube,) * 2
    return jax.shard_map(
        functools.partial(shards, mesh.shape["seq"]),
        mesh=mesh,
        in_specs=in_specs,
        out_specs=out_specs,
        check_vma=False,
    )
```

```python
import functools

import jax
import jax.numpy as jnp
import numpy as np
from jax import lax
from jax.experimental import pallas as pl
from jax.experimental.pallas import tpu as pltpu
from jax.sharding import PartitionSpec as P

HEADS = 12
HEAD_DIM = 64
BUCKETS = 32
PAIRS = HEADS // 2
PART = PAIRS // 2
LANES = 128
BLOCK = 3 * LANES

epsilon = 1e-06
bucket_edges = (1, 2, 3, 4, 5, 6, 7, 8, 12, 16, 23, 32, 46, 64, 91)
gelu_coef = 0.7978845608028654
cubic_coef = 0.044715

f32 = jnp.float32
bf16 = jnp.bfloat16


def bit_groups(count):
    bits = count.bit_length() - 1
    groups, low = [(0, 1)], 1
    while low < bits:
        width = min(2, bits - low)
        groups.append((low, width))
        low += width
    return groups


def relative_order(count):
    order = [0]
    for low, width in bit_groups(count):
        order = [base + (m << low) for base in order for m in range(1 << width)]
    return order


def swap(values, distance, count):
    return lax.ppermute(values, "seq", [(i, i ^ distance) for i in range(count)])


def after(values, *others):
    return lax.optimization_barrier((values, *others))[0]


def mm(left, right):
    return jnp.dot(left, right, preferred_element_type=f32)


def mm_nt(left, right):
    return lax.dot_general(left, right, (((1,), (1,)), ((), ())), preferred_element_type=f32)


def mm_tn(left, right):
    return lax.dot_general(left, right, (((0,), (0,)), ((), ())), preferred_element_type=f32)


def split_two(values):
    high = values.astype(bf16)
    return high, (values - high.astype(f32)).astype(bf16)


class Far:
    def __init__(self, values):
        self.values = values


def near(shape, dtype):
    return pltpu.VMEM(shape, dtype)


def far(shape, dtype):
    return pltpu.HBM(shape, dtype)


class Fetched:
    def __init__(self, copy, ref):
        self.copy, self.ref, self.here = copy, ref, False

    def __call__(self):
        if not self.here:
            self.copy.wait()
            self.here = True
        return self.ref


class Stored:
    def __init__(self, copy, ref):
        self.copy, self.ref, self.sent = copy, ref, False

    def send(self):
        self.copy.start()
        self.sent = True


def place(a):
    if isinstance(a, Far):
        return pltpu.with_memory_space_constraint(a.values, pltpu.HBM)
    return a


def parameters(vmem):
    return dict(
        compiler_params=pltpu.CompilerParams(vmem_limit_bytes=vmem * 1024 * 1024),
        cost_estimate=pl.CostEstimate(flops=1000, bytes_accessed=1000, transcendentals=0),
    )


def grid_call(body, outs, grid, in_specs, out_specs, scratch=(), vmem=40):
    call = pl.pallas_call(
        body,
        out_shape=list(outs),
        grid=grid,
        in_specs=in_specs,
        out_specs=out_specs,
        scratch_shapes=list(scratch),
        **parameters(vmem),
    )
    return lambda *args: call(*[place(a) for a in args])


def flat_call(body, outs, scratch=(), vmem=32):
    def run(*args):
        lazy = [isinstance(a, Far) for a in args]
        late = [o.memory_space == pltpu.HBM for o in outs]
        values = [a.values if f else a for a, f in zip(args, lazy)]
        n_in, n_out, n_scratch = len(args), len(outs), len(scratch)
        any_ref, vmem_ref, smem_ref = (
            pl.BlockSpec(memory_space=m) for m in (pl.ANY, pltpu.VMEM, pltpu.SMEM)
        )
        in_copies = [pltpu.VMEM(v.shape, v.dtype) for v, f in zip(values, lazy) if f]
        out_copies = [pltpu.VMEM(o.shape, o.dtype) for o, f in zip(outs, late) if f]

        def wrapped(*refs):
            ins, rest = refs[:n_in], refs[n_in:]
            results, rest = rest[:n_out], rest[n_out:]
            own, rest = rest[:n_scratch], rest[n_scratch:]
            fetched, rest = list(rest[: len(in_copies)]), rest[len(in_copies) :]
            stored, rest = list(rest[: len(out_copies)]), rest[len(out_copies) :]
            sems = list(rest)
            given, made = [], []
            for ref, f in zip(ins, lazy):
                if f:
                    copy = pltpu.make_async_copy(ref, fetched[0], sems.pop())
                    copy.start()
                    given.append(Fetched(copy, fetched.pop(0)))
                else:
                    given.append(ref)
            for ref, f in zip(results, late):
                if f:
                    made.append(
                        Stored(pltpu.make_async_copy(stored[0], ref, sems.pop()), stored[0])
                    )
                    stored.pop(0)
                else:
                    made.append(ref)
            body(*given, *made, *own)
            for item in given:
                if isinstance(item, Fetched):
                    item()
            for item in made:
                if isinstance(item, Stored):
                    if not item.sent:
                        item.send()
                    item.copy.wait()

        return pl.pallas_call(
            wrapped,
            out_shape=list(outs),
            in_specs=[
                any_ref if f else (smem_ref if v.size == 1 else vmem_ref)
                for v, f in zip(values, lazy)
            ],
            out_specs=[any_ref if f else vmem_ref for f in late],
            scratch_shapes=list(scratch)
            + in_copies
            + out_copies
            + [pltpu.SemaphoreType.DMA] * (len(in_copies) + len(out_copies)),
            **parameters(vmem),
        )(*[place(a) for a in args])

    return run


def to_slab(values, stage, out_ref):
    slots, width = values.shape
    blocks = width // LANES
    for c in range(blocks):
        stage[pl.ds(c, slots, stride=blocks), :] = values[:, c * LANES : (c + 1) * LANES]
    out_ref[...] = stage[...].astype(out_ref.dtype)


def from_slab(in_ref, stage, slots, put):
    stage[...] = in_ref[...].astype(f32)
    blocks = in_ref.shape[0] // slots
    for c in range(blocks):
        put(c, stage[pl.ds(c, slots, stride=blocks), :])


def to_column(row, width=LANES):
    return jnp.transpose(jnp.broadcast_to(row, (width, row.shape[1])))


def inverse_rms(values):
    return lax.rsqrt(jnp.mean(values * values, axis=-1, keepdims=True) + epsilon)


def buckets_of(offset):
    magnitude = jnp.abs(offset)
    bucket = jnp.zeros(offset.shape, jnp.int32)
    for edge in bucket_edges:
        bucket = bucket + (magnitude >= edge).astype(jnp.int32)
    return bucket + BUCKETS // 2 * (offset > 0).astype(jnp.int32)


def prepare_kernel(
    rows_local, entries, experts, capacity,
    me_ref, rel_ref, off_ref, x_get, seg_get, routes_get,
    perm_out, xperm_out, segrow_out, segcol_out, hmask_out, umask_out, dt_out, dm_out,
):
    perm_ref, xperm_ref, segrow_ref, segcol_ref, hmask_ref, umask_ref, dt_ref, dm_ref = (
        out.ref
        for out in (perm_out, xperm_out, segrow_out, segcol_out, hmask_out, umask_out, dt_out, dm_out)
    )
    x_ref, seg_ref, routes_ref = x_get(), seg_get(), routes_get()
    tokens, width = x_ref.shape
    slots = dm_ref.shape[0]
    me = me_ref[0]
    device_row = rel_ref()[...] ^ me
    off_row = off_ref()[...]
    true_row = device_row * rows_local + off_row
    perm = (lax.broadcasted_iota(jnp.int32, (width, width), 0) == true_row).astype(f32).astype(bf16)
    perm_ref[...] = perm
    perm_out.send()
    xperm_ref[...] = mm(x_ref[...], perm).astype(bf16)
    segments = seg_ref[...].astype(f32)
    segrow_ref[...] = jnp.broadcast_to(segments, segrow_ref.shape)
    segcol_ref[...] = to_column(segments)
    flat = device_row * entries + off_row
    bucket_row = ((flat.astype(f32) + 0.5) * (1.0 / HEADS)).astype(jnp.int32)
    head_row = jnp.where(off_row < entries, flat - bucket_row * HEADS, -1)
    bucket_col = to_column(bucket_row.astype(f32))
    head_col = to_column(head_row.astype(f32))
    lane = lax.broadcasted_iota(jnp.int32, (width, LANES), 1).astype(f32)
    hmask_ref[...] = (head_col == lane).astype(f32).astype(bf16)
    umask_ref[...] = (bucket_col == lane).astype(f32).astype(bf16)
    routes = routes_ref[...]
    labels = lax.broadcasted_iota(jnp.int32, (tokens, experts), 1)
    picked = (routes == labels).astype(f32)
    earlier = (
        lax.broadcasted_iota(jnp.int32, (tokens, tokens), 1)
        <= lax.broadcasted_iota(jnp.int32, (tokens, tokens), 0)
    ).astype(f32).astype(bf16)
    counts = mm(earlier, picked.astype(bf16))
    position = jnp.sum(counts * picked, axis=1, keepdims=True) - 1.0
    slot_col = jnp.where(
        position < capacity, routes.astype(f32) * capacity + position, -1.0
    )
    slot_lane = lax.broadcasted_iota(jnp.int32, (tokens, slots), 1).astype(f32)
    dt_ref[...] = (slot_col == slot_lane).astype(f32).astype(bf16)
    slot_row = jnp.transpose(jnp.broadcast_to(slot_col, (tokens, LANES)))[0:1, :]
    slot_sub = lax.broadcasted_iota(jnp.int32, (slots, tokens), 0).astype(f32)
    dm_ref[...] = (slot_sub == slot_row).astype(f32).astype(bf16)


def dispatch_kernel(dm_get, cot_get, send_out, stage):
    to_slab(mm(dm_get()[...], cot_get()[...]), stage, send_out.ref)


def pack_kernel(
    experts, gain_get, gain_two_get, table_get, wq_get, wk_get, wv_get, wo_get, router_get,
    piece, tail,
):
    gain_ref, gain_two_ref, table_ref = gain_get(), gain_two_get(), table_get()
    wq_ref, wk_ref, wv_ref, wo_ref, router_ref = (
        get() for get in (wq_get, wk_get, wv_get, wo_get, router_get)
    )
    rows, width = wq_ref.shape

    def column(ref):
        size = ref.shape[1]
        same = lax.broadcasted_iota(jnp.int32, (rows, size), 0) == lax.broadcasted_iota(
            jnp.int32, (rows, size), 1
        )
        return jnp.sum(jnp.where(same, ref[...], 0.0), axis=1, keepdims=True)

    for c in range(PAIRS):
        for k, w in enumerate((wq_ref, wk_ref, wv_ref)):
            at = c * BLOCK + k * LANES
            piece[:, at : at + LANES] = w[:, c * LANES : (c + 1) * LANES].astype(bf16)
    lane = lax.broadcasted_iota(jnp.int32, (rows, LANES), 1)
    small = jnp.where(lane == 0, column(gain_ref), jnp.where(lane == 1, column(table_ref), 0.0))
    piece[:, PAIRS * BLOCK :] = small.astype(bf16)
    tail[:, :width] = wo_ref[...].astype(bf16)
    lane = lax.broadcasted_iota(jnp.int32, (rows, tail.shape[1] - width), 1)
    tail[:, width:] = jnp.where(lane == experts, column(gain_two_ref), 0.0).astype(bf16)
    tail[:, width : width + experts] = router_ref[...].astype(bf16)


def attend_forward_kernel(
    xperm_ref, own_ref, oth_ref, own_small, oth_small, hmask_ref, umask_ref, segrow_ref, segcol_ref,
    qkv_ref, probs_ref, mixed_ref, normed_ref, gain_ref,
    vec_ref, score_ref, strip_ref,
):
    half = own_ref.shape[0]
    tokens = segcol_ref.shape[0]
    blocks = tokens // LANES
    pair = pl.program_id(0)

    @pl.when(pair == 0)
    def _():
        packed = jnp.concatenate([own_small[...].astype(f32), oth_small[...].astype(f32)], axis=0)
        gain = jnp.transpose(packed)[0:1, :]
        gain_ref[...] = jnp.broadcast_to(gain, gain_ref.shape)
        spread = (packed[:, 1:2] * hmask_ref[...].astype(f32)).astype(bf16)
        table = mm_tn(spread, umask_ref[...])[:16]
        offset = lax.broadcasted_iota(jnp.int32, (LANES, 4 * LANES), 1) - 255
        onehot = (
            lax.broadcasted_iota(jnp.int32, (LANES, 4 * LANES), 0) == buckets_of(offset)
        ).astype(f32).astype(bf16)
        vec_ref[...] = mm(table.astype(bf16), onehot)
        x = xperm_ref[...].astype(f32)
        normed_ref[...] = (x * inverse_rms(x) * gain).astype(bf16)

    qkv = mm(normed_ref[:, :half], own_ref[...]) + mm(normed_ref[:, half:], oth_ref[...])
    query = (qkv[:, :LANES].astype(bf16) * HEAD_DIM ** (-0.5)).astype(bf16)
    keys = qkv[:, LANES : 2 * LANES].astype(bf16)
    vals = qkv[:, 2 * LANES :].astype(bf16)
    qkv_ref[:, :LANES] = query
    qkv_ref[:, LANES : 2 * LANES] = keys
    qkv_ref[:, 2 * LANES :] = vals
    low_half = lax.broadcasted_iota(jnp.int32, (tokens, LANES), 1) < HEAD_DIM
    left, right = [], []
    for k in range(2):
        keep = low_half if k == 0 else jnp.logical_not(low_half)
        score_ref[k] = mm_nt(jnp.where(keep, query, jnp.zeros_like(query)), keys)
        row = vec_ref[pl.ds(pair * 2 + k, 1), :]
        left.append(row[:, 0:1])
        right.append(row[:, 510:511])
        rolled = pltpu.roll(
            jnp.broadcast_to(row, (LANES, 4 * LANES)), 3 * LANES + 1, 1, stride=1, stride_axis=0
        )
        strip_ref[k] = rolled[:, : 3 * LANES]
    for i in range(blocks):
        rows = slice(i * LANES, (i + 1) * LANES)
        same = segcol_ref[rows, 0:1] == segrow_ref[0:1, :]
        for k in range(2):
            bias = []
            for j in range(blocks):
                if j < i - 1:
                    bias.append(jnp.broadcast_to(left[k], (LANES, LANES)))
                elif j > i + 1:
                    bias.append(jnp.broadcast_to(right[k], (LANES, LANES)))
                else:
                    at = (j - i + 1) * LANES
                    bias.append(strip_ref[k, :, at : at + LANES])
            scores = score_ref[k, rows, :] + jnp.concatenate(bias, axis=1)
            scores = jnp.where(same, scores, -1000000000.0)
            top = jnp.max(scores, axis=-1, keepdims=True)
            weights = jnp.exp(scores - top)
            total = jnp.sum(weights, axis=-1, keepdims=True)
            probs_ref[k, rows, :] = (weights * (1.0 / total)).astype(bf16)
    mixed = [mm(probs_ref[k], vals) for k in range(2)]
    mixed_ref[:, pl.ds(pl.multiple_of(pair * LANES, LANES), LANES)] = jnp.where(
        low_half, mixed[0], mixed[1]
    ).astype(bf16)


def after_kernel(
    experts, mixed_ref, perm_get, own_ref, oth_ref, x_get, dm_get,
    after_out, low_out, send_out, gain_out, mixed_out,
    stage,
):
    half = own_ref.shape[0]
    width = mixed_ref.shape[1]
    perm = perm_get()[...]
    mixed = mm(mixed_ref[...], perm).astype(bf16)
    mixed_out.ref[...] = mixed
    mixed_out.send()
    block = width + (experts // LANES) * LANES
    lanes = jnp.transpose(
        jnp.concatenate(
            [own_ref[:, block : block + LANES].astype(f32), oth_ref[:, block : block + LANES].astype(f32)],
            axis=0,
        )
    )
    at = experts % LANES
    gain = mm_nt(jnp.broadcast_to(lanes[at : at + 1, :], (8, width)).astype(bf16), perm)
    gain_out.ref[...] = gain
    gain_out.send()
    after = x_get()[...].astype(f32) + (
        mm(mixed[:, :half], own_ref[:, :width]) + mm(mixed[:, half:], oth_ref[:, :width])
    )
    after_out.ref[...] = after
    after_out.send()
    low = (after * inverse_rms(after) * gain[0:1, :]).astype(bf16)
    low_out.ref[...] = low
    low_out.send()
    to_slab(mm(dm_get()[...], low), stage, send_out.ref)


def between_kernel(
    mixed_get, normed_get, own_ref, oth_ref, perm_get, mixed_t_out, normed_t_out, wo_out, router_out
):
    mixed_t_out.ref[...] = jnp.transpose(mixed_get()[...].astype(f32)).astype(bf16)
    mixed_t_out.send()
    normed_t_out.ref[...] = jnp.transpose(normed_get()[...].astype(f32)).astype(bf16)
    normed_t_out.send()
    half = own_ref.shape[0]
    perm = perm_get()[...]
    rest = (mm(perm[:, :half], own_ref[...]) + mm(perm[:, half:], oth_ref[...])).astype(bf16)
    width = wo_out.ref.shape[1]
    wo_out.ref[...] = rest[:, :width]
    router_out.ref[...] = rest[:, width:]


def early_expert_kernel(recv_ref, win_ref, wout_ref, cot_ref, win_low_ref, wout_low_ref, g_ref, stage):
    slots = cot_ref.shape[0]

    @pl.when(pl.program_id(0) == 0)
    def _():
        def put(c, values):
            cot_ref[:, c * LANES : (c + 1) * LANES] = values.astype(bf16)

        from_slab(recv_ref, stage, slots, put)

    win_low_ref[0] = win_ref[0].astype(bf16)
    wout = wout_ref[0].astype(bf16)
    wout_low_ref[0] = wout
    g_ref[0] = mm_nt(cot_ref[...], wout).astype(bf16)


def activate(pre):
    squared = pre * pre
    bent = jnp.tanh(pre * (gelu_coef + (gelu_coef * cubic_coef) * squared))
    rise = 0.5 + 0.5 * bent
    value = pre * rise
    slope = rise + (value - value * rise) * (
        2.0 * gelu_coef + (6.0 * gelu_coef * cubic_coef) * squared
    )
    return value, slope


def expert_kernel(
    experts, steps, ahead,
    me_ref, recv_ref, router_get, cot_get, *refs,
):
    win_gets, wout_gets, g_gets = refs[:steps], refs[steps : 2 * steps], refs[2 * steps : 3 * steps]
    back_out, prod_out, x_out, rows_out, glog_out, gate_out, stage, acc_prod, acc_back = refs[3 * steps :]
    x_ref = x_out.ref
    slots = x_ref.shape[0]

    def put(c, values):
        x_ref[:, c * LANES : (c + 1) * LANES] = values.astype(bf16)

    from_slab(recv_ref, stage, slots, put)
    router = router_get()[...]
    wide = router.shape[1]
    logits = mm(x_ref[...], router)
    lane = lax.broadcasted_iota(jnp.int32, (slots, wide), 1)
    logits = jnp.where(lane < experts, logits, -jnp.inf)
    weights = jnp.exp(logits - jnp.max(logits, axis=-1, keepdims=True))
    probs = weights / jnp.sum(weights, axis=-1, keepdims=True)
    own = (lane == me_ref[0]).astype(f32)
    gate = jnp.sum(probs * own, axis=-1, keepdims=True)
    gate_out.ref[...] = jnp.broadcast_to(gate, (slots, LANES))
    gate_out.send()
    for step in range(steps):
        ahead(step + 2)
        win = win_gets[step]()[...]
        value, slope = activate(mm(x_ref[...], win))
        hidden = value.astype(bf16)
        act = (gate * g_gets[step]()[...].astype(f32) * slope).astype(bf16)
        prod, back = mm(hidden, wout_gets[step]()[...]), mm_nt(act, win)
        if step == 0:
            acc_prod[...] = prod
            acc_back[...] = back
        else:
            acc_prod[...] += prod
            acc_back[...] += back
    produced = acc_prod[...].astype(bf16).astype(f32)
    cot = cot_get()[...].astype(f32)
    rows_out.ref[...] = (gate * cot).astype(bf16)
    grad_gate = jnp.sum(cot * produced, axis=-1, keepdims=True)
    grad_logits = (probs * (own - gate) * grad_gate).astype(bf16)
    glog_out.ref[...] = grad_logits
    glog_out.send()
    to_slab(acc_back[...].astype(bf16).astype(f32) + mm_nt(grad_logits, router), stage, back_out.ref)
    back_out.send()
    x_out.send()
    rows_out.send()
    to_slab(produced, stage, prod_out.ref)


def expert_weights_kernel(
    x_ref, rows_ref, glog_ref, gate_ref, perm_ref, win_ref, g_ref, gin_ref, gout_ref, grouter_ref, xt
):
    @pl.when(pl.program_id(0) == 0)
    def _():
        xt[...] = jnp.transpose(x_ref[...].astype(f32)).astype(bf16)
        moved = mm(x_ref[...], perm_ref[...]).astype(bf16)
        grouter_ref[...] = mm_tn(moved, glog_ref[...])

    value, slope = activate(mm(x_ref[...], win_ref[0]))
    act = (gate_ref[:, 0:1] * g_ref[0].astype(f32) * slope).astype(bf16)
    gout_ref[0] = mm_tn(value.astype(bf16), rows_ref[...])
    gin_ref[0] = mm(xt[...], act)


def output_kernel(experts, recv_ref, dt_get, low_get, router_get, routes_get, after_get, out_out, stage, rows):
    def put(c, values):
        rows[:, c * LANES : (c + 1) * LANES] = values.astype(bf16)

    dt = dt_get()[...]
    from_slab(recv_ref, stage, dt.shape[1], put)
    produced = mm(dt, rows[...])
    logits = mm(low_get()[...], router_get()[...])
    lane = lax.broadcasted_iota(jnp.int32, logits.shape, 1)
    logits = jnp.where(lane < experts, logits, -jnp.inf)
    weights = jnp.exp(logits - jnp.max(logits, axis=-1, keepdims=True))
    own = (lane == routes_get()[...]).astype(f32)
    gate = jnp.sum(weights * own, axis=-1, keepdims=True) / jnp.sum(weights, axis=-1, keepdims=True)
    out_out.ref[...] = (after_get()[...] + gate * produced).astype(bf16)


def norm_two_kernel(
    experts,
    recv_ref, dt_get, after_get, gain_get, cot_get, wo_get, mixed_t_get, perm_get, grouter_get,
    grad_after_ref, grad_mixed_ref, keep_ref, send_ref,
    stage, rows,
):
    def put(c, values):
        rows[:, c * LANES : (c + 1) * LANES] = values.astype(bf16)

    slots = recv_ref.shape[0] * LANES // grad_mixed_ref.shape[1]
    from_slab(recv_ref, stage, slots, put)
    grad = mm(dt_get()[...], rows[...])
    after = after_get()[...]
    inverse = inverse_rms(after)
    unit = after * inverse
    scaled = grad * gain_get()[0:1, :]
    back = inverse * (scaled - unit * jnp.mean(scaled * unit, axis=-1, keepdims=True))
    grad_after = cot_get()[...].astype(f32) + back
    grad_after_ref[...] = grad_after
    low = grad_after.astype(bf16)
    grad_mixed_ref[...] = mm_nt(low, wo_get()[...]).astype(bf16)
    half = keep_ref.shape[0]
    width = low.shape[1]
    mixed_t_ref = mixed_t_get()
    keep_ref[:, :width] = mm(mixed_t_ref[:half, :], low)
    send_ref[:, :width] = mm(mixed_t_ref[half:, :], low).astype(bf16)
    gain_row = jnp.sum(grad * unit, axis=0, keepdims=True)
    high, rest = split_two(jnp.broadcast_to(gain_row, (8, width)))
    perm = perm_get()[...]
    gain_row = (mm(high, perm) + mm(rest, perm))[0:1, :]
    grouter = grouter_get()[...]
    lane = lax.broadcasted_iota(jnp.int32, grouter.shape, 1)
    packed = jnp.where(
        lane < experts, grouter, jnp.where(lane == experts, to_column(gain_row, grouter.shape[1]), 0.0)
    )
    keep_ref[:, width:] = packed[:half]
    send_ref[:, width:] = packed[half:].astype(bf16)


def unskew(skewed):
    span = 4 * LANES
    total = None
    for g in range(LANES // 8):
        moved = pltpu.roll(skewed[8 * g : 8 * g + 8, :], (LANES - 1 - 8 * g) % span, 1)
        total = moved if total is None else total + moved
    turned = jnp.concatenate([total[7 - s : 8 - s, :] for s in range(8)], axis=0)
    turned = pltpu.roll(turned, span - 7, 1, stride=1, stride_axis=0)
    return jnp.sum(turned, axis=0, keepdims=True)


def attend_backward_kernel(
    before, last, qkv_ref, probs_ref, gm_ref, normed_t_ref, own_ref, oth_ref, *refs
):
    refs = list(refs)
    total_in, vec_in, keep_in, send_in = (refs.pop(0) if b else None for b in before)
    if last:
        xperm_ref, hmask_ref, umask_ref = refs.pop(0), refs.pop(0), refs.pop(0)
    keep_ref, send_ref, dvec_ref, total_ref, dqkv_ref, dp_ref, ds_ref = refs
    earlier = 0 if keep_in is None else keep_in.shape[1]
    pairs_before = 0 if vec_in is None else vec_in.shape[0] // 2
    pair = pl.program_id(0)
    tokens = qkv_ref.shape[0]
    blocks = tokens // LANES
    low_half = lax.broadcasted_iota(jnp.int32, (tokens, LANES), 1) < HEAD_DIM
    lane = lax.broadcasted_iota(jnp.int32, (1, 4 * LANES), 1)
    query, keys, vals = (qkv_ref[:, k * LANES : (k + 1) * LANES] for k in range(3))
    grad = gm_ref[:, pl.ds(pl.multiple_of((pair + pairs_before) * LANES, LANES), LANES)]
    query_t = jnp.transpose(query.astype(f32)).astype(bf16)
    grad_t = jnp.transpose(grad.astype(f32)).astype(bf16)
    dq, dk_t, dv_t = [], [], []
    for k in range(2):
        keep = low_half if k == 0 else jnp.logical_not(low_half)
        dp_ref[k] = mm_nt(jnp.where(keep, grad, jnp.zeros_like(grad)), vals)
    for k in range(2):
        strip = [None] * 3
        far_left = far_right = None
        for i in range(blocks):
            rows = slice(i * LANES, (i + 1) * LANES)
            dp = dp_ref[k, rows, :]
            probs = probs_ref[k, rows, :].astype(f32)
            delta = jnp.sum(probs * dp, axis=-1, keepdims=True)
            ds = (probs * (dp - delta)).astype(bf16)
            ds_ref[k, rows, :] = ds
            wide = ds.astype(f32)
            for j in range(blocks):
                piece = wide[:, j * LANES : (j + 1) * LANES]
                if j < i - 1:
                    far_left = piece if far_left is None else far_left + piece
                elif j > i + 1:
                    far_right = piece if far_right is None else far_right + piece
                else:
                    at = j - i + 1
                    strip[at] = piece if strip[at] is None else strip[at] + piece
        part = slice(k * HEAD_DIM, (k + 1) * HEAD_DIM)
        dq.append(mm(ds_ref[k], keys))
        dk_t.append(mm(query_t[part, :], ds_ref[k]))
        dv_t.append(mm(grad_t[part, :], probs_ref[k]))
        vec = unskew(jnp.concatenate(strip + [jnp.zeros((LANES, LANES), f32)], axis=1))
        left = jnp.sum(jnp.sum(far_left, axis=0, keepdims=True), axis=1, keepdims=True)
        right = jnp.sum(jnp.sum(far_right, axis=0, keepdims=True), axis=1, keepdims=True)
        vec = vec + jnp.where(lane == 0, left, 0.0) + jnp.where(lane == 510, right, 0.0)
        dvec_ref[pl.ds((pair + pairs_before) * 2 + k, 1), :] = vec
    dqkv_ref[:, :LANES] = (jnp.where(low_half, dq[0], dq[1]) * HEAD_DIM ** (-0.5)).astype(bf16)
    dqkv_ref[:, LANES : 2 * LANES] = jnp.transpose(jnp.concatenate(dk_t, axis=0)).astype(bf16)
    dqkv_ref[:, 2 * LANES :] = jnp.transpose(jnp.concatenate(dv_t, axis=0)).astype(bf16)
    half = keep_ref.shape[0]
    grads = dqkv_ref[...]
    cols = pl.ds(pl.multiple_of(pair * BLOCK, LANES) + earlier, BLOCK)
    send_ref[:, cols] = mm(normed_t_ref[half:, :], grads).astype(bf16)
    keep_ref[:, cols] = mm(normed_t_ref[:half, :], grads)
    one, two = mm_nt(grads, own_ref[...]), mm_nt(grads, oth_ref[...])

    @pl.when(pair == 0)
    def _():
        if total_in is None:
            total_ref[:, :half] = one
            total_ref[:, half:] = two
        else:
            total_ref[:, :half] = total_in[:, :half] + one
            total_ref[:, half:] = total_in[:, half:] + two
        if vec_in is not None:
            dvec_ref[: 2 * pairs_before, :] = vec_in[...]
        if keep_in is not None:
            keep_ref[:, :earlier] = keep_in[...]
            send_ref[:, :earlier] = send_in[...]

    @pl.when(pair > 0)
    def _():
        total_ref[:, :half] += one
        total_ref[:, half:] += two

    if not last:
        return

    @pl.when(pair == pl.num_programs(0) - 1)
    def _():
        x = xperm_ref[...].astype(f32)
        unit = x * inverse_rms(x)
        gain_col = to_column(jnp.sum(total_ref[...] * unit, axis=0, keepdims=True))
        table_col = table_column(
            jnp.concatenate([dvec_ref[...], jnp.zeros((16 - HEADS, 4 * LANES), f32)], axis=0),
            hmask_ref,
            umask_ref,
        )
        lane = lax.broadcasted_iota(jnp.int32, gain_col.shape, 1)
        packed = jnp.where(lane == 0, gain_col, jnp.where(lane == 1, table_col, 0.0))
        keep_ref[:, PART * BLOCK :] = packed[:half]
        send_ref[:, PART * BLOCK :] = packed[half:].astype(bf16)


def split_three(values):
    one, rest = split_two(values)
    two, three = split_two(values - one.astype(f32))
    return one, two, three


def table_column(vec, hmask_ref, umask_ref):
    offset = lax.broadcasted_iota(jnp.int32, (LANES, 4 * LANES), 1) - 255
    onehot = (
        lax.broadcasted_iota(jnp.int32, (LANES, 4 * LANES), 0) == buckets_of(offset)
    ).astype(f32).astype(bf16)
    one, two, three = split_three(vec)
    table = mm_nt(one, onehot) + (mm_nt(two, onehot) + mm_nt(three, onehot))
    heads = hmask_ref[:, :16]
    one, two, three = split_three(table)
    spread = mm(heads, one) + (mm(heads, two) + mm(heads, three))
    return jnp.sum(spread * umask_ref[...].astype(f32), axis=1, keepdims=True)


def last_kernel(total_ref, xperm_get, gain_get, perm_get, after_ref, out_out):
    grad = total_ref[...]
    x = xperm_get()[...].astype(f32)
    inverse = inverse_rms(x)
    unit = x * inverse
    scaled = grad * gain_get()[0:1, :]
    back = inverse * (scaled - unit * jnp.mean(scaled * unit, axis=-1, keepdims=True))
    high, rest = split_two(back)
    perm = perm_get()[...]
    out_out.ref[...] = (after_ref[...] + (mm_nt(high, perm) + mm_nt(rest, perm))).astype(bf16)


def fold_kernel(plan, *refs):
    refs = list(refs)
    total_in = sum(1 + n for n, _ in plan)
    ins, outs = refs[:total_in], refs[total_in:]
    for arrived, parts in plan:
        total = ins.pop(0)[...]
        for _ in range(arrived):
            total = total + ins.pop(0)[...].astype(f32)
        rows = total.shape[0] // parts
        outs.pop(0)[...] = total[:rows]
        for m in range(1, parts):
            outs.pop(0)[...] = total[m * rows : (m + 1) * rows].astype(bf16)


def summed(first_ref, moved):
    total = first_ref[...]
    for piece in moved:
        total = total + piece[...].astype(f32)
    return total


def as_row(column):
    size = column.shape[0]
    same = lax.broadcasted_iota(jnp.int32, (size, size), 0) == lax.broadcasted_iota(
        jnp.int32, (size, size), 1
    )
    return jnp.sum(jnp.where(same, column, 0.0), axis=0, keepdims=True)


def rest_sums_kernel(first_ref, *refs):
    *moved, wo_out, router_out, gain_out = refs
    total = summed(first_ref, moved)
    width, experts = wo_out.ref.shape[1], router_out.ref.shape[1]
    wo_out.ref[...] = total[:, :width]
    router_out.ref[...] = total[:, width : width + experts]
    gain_out.ref[...] = as_row(total[:, width + experts : width + experts + 1])


def finish_kernel(a_ref, b_ref, *refs):
    *moved, wq_out, wk_out, wv_out, gain_out, table_out = refs
    total = summed(b_ref, moved)
    for c in range(PAIRS):
        source = a_ref if c < PART else total
        for k, out in enumerate((wq_out, wk_out, wv_out)):
            at = (c % PART) * BLOCK + k * LANES
            out.ref[:, c * LANES : (c + 1) * LANES] = source[:, at : at + LANES]
    for out in (wq_out, wk_out, wv_out):
        out.send()
    at = PART * BLOCK
    gain_out.ref[...] = as_row(total[:, at : at + 1])
    entries = table_out.ref.shape[1]
    table_out.ref[...] = as_row(total[:, at + 1 : at + 2])[:, :entries]


def expert_call(experts, steps, slab, outs, scratch):
    def run(me, recv, router, cot, win, wout, hidden):
        far_args = [router, cot, win, wout, hidden]
        n_far = 2 + 3 * steps
        copies = [pltpu.VMEM(router.shape, router.dtype), pltpu.VMEM(cot.shape, cot.dtype)]
        copies += [pltpu.VMEM(a.shape[1:], a.dtype) for a in (win, wout, hidden) for _ in range(steps)]
        out_copies = [pltpu.VMEM(o.shape, o.dtype) for o in outs]

        def wrapped(me_ref, recv_ref, router_ref, cot_ref, win_ref, wout_ref, hidden_ref, *refs):
            refs = list(refs)
            results, refs = refs[: len(outs)], refs[len(outs) :]
            own, refs = refs[: len(scratch)], refs[len(scratch) :]
            fetched, refs = refs[:n_far], refs[n_far:]
            stored, sems = refs[: len(outs)], refs[len(outs) :]
            sources = [router_ref, cot_ref]
            sources += [r.at[i] for r in (win_ref, wout_ref, hidden_ref) for i in range(steps)]
            gets = [
                Fetched(pltpu.make_async_copy(a, b, c), b) for a, b, c in zip(sources, fetched, sems)
            ]
            def ahead(step):
                if step < steps:
                    for i in (2 + step, 2 + 2 * steps + step, 2 + steps + step):
                        gets[i].copy.start()
                elif step == steps:
                    gets[1].copy.start()

            gets[0].copy.start()
            ahead(0)
            ahead(1)
            made = [
                Stored(pltpu.make_async_copy(b, a, c), b)
                for a, b, c in zip(results, stored, sems[n_far:])
            ]
            expert_kernel(experts, steps, ahead, me_ref, recv_ref, *gets, *made, *own)
            for item in made:
                if not item.sent:
                    item.send()
            for item in made:
                item.copy.wait()

        any_ref, vmem_ref = (pl.BlockSpec(memory_space=m) for m in (pl.ANY, pltpu.VMEM))
        return pl.pallas_call(
            wrapped,
            out_shape=list(outs),
            in_specs=[pl.BlockSpec(memory_space=pltpu.SMEM), vmem_ref] + [any_ref] * len(far_args),
            out_specs=[any_ref] * len(outs),
            scratch_shapes=list(scratch)
            + copies
            + out_copies
            + [pltpu.SemaphoreType.DMA] * (n_far + len(outs)),
            **parameters(48),
        )(me, recv, *[place(Far(a)) for a in far_args])

    return run


def shards(
    count,
    inputs,
    segment_ids,
    routes,
    cotangent,
    gain_attn,
    gain_ffn,
    bias_table,
    w_query,
    w_key,
    w_value,
    w_output,
    w_router,
    w_in,
    w_out,
):
    tokens, width = inputs.shape
    experts = w_router.shape[1]
    rows_local = w_query.shape[0]
    entries = bias_table.shape[0]
    hidden_units = w_in.shape[2]
    capacity = max(2, 5 * tokens // (4 * experts))
    slots = experts * capacity
    blocks = width // LANES
    half = width // 2
    wide = -(-(experts + 1) // LANES) * LANES
    me = lax.axis_index("seq").astype(jnp.int32).reshape(1)
    vmem = pl.BlockSpec(memory_space=pltpu.VMEM)

    groups = bit_groups(count)
    levels = list(reversed(groups[1:]))
    columns = PART * BLOCK
    piece, tail = flat_call(
        functools.partial(pack_kernel, experts),
        [near((rows_local, 2 * columns + LANES), bf16), near((rows_local, width + wide), bf16)],
    )(
        *map(Far, (gain_attn[None, :], gain_ffn[None, :], bias_table[None, :])),
        *map(Far, (w_query, w_key, w_value, w_output, w_router)),
    )

    def reach(values, low_bit, bits):
        return [swap(values, m << low_bit, count) for m in range(1, 1 << bits)]

    def join(values, moved):
        return jnp.concatenate([values, *moved], axis=0)

    order = np.asarray(relative_order(count), np.int32)
    rel_row = jnp.asarray(np.repeat(order, rows_local)[None, :])
    off_row = jnp.asarray(np.tile(np.arange(rows_local, dtype=np.int32), count)[None, :])
    slab = (slots * blocks, LANES)
    slab_stage = pltpu.VMEM(slab, f32)
    perm, xperm, segrow, segcol, hmask, umask, dt, dm = flat_call(
        functools.partial(prepare_kernel, rows_local, entries, experts, capacity),
        [
            far((width, width), bf16),
            far((tokens, width), bf16),
            far((8, tokens), f32),
            far((tokens, LANES), f32),
            far((width, LANES), bf16),
            far((width, LANES), bf16),
            far((tokens, slots), bf16),
            far((slots, tokens), bf16),
        ],
    )(me, Far(rel_row), Far(off_row), Far(inputs), Far(segment_ids), Far(routes))
    cot_send = flat_call(dispatch_kernel, [far(slab, bf16)], scratch=[slab_stage])(
        Far(dm), Far(cotangent)
    )[0]

    moved = reach(piece, *levels[0])
    beside = [perm]
    for k, level in enumerate(levels[1:]):
        moved = lax.optimization_barrier((*moved, *beside))[: len(moved)]
        piece = join(piece, moved)
        moved = reach(piece, *level)
        tail_moved = reach(after(tail, piece), *levels[k])
        tail_moved = lax.optimization_barrier((*tail_moved, cot_send))[:-1]
        tail = join(tail, tail_moved)
        beside = [tail]
    moved = lax.optimization_barrier((*moved, *beside))[: len(moved)]
    piece = join(piece, moved)
    other = swap(piece, 1, count)
    tail_moved = reach(after(tail, piece), *levels[-1])

    slab_split = (count, slots * blocks // count, LANES)

    def exchange(rows):
        return lax.all_to_all(
            rows.reshape(slab_split), "seq", split_axis=0, concat_axis=0, tiled=True
        ).reshape(slab)

    cot_recv = exchange(after(cot_send, other))

    def whole(shape):
        return pl.BlockSpec(shape, lambda i: (0,) * len(shape))

    pair_probs = pl.BlockSpec((2, tokens, tokens), lambda i: (i, 0, 0))
    piece, other = Far(piece), Far(other)
    small_block = pl.BlockSpec((half, LANES), lambda i: (0, 2 * columns // LANES))
    pair_weights = pl.BlockSpec((half, BLOCK), lambda i: (0, i))
    qkv, probs, mixed, normed, gain_one = grid_call(
        attend_forward_kernel,
        [
            far((tokens, PAIRS * BLOCK), bf16),
            far((HEADS, tokens, tokens), bf16),
            near((tokens, width), bf16),
            far((tokens, width), bf16),
            far((8, width), f32),
        ],
        grid=(PAIRS,),
        in_specs=[whole((tokens, width))]
        + [pair_weights, pair_weights, small_block, small_block]
        + [whole(shape) for shape in ((width, LANES), (width, LANES), (8, tokens), (tokens, LANES))],
        out_specs=[
            pl.BlockSpec((tokens, BLOCK), lambda i: (0, i)),
            pair_probs,
            vmem,
            whole((tokens, width)),
            whole((8, width)),
        ],
        scratch=[
            pltpu.VMEM((16, 4 * LANES), f32),
            pltpu.VMEM((2, tokens, tokens), f32),
            pltpu.VMEM((2, LANES, 3 * LANES), f32),
        ],
    )(
        Far(after(xperm, tail)), piece, other, piece, other,
        *map(Far, (hmask, umask, segrow, segcol)),
    )
    tail_moved = lax.optimization_barrier((*tail_moved, mixed))[:-1]
    tail = join(tail, tail_moved)
    tail_other = swap(tail, 1, count)

    after_rows, low_two, row_send, gain_two, mixed_perm = flat_call(
        functools.partial(after_kernel, experts),
        [
            far((tokens, width), f32),
            far((tokens, width), bf16),
            far(slab, bf16),
            far((8, width), f32),
            far((tokens, width), bf16),
        ],
        scratch=[slab_stage],
    )(mixed, Far(perm), tail, tail_other, Far(inputs), Far(dm))
    row_recv = exchange(row_send)

    steps = 6
    units = hidden_units // steps
    weight_in = pl.BlockSpec((1, width, units), lambda i: (0, 0, i))
    weight_out = pl.BlockSpec((1, units, width), lambda i: (0, i, 0))

    def stacked(rows, cols):
        return pl.BlockSpec((1, rows, cols), lambda i: (i, 0, 0))

    cot_rows, win_low, wout_low, grad_hidden = grid_call(
        early_expert_kernel,
        [
            far((slots, width), bf16),
            far((steps, width, units), bf16),
            far((steps, units, width), bf16),
            far((steps, slots, units), bf16),
        ],
        grid=(steps,),
        in_specs=[whole(slab), weight_in, weight_out],
        out_specs=[
            whole((slots, width)),
            stacked(width, units),
            stacked(units, width),
            stacked(slots, units),
        ],
        scratch=[slab_stage],
    )(cot_recv, Far(w_in), Far(w_out))
    mixed_t, normed_t, output_w, router_w = flat_call(
        between_kernel,
        [
            far((width, tokens), bf16),
            far((width, tokens), bf16),
            far((width, width), bf16),
            far((width, wide), bf16),
        ],
    )(Far(mixed_perm), Far(normed), tail, tail_other, Far(perm))
    back_send, prod_send, x_rows, grad_rows, grad_logits, gates = expert_call(
        experts, steps, slab,
        [
            far(slab, bf16),
            far(slab, bf16),
            far((slots, width), bf16),
            far((slots, width), bf16),
            far((slots, wide), bf16),
            far((slots, LANES), f32),
        ],
        [slab_stage, pltpu.VMEM((slots, width), f32), pltpu.VMEM((slots, width), f32)],
    )(me, row_recv, router_w, cot_rows, win_low, wout_low, grad_hidden)
    back_recv = exchange(back_send)
    grad_inner, grad_outer, grad_router = grid_call(
        expert_weights_kernel,
        [
            far((1, width, hidden_units), f32),
            far((1, hidden_units, width), f32),
            far((width, wide), f32),
        ],
        grid=(steps,),
        in_specs=[
            whole((slots, width)),
            whole((slots, width)),
            whole((slots, wide)),
            whole((slots, LANES)),
            whole((width, width)),
            stacked(width, units),
            stacked(slots, units),
        ],
        out_specs=[weight_in, weight_out, whole((width, wide))],
        scratch=[pltpu.VMEM((width, slots), bf16)],
    )(*map(Far, (x_rows, grad_rows, grad_logits, gates, perm, win_low, grad_hidden)))
    prod_recv = exchange(after(prod_send, grad_router))

    row_scratch = pltpu.VMEM((slots, width), bf16)
    grad_after, grad_mixed, keep_o, send_o = flat_call(
        functools.partial(norm_two_kernel, experts),
        [
            near((tokens, width), f32),
            near((tokens, width), bf16),
            near((half, width + wide), f32),
            near((half, width + wide), bf16),
        ],
        scratch=[slab_stage, row_scratch],
    )(
        back_recv,
        *map(Far, (dt, after_rows, gain_two, cotangent, output_w, mixed_t, perm, grad_router)),
    )

    def backward(start, stop, ready):
        last = stop == PAIRS
        sums = dict(before)
        if start != PART and start:
            held_back = [sums["total"], sums["vec"], sums["keep"], sums["send"]]
        else:
            held_back = [sums.get("total"), sums.get("vec"), None, None]
        here = [Far(qkv), Far(probs), after(grad_mixed, *ready), Far(normed_t), piece, other]
        specs = [
            pl.BlockSpec((tokens, BLOCK), lambda i: (0, i + start)),
            pl.BlockSpec((2, tokens, tokens), lambda i: (i + start, 0, 0)),
            vmem,
            whole((width, tokens)),
        ] + [pl.BlockSpec((half, BLOCK), lambda i: (0, i + start))] * 2
        given = [v for v in held_back if v is not None]
        here += given
        specs += [vmem] * len(given)
        if last:
            here += [Far(xperm), Far(hmask), Far(umask)]
            specs += [whole(shape) for shape in ((tokens, width), (width, LANES), (width, LANES))]
        cols = (stop - (PART if stop > PART else 0)) * BLOCK + (LANES if last else 0)
        keep, send, vec, total = grid_call(
            functools.partial(attend_backward_kernel, [v is not None for v in held_back], last),
            [
                near((half, cols), f32),
                near((half, cols), bf16),
                near((2 * stop, 4 * LANES), f32),
                near((tokens, width), f32),
            ],
            grid=(stop - start,),
            in_specs=specs,
            out_specs=[vmem] * 4,
            scratch=[
                pltpu.VMEM((tokens, BLOCK), bf16),
                pltpu.VMEM((2, tokens, tokens), f32),
                pltpu.VMEM((2, tokens, tokens), bf16),
            ],
            vmem=24,
        )(*here)
        before.update(total=total, vec=vec, keep=keep, send=send)
        return total, ((keep, send) if stop in (PART, PAIRS) else None)

    def results(ready):
        return flat_call(
            functools.partial(output_kernel, experts),
            [far((tokens, width), bf16)],
            scratch=[slab_stage, row_scratch],
            vmem=20,
        )(after(prod_recv, *ready), *map(Far, (dt, low_two, router_w, routes, after_rows)))[0], None

    def finish(ready):
        return flat_call(last_kernel, [far((tokens, width), bf16)], vmem=20)(
            after(before["total"], *ready), Far(xperm), Far(gain_one), Far(perm), grad_after
        )[0], None

    before = {}
    work = [
        functools.partial(backward, 0, PART),
        functools.partial(backward, PART, PART + 1),
        functools.partial(backward, PART + 1, PAIRS),
        results,
        finish,
    ]
    ups = groups[1:]
    done = []
    own, out_going, began = [keep_o], [[send_o]], [0]
    final = [None, None]
    slot = 0
    while True:
        moving = {}
        for c in range(len(own)):
            stage_no = slot - began[c]
            if stage_no == 0:
                moving[c] = [swap(out_going[c][0], 1, count)]
            elif 0 < stage_no <= len(ups):
                low_bit, _ = ups[stage_no - 1]
                moving[c] = [
                    swap(piece, (m + 1) << low_bit, count) for m, piece in enumerate(out_going[c])
                ]
        fresh = None
        if slot < len(work):
            value, fresh = work[slot]([own[c] for c in moving])
            done.append(value)
            for c, pieces in moving.items():
                moving[c] = list(lax.optimization_barrier((*pieces, value))[:-1])
        plan, args, outs = [], [], []
        for c, pieces in list(moving.items()):
            if slot - began[c] == len(ups) and c != 1:
                final[c // 2] = (own[c], *pieces)
                continue
            parts = 1 << ups[slot - began[c]][1] if slot - began[c] < len(ups) else 1
            plan.append((c, len(pieces), parts))
            args += [own[c], *pieces]
            rows, cols = own[c].shape[0] // parts, own[c].shape[1]
            outs.append(near((rows, cols), f32))
            outs += [near((rows, cols), bf16)] * (parts - 1)
        if plan:
            folded = list(
                flat_call(
                    functools.partial(fold_kernel, [p[1:] for p in plan]), outs, vmem=16
                )(*args)
            )
            for c, _, parts in plan:
                own[c] = folded.pop(0)
                out_going[c] = [folded.pop(0) for _ in range(parts - 1)]
        if fresh is not None:
            own.append(fresh[0])
            out_going.append([fresh[1]])
            began.append(slot + 1)
        if final[1] is not None:
            break
        slot += 1

    def row(size):
        return far((1, size), f32)

    square = far((rows_local, width), f32)
    grad_wo, grad_wr, grad_gain_two = flat_call(
        rest_sums_kernel, [square, far((rows_local, experts), f32), row(rows_local)], vmem=16
    )(*final[0])
    grad_q, grad_k, grad_v, grad_gain_one, grad_table = flat_call(
        finish_kernel, [square, square, square, row(rows_local), row(entries)], vmem=16
    )(own[1], *final[1])
    output, grad_inputs = done[3], done[4]

    return (
        output,
        grad_inputs,
        grad_gain_one[0],
        grad_gain_two[0],
        grad_table[0],
        grad_q,
        grad_k,
        grad_v,
        grad_wo,
        grad_wr,
        grad_inner,
        grad_outer,
    )


def solution(mesh):
    row, flat, cube = P("seq", None), P("seq"), P("seq", None, None)
    in_specs = (row,) * 4 + (flat,) * 3 + (row,) * 5 + (cube,) * 2
    out_specs = (row,) * 2 + (flat,) * 3 + (row,) * 5 + (cube,) * 2
    return jax.shard_map(
        functools.partial(shards, mesh.shape["seq"]),
        mesh=mesh,
        in_specs=in_specs,
        out_specs=out_specs,
        check_vma=False,
    )
```

```python
import functools

import jax
import jax.numpy as jnp
import numpy as np
from jax import lax
from jax.experimental import pallas as pl
from jax.experimental.pallas import tpu as pltpu
from jax.sharding import PartitionSpec as P

HEADS = 12
HEAD_DIM = 64
BUCKETS = 32
PAIRS = HEADS // 2
RUNS = (0, 3, 6)
LANES = 128
BLOCK = 3 * LANES

epsilon = 1e-06
bucket_edges = (1, 2, 3, 4, 5, 6, 7, 8, 12, 16, 23, 32, 46, 64, 91)
gelu_coef = 0.7978845608028654
cubic_coef = 0.044715

f32 = jnp.float32
bf16 = jnp.bfloat16


def bit_groups(count):
    bits = count.bit_length() - 1
    groups, low = [(0, 1)], 1
    while low < bits:
        width = min(2, bits - low)
        groups.append((low, width))
        low += width
    return groups


def relative_order(count):
    order = [0]
    for low, width in bit_groups(count):
        order = [base + (m << low) for base in order for m in range(1 << width)]
    return order


def swap(values, distance, count):
    return lax.ppermute(values, "seq", [(i, i ^ distance) for i in range(count)])


def after(values, *others):
    return lax.optimization_barrier((values, *others))[0]


def mm(left, right):
    return jnp.dot(left, right, preferred_element_type=f32)


def mm_nt(left, right):
    return lax.dot_general(left, right, (((1,), (1,)), ((), ())), preferred_element_type=f32)


def mm_tn(left, right):
    return lax.dot_general(left, right, (((0,), (0,)), ((), ())), preferred_element_type=f32)


def split_two(values):
    high = values.astype(bf16)
    return high, (values - high.astype(f32)).astype(bf16)


class Far:
    def __init__(self, values):
        self.values = values


def near(shape, dtype):
    return pltpu.VMEM(shape, dtype)


def far(shape, dtype):
    return pltpu.HBM(shape, dtype)


class Fetched:
    def __init__(self, copy, ref):
        self.copy, self.ref, self.here = copy, ref, False

    def __call__(self):
        if not self.here:
            self.copy.wait()
            self.here = True
        return self.ref


class Stored:
    def __init__(self, copy, ref):
        self.copy, self.ref, self.sent = copy, ref, False

    def send(self):
        self.copy.start()
        self.sent = True


def place(a):
    if isinstance(a, Far):
        return pltpu.with_memory_space_constraint(a.values, pltpu.HBM)
    return a


def parameters(vmem, us):
    return dict(
        compiler_params=pltpu.CompilerParams(vmem_limit_bytes=vmem * 1024 * 1024),
        cost_estimate=pl.CostEstimate(
            flops=int(us * 10**9), bytes_accessed=int(us * 10**6), transcendentals=0
        ),
    )


def grid_call(body, outs, grid, in_specs, out_specs, us, scratch=(), vmem=40):
    call = pl.pallas_call(
        body,
        out_shape=list(outs),
        grid=grid,
        in_specs=in_specs,
        out_specs=out_specs,
        scratch_shapes=list(scratch),
        **parameters(vmem, us),
    )
    return lambda *args: call(*[place(a) for a in args])


def flat_call(body, outs, us, scratch=(), vmem=32):
    def run(*args):
        lazy = [isinstance(a, Far) for a in args]
        late = [o.memory_space == pltpu.HBM for o in outs]
        values = [a.values if f else a for a, f in zip(args, lazy)]
        n_in, n_out, n_scratch = len(args), len(outs), len(scratch)
        any_ref, vmem_ref, smem_ref = (
            pl.BlockSpec(memory_space=m) for m in (pl.ANY, pltpu.VMEM, pltpu.SMEM)
        )
        in_copies = [pltpu.VMEM(v.shape, v.dtype) for v, f in zip(values, lazy) if f]
        out_copies = [pltpu.VMEM(o.shape, o.dtype) for o, f in zip(outs, late) if f]

        def wrapped(*refs):
            ins, rest = refs[:n_in], refs[n_in:]
            results, rest = rest[:n_out], rest[n_out:]
            own, rest = rest[:n_scratch], rest[n_scratch:]
            fetched, rest = list(rest[: len(in_copies)]), rest[len(in_copies) :]
            stored, rest = list(rest[: len(out_copies)]), rest[len(out_copies) :]
            sems = list(rest)
            given, made = [], []
            for ref, f in zip(ins, lazy):
                if f:
                    copy = pltpu.make_async_copy(ref, fetched[0], sems.pop())
                    copy.start()
                    given.append(Fetched(copy, fetched.pop(0)))
                else:
                    given.append(ref)
            for ref, f in zip(results, late):
                if f:
                    made.append(
                        Stored(pltpu.make_async_copy(stored[0], ref, sems.pop()), stored[0])
                    )
                    stored.pop(0)
                else:
                    made.append(ref)
            body(*given, *made, *own)
            for item in given:
                if isinstance(item, Fetched):
                    item()
            for item in made:
                if isinstance(item, Stored):
                    if not item.sent:
                        item.send()
                    item.copy.wait()

        return pl.pallas_call(
            wrapped,
            out_shape=list(outs),
            in_specs=[
                any_ref if f else (smem_ref if v.size == 1 else vmem_ref)
                for v, f in zip(values, lazy)
            ],
            out_specs=[any_ref if f else vmem_ref for f in late],
            scratch_shapes=list(scratch)
            + in_copies
            + out_copies
            + [pltpu.SemaphoreType.DMA] * (len(in_copies) + len(out_copies)),
            **parameters(vmem, us),
        )(*[place(a) for a in args])

    return run


def to_slab(values, stage, out_ref):
    slots, width = values.shape
    blocks = width // LANES
    for c in range(blocks):
        stage[pl.ds(c, slots, stride=blocks), :] = values[:, c * LANES : (c + 1) * LANES]
    out_ref[...] = stage[...].astype(out_ref.dtype)


def from_slab(in_ref, stage, slots, put):
    stage[...] = in_ref[...].astype(f32)
    blocks = in_ref.shape[0] // slots
    for c in range(blocks):
        put(c, stage[pl.ds(c, slots, stride=blocks), :])


def to_column(row, width=LANES):
    return jnp.transpose(jnp.broadcast_to(row, (width, row.shape[1])))


def inverse_rms(values):
    return lax.rsqrt(jnp.mean(values * values, axis=-1, keepdims=True) + epsilon)


def buckets_of(offset):
    magnitude = jnp.abs(offset)
    bucket = jnp.zeros(offset.shape, jnp.int32)
    for edge in bucket_edges:
        bucket = bucket + (magnitude >= edge).astype(jnp.int32)
    return bucket + BUCKETS // 2 * (offset > 0).astype(jnp.int32)


def prepare_kernel(
    rows_local, entries, experts, capacity,
    me_ref, rel_ref, off_ref, x_get, seg_get, routes_get,
    perm_out, xperm_out, segrow_out, segcol_out, hmask_out, umask_out, dt_out, dm_out,
):
    perm_ref, xperm_ref, segrow_ref, segcol_ref, hmask_ref, umask_ref, dt_ref, dm_ref = (
        out.ref
        for out in (perm_out, xperm_out, segrow_out, segcol_out, hmask_out, umask_out, dt_out, dm_out)
    )
    x_ref, seg_ref, routes_ref = x_get(), seg_get(), routes_get()
    tokens, width = x_ref.shape
    slots = dm_ref.shape[0]
    me = me_ref[0]
    device_row = rel_ref()[...] ^ me
    off_row = off_ref()[...]
    true_row = device_row * rows_local + off_row
    perm = (lax.broadcasted_iota(jnp.int32, (width, width), 0) == true_row).astype(f32).astype(bf16)
    perm_ref[...] = perm
    perm_out.send()
    xperm_ref[...] = mm(x_ref[...], perm).astype(bf16)
    segments = seg_ref[...].astype(f32)
    segrow_ref[...] = jnp.broadcast_to(segments, segrow_ref.shape)
    segcol_ref[...] = to_column(segments)
    flat = device_row * entries + off_row
    bucket_row = ((flat.astype(f32) + 0.5) * (1.0 / HEADS)).astype(jnp.int32)
    head_row = jnp.where(off_row < entries, flat - bucket_row * HEADS, -1)
    bucket_col = to_column(bucket_row.astype(f32))
    head_col = to_column(head_row.astype(f32))
    lane = lax.broadcasted_iota(jnp.int32, (width, LANES), 1).astype(f32)
    hmask_ref[...] = (head_col == lane).astype(f32).astype(bf16)
    umask_ref[...] = (bucket_col == lane).astype(f32).astype(bf16)
    routes = routes_ref[...]
    labels = lax.broadcasted_iota(jnp.int32, (tokens, experts), 1)
    picked = (routes == labels).astype(f32)
    earlier = (
        lax.broadcasted_iota(jnp.int32, (tokens, tokens), 1)
        <= lax.broadcasted_iota(jnp.int32, (tokens, tokens), 0)
    ).astype(f32).astype(bf16)
    counts = mm(earlier, picked.astype(bf16))
    position = jnp.sum(counts * picked, axis=1, keepdims=True) - 1.0
    slot_col = jnp.where(
        position < capacity, routes.astype(f32) * capacity + position, -1.0
    )
    slot_lane = lax.broadcasted_iota(jnp.int32, (tokens, slots), 1).astype(f32)
    dt_ref[...] = (slot_col == slot_lane).astype(f32).astype(bf16)
    slot_row = jnp.transpose(jnp.broadcast_to(slot_col, (tokens, LANES)))[0:1, :]
    slot_sub = lax.broadcasted_iota(jnp.int32, (slots, tokens), 0).astype(f32)
    dm_ref[...] = (slot_sub == slot_row).astype(f32).astype(bf16)


def dispatch_kernel(dm_get, cot_get, send_out, stage):
    to_slab(mm(dm_get()[...], cot_get()[...]), stage, send_out.ref)


def pack_kernel(
    experts, gain_get, gain_two_get, table_get, wq_get, wk_get, wv_get, wo_get, router_get,
    piece, tail,
):
    gain_ref, gain_two_ref, table_ref = gain_get(), gain_two_get(), table_get()
    wq_ref, wk_ref, wv_ref, wo_ref, router_ref = (
        get() for get in (wq_get, wk_get, wv_get, wo_get, router_get)
    )
    rows, width = wq_ref.shape

    def column(ref):
        size = ref.shape[1]
        same = lax.broadcasted_iota(jnp.int32, (rows, size), 0) == lax.broadcasted_iota(
            jnp.int32, (rows, size), 1
        )
        return jnp.sum(jnp.where(same, ref[...], 0.0), axis=1, keepdims=True)

    for c in range(PAIRS):
        for k, w in enumerate((wq_ref, wk_ref, wv_ref)):
            at = c * BLOCK + k * LANES
            piece[:, at : at + LANES] = w[:, c * LANES : (c + 1) * LANES].astype(bf16)
    lane = lax.broadcasted_iota(jnp.int32, (rows, LANES), 1)
    small = jnp.where(lane == 0, column(gain_ref), jnp.where(lane == 1, column(table_ref), 0.0))
    piece[:, PAIRS * BLOCK :] = small.astype(bf16)
    tail[:, :width] = wo_ref[...].astype(bf16)
    lane = lax.broadcasted_iota(jnp.int32, (rows, tail.shape[1] - width), 1)
    tail[:, width:] = jnp.where(lane == experts, column(gain_two_ref), 0.0).astype(bf16)
    tail[:, width : width + experts] = router_ref[...].astype(bf16)


def attend_forward_kernel(
    xperm_ref, own_ref, oth_ref, own_small, oth_small, hmask_ref, umask_ref, segrow_ref, segcol_ref,
    qkv_ref, probs_ref, mixed_ref, normed_ref, gain_ref,
    vec_ref, score_ref, strip_ref,
):
    half = own_ref.shape[0]
    tokens = segcol_ref.shape[0]
    blocks = tokens // LANES
    pair = pl.program_id(0)

    @pl.when(pair == 0)
    def _():
        packed = jnp.concatenate([own_small[...].astype(f32), oth_small[...].astype(f32)], axis=0)
        gain = jnp.transpose(packed)[0:1, :]
        gain_ref[...] = jnp.broadcast_to(gain, gain_ref.shape)
        spread = (packed[:, 1:2] * hmask_ref[...].astype(f32)).astype(bf16)
        table = mm_tn(spread, umask_ref[...])[:16]
        offset = lax.broadcasted_iota(jnp.int32, (LANES, 4 * LANES), 1) - 255
        onehot = (
            lax.broadcasted_iota(jnp.int32, (LANES, 4 * LANES), 0) == buckets_of(offset)
        ).astype(f32).astype(bf16)
        vec_ref[...] = mm(table.astype(bf16), onehot)
        x = xperm_ref[...].astype(f32)
        normed_ref[...] = (x * inverse_rms(x) * gain).astype(bf16)

    qkv = mm(normed_ref[:, :half], own_ref[...]) + mm(normed_ref[:, half:], oth_ref[...])
    query = (qkv[:, :LANES].astype(bf16) * HEAD_DIM ** (-0.5)).astype(bf16)
    keys = qkv[:, LANES : 2 * LANES].astype(bf16)
    vals = qkv[:, 2 * LANES :].astype(bf16)
    qkv_ref[:, :LANES] = query
    qkv_ref[:, LANES : 2 * LANES] = keys
    qkv_ref[:, 2 * LANES :] = vals
    low_half = lax.broadcasted_iota(jnp.int32, (tokens, LANES), 1) < HEAD_DIM
    left, right = [], []
    for k in range(2):
        keep = low_half if k == 0 else jnp.logical_not(low_half)
        score_ref[k] = mm_nt(jnp.where(keep, query, jnp.zeros_like(query)), keys)
        row = vec_ref[pl.ds(pair * 2 + k, 1), :]
        left.append(row[:, 0:1])
        right.append(row[:, 510:511])
        rolled = pltpu.roll(
            jnp.broadcast_to(row, (LANES, 4 * LANES)), 3 * LANES + 1, 1, stride=1, stride_axis=0
        )
        strip_ref[k] = rolled[:, : 3 * LANES]
    for i in range(blocks):
        rows = slice(i * LANES, (i + 1) * LANES)
        same = segcol_ref[rows, 0:1] == segrow_ref[0:1, :]
        for k in range(2):
            bias = []
            for j in range(blocks):
                if j < i - 1:
                    bias.append(jnp.broadcast_to(left[k], (LANES, LANES)))
                elif j > i + 1:
                    bias.append(jnp.broadcast_to(right[k], (LANES, LANES)))
                else:
                    at = (j - i + 1) * LANES
                    bias.append(strip_ref[k, :, at : at + LANES])
            scores = score_ref[k, rows, :] + jnp.concatenate(bias, axis=1)
            scores = jnp.where(same, scores, -1000000000.0)
            top = jnp.max(scores, axis=-1, keepdims=True)
            weights = jnp.exp(scores - top)
            total = jnp.sum(weights, axis=-1, keepdims=True)
            probs_ref[k, rows, :] = (weights * (1.0 / total)).astype(bf16)
    mixed = [mm(probs_ref[k], vals) for k in range(2)]
    mixed_ref[:, pl.ds(pl.multiple_of(pair * LANES, LANES), LANES)] = jnp.where(
        low_half, mixed[0], mixed[1]
    ).astype(bf16)


def after_kernel(
    experts, mixed_ref, perm_get, own_ref, oth_ref, x_get, dm_get,
    after_out, low_out, send_out, gain_out, mixed_out,
    stage,
):
    half = own_ref.shape[0]
    width = mixed_ref.shape[1]
    perm = perm_get()[...]
    mixed = mm(mixed_ref[...], perm).astype(bf16)
    mixed_out.ref[...] = mixed
    mixed_out.send()
    block = width + (experts // LANES) * LANES
    lanes = jnp.transpose(
        jnp.concatenate(
            [own_ref[:, block : block + LANES].astype(f32), oth_ref[:, block : block + LANES].astype(f32)],
            axis=0,
        )
    )
    at = experts % LANES
    gain = mm_nt(jnp.broadcast_to(lanes[at : at + 1, :], (8, width)).astype(bf16), perm)
    gain_out.ref[...] = gain
    gain_out.send()
    after = x_get()[...].astype(f32) + (
        mm(mixed[:, :half], own_ref[:, :width]) + mm(mixed[:, half:], oth_ref[:, :width])
    )
    after_out.ref[...] = after
    after_out.send()
    low = (after * inverse_rms(after) * gain[0:1, :]).astype(bf16)
    low_out.ref[...] = low
    low_out.send()
    to_slab(mm(dm_get()[...], low), stage, send_out.ref)


def between_kernel(
    mixed_get, normed_get, own_ref, oth_ref, perm_get, qkv_get,
    mixed_t_out, normed_t_out, wo_out, router_out, query_t_out,
):
    mixed_t_out.ref[...] = jnp.transpose(mixed_get()[...].astype(f32)).astype(bf16)
    mixed_t_out.send()
    normed_t_out.ref[...] = jnp.transpose(normed_get()[...].astype(f32)).astype(bf16)
    normed_t_out.send()
    half = own_ref.shape[0]
    perm = perm_get()[...]
    rest = (mm(perm[:, :half], own_ref[...]) + mm(perm[:, half:], oth_ref[...])).astype(bf16)
    width = wo_out.ref.shape[1]
    wo_out.ref[...] = rest[:, :width]
    router_out.ref[...] = rest[:, width:]
    wo_out.send()
    qkv_ref = qkv_get()
    for c in range(PAIRS):
        query = qkv_ref[:, c * BLOCK : c * BLOCK + LANES].astype(f32)
        query_t_out.ref[c * LANES : (c + 1) * LANES, :] = jnp.transpose(query).astype(bf16)


def early_expert_kernel(recv_ref, win_ref, wout_ref, cot_ref, win_low_ref, wout_low_ref, g_ref, stage):
    slots = cot_ref.shape[0]

    @pl.when(pl.program_id(0) == 0)
    def _():
        def put(c, values):
            cot_ref[:, c * LANES : (c + 1) * LANES] = values.astype(bf16)

        from_slab(recv_ref, stage, slots, put)

    win_low_ref[...] = win_ref[0].astype(bf16)
    wout = wout_ref[0].astype(bf16)
    wout_low_ref[...] = wout
    g_ref[...] = mm_nt(cot_ref[...], wout).astype(bf16)


def activate(pre):
    squared = pre * pre
    bent = jnp.tanh(pre * (gelu_coef + (gelu_coef * cubic_coef) * squared))
    rise = 0.5 + 0.5 * bent
    value = pre * rise
    slope = rise + (value - value * rise) * (
        2.0 * gelu_coef + (6.0 * gelu_coef * cubic_coef) * squared
    )
    return value, slope


def expert_kernel(
    experts, steps,
    me_ref, recv_ref, router_hbm, cot_hbm, win_hbm, wout_hbm, g_hbm,
    back_hbm, made_hbm, x_hbm, rows_hbm, glog_hbm, gate_hbm,
    stage, router_ref, cot_ref, win_ref, wout_ref, g_ref, hidden_ref, act_ref,
    back_ref, made_ref, x_ref, rows_ref, glog_ref, gate_ref, in_sems, out_sems,
):
    slots, width = x_ref.shape
    units = win_ref.shape[1] // steps
    parts = [slice(i * units, (i + 1) * units) for i in range(steps)]
    fetch = [(router_hbm, router_ref), (cot_hbm, cot_ref)]
    fetch += [(win_hbm.at[:, p], win_ref.at[:, p]) for p in parts]
    fetch += [(g_hbm.at[:, p], g_ref.at[:, p]) for p in parts]
    fetch += [(wout_hbm.at[p, :], wout_ref.at[p, :]) for p in parts]
    copies = [pltpu.make_async_copy(a, b, in_sems.at[i]) for i, (a, b) in enumerate(fetch)]
    stores = [
        pltpu.make_async_copy(a, b, out_sems.at[i])
        for i, (a, b) in enumerate(
            (
                (back_ref, back_hbm), (made_ref, made_hbm), (x_ref, x_hbm),
                (rows_ref, rows_hbm), (glog_ref, glog_hbm), (gate_ref, gate_hbm),
            )
        )
    ]
    sequence = [0, 2, 2 + steps, 3, 3 + steps]
    for i in sequence:
        copies[i].start()

    def put(c, values):
        x_ref[:, c * LANES : (c + 1) * LANES] = values.astype(bf16)

    from_slab(recv_ref, stage, slots, put)
    stores[2].start()
    copies[0].wait()
    router = router_ref[...]
    wide = router.shape[1]
    logits = mm(x_ref[...], router)
    for step, part in enumerate(parts):
        if step + 2 < steps:
            copies[4 + step].start()
            copies[4 + step + steps].start()
        else:
            for i in range(steps // 2):
                copies[2 + 2 * steps + (step + 2 - steps) * (steps // 2) + i].start()
        if step == steps - 1:
            copies[1].start()
        copies[2 + step].wait()
        copies[2 + step + steps].wait()
        value, slope = activate(mm(x_ref[...], win_ref[:, part]))
        hidden_ref[:, part] = value.astype(bf16)
        act_ref[:, part] = (g_ref[:, part].astype(f32) * slope).astype(bf16)
    for step in range(steps):
        copies[2 + 2 * steps + step].wait()
    produced = mm(hidden_ref[...], wout_ref[...]).astype(bf16)
    made_ref[...] = produced
    stores[1].start()
    lane = lax.broadcasted_iota(jnp.int32, (slots, wide), 1)
    logits = jnp.where(lane < experts, logits, -jnp.inf)
    weights = jnp.exp(logits - jnp.max(logits, axis=-1, keepdims=True))
    probs = weights / jnp.sum(weights, axis=-1, keepdims=True)
    own = (lane == me_ref[0]).astype(f32)
    gate = jnp.sum(probs * own, axis=-1, keepdims=True)
    gate_ref[...] = jnp.broadcast_to(gate, (slots, LANES))
    stores[5].start()
    copies[1].wait()
    cot = cot_ref[...].astype(f32)
    rows_ref[...] = (gate * cot).astype(bf16)
    stores[3].start()
    grad_gate = jnp.sum(cot * produced.astype(f32), axis=-1, keepdims=True)
    grad_logits = (probs * (own - gate) * grad_gate).astype(bf16)
    glog_ref[...] = grad_logits
    stores[4].start()
    back = (gate * mm_nt(act_ref[...], win_ref[...])).astype(bf16).astype(f32)
    to_slab(back + mm_nt(grad_logits, router), stage, back_ref)
    stores[0].start()
    for copy in stores:
        copy.wait()


def expert_weights_kernel(
    x_ref, rows_ref, glog_ref, gate_ref, made_ref, perm_ref, win_ref, g_ref,
    gin_ref, gout_ref, grouter_ref, prod_ref,
    xt, stage,
):
    @pl.when(pl.program_id(0) == 0)
    def _():
        to_slab(made_ref[...].astype(f32), stage, prod_ref)
        x = x_ref[...]
        xt[...] = jnp.transpose(gate_ref[:, 0:1] * x.astype(f32)).astype(bf16)
        moved = mm(x, perm_ref[...]).astype(bf16)
        grouter_ref[...] = mm_tn(moved, glog_ref[...])

    value, slope = activate(mm(x_ref[...], win_ref[...]))
    act = (g_ref[...].astype(f32) * slope).astype(bf16)
    gout_ref[0] = mm_tn(value.astype(bf16), rows_ref[...])
    gin_ref[0] = mm(xt[...], act)


def output_kernel(experts, recv_ref, dt_get, low_get, router_get, routes_get, after_get, out_out, stage, rows):
    def put(c, values):
        rows[:, c * LANES : (c + 1) * LANES] = values.astype(bf16)

    dt = dt_get()[...]
    from_slab(recv_ref, stage, dt.shape[1], put)
    produced = mm(dt, rows[...])
    logits = mm(low_get()[...], router_get()[...])
    lane = lax.broadcasted_iota(jnp.int32, logits.shape, 1)
    logits = jnp.where(lane < experts, logits, -jnp.inf)
    weights = jnp.exp(logits - jnp.max(logits, axis=-1, keepdims=True))
    own = (lane == routes_get()[...]).astype(f32)
    gate = jnp.sum(weights * own, axis=-1, keepdims=True) / jnp.sum(weights, axis=-1, keepdims=True)
    out_out.ref[...] = (after_get()[...] + gate * produced).astype(bf16)


def norm_two_kernel(
    experts,
    recv_ref, dt_get, after_get, gain_get, cot_get, wo_get, mixed_t_get, perm_get, grouter_get,
    grad_after_out, grad_mixed_ref, keep_ref, send_ref,
    stage, rows,
):
    def put(c, values):
        rows[:, c * LANES : (c + 1) * LANES] = values.astype(bf16)

    slots = recv_ref.shape[0] * LANES // grad_mixed_ref.shape[1]
    from_slab(recv_ref, stage, slots, put)
    grad = mm(dt_get()[...], rows[...])
    after = after_get()[...]
    inverse = inverse_rms(after)
    unit = after * inverse
    scaled = grad * gain_get()[0:1, :]
    back = inverse * (scaled - unit * jnp.mean(scaled * unit, axis=-1, keepdims=True))
    grad_after = cot_get()[...].astype(f32) + back
    grad_after_out.ref[...] = grad_after
    grad_after_out.send()
    low = grad_after.astype(bf16)
    grad_mixed_ref[...] = mm_nt(low, wo_get()[...]).astype(bf16)
    half = keep_ref.shape[0]
    width = low.shape[1]
    mixed_t_ref = mixed_t_get()
    keep_ref[:, :width] = mm(mixed_t_ref[:half, :], low)
    send_ref[:, :width] = mm(mixed_t_ref[half:, :], low).astype(bf16)
    gain_row = jnp.sum(grad * unit, axis=0, keepdims=True)
    high, rest = split_two(jnp.broadcast_to(gain_row, (8, width)))
    perm = perm_get()[...]
    gain_row = (mm(high, perm) + mm(rest, perm))[0:1, :]
    grouter = grouter_get()[...]
    lane = lax.broadcasted_iota(jnp.int32, grouter.shape, 1)
    packed = jnp.where(
        lane < experts, grouter, jnp.where(lane == experts, to_column(gain_row, grouter.shape[1]), 0.0)
    )
    keep_ref[:, width:] = packed[:half]
    send_ref[:, width:] = packed[half:].astype(bf16)


def unskew(skewed):
    span = 4 * LANES
    total = None
    for g in range(LANES // 8):
        moved = pltpu.roll(skewed[8 * g : 8 * g + 8, :], (LANES - 1 - 8 * g) % span, 1)
        total = moved if total is None else total + moved
    turned = jnp.concatenate([total[7 - s : 8 - s, :] for s in range(8)], axis=0)
    turned = pltpu.roll(turned, span - 7, 1, stride=1, stride_axis=0)
    return jnp.sum(turned, axis=0, keepdims=True)


def attend_backward_kernel(
    before, last, qkv_ref, query_t_ref, probs_ref, gm_ref, normed_t_ref, *refs
):
    refs = list(refs)
    vec_in = refs.pop(0) if before else None
    if last:
        hmask_ref, umask_ref = refs.pop(0), refs.pop(0)
    keep_ref, send_ref, dvec_ref, dq_ref, dkv_ref, dp_ref, ds_ref = refs
    pairs_before = 0 if vec_in is None else vec_in.shape[0] // 2
    pair = pl.program_id(0)
    tokens = qkv_ref.shape[0]
    blocks = tokens // LANES
    low_half = lax.broadcasted_iota(jnp.int32, (tokens, LANES), 1) < HEAD_DIM
    lane = lax.broadcasted_iota(jnp.int32, (1, 4 * LANES), 1)
    keys, vals = (qkv_ref[:, k * LANES : (k + 1) * LANES] for k in (1, 2))
    grad = gm_ref[:, pl.ds(pl.multiple_of((pair + pairs_before) * LANES, LANES), LANES)]
    grad_t = jnp.transpose(grad.astype(f32)).astype(bf16)
    dq = []
    for k in range(2):
        keep = low_half if k == 0 else jnp.logical_not(low_half)
        dp_ref[k] = mm_nt(jnp.where(keep, grad, jnp.zeros_like(grad)), vals)
    for k in range(2):
        strip = [None] * 3
        far_left = far_right = None
        for i in range(blocks):
            rows = slice(i * LANES, (i + 1) * LANES)
            dp = dp_ref[k, rows, :]
            probs = probs_ref[k, rows, :].astype(f32)
            delta = jnp.sum(probs * dp, axis=-1, keepdims=True)
            ds = (probs * (dp - delta)).astype(bf16)
            ds_ref[k, rows, :] = ds
            wide = ds.astype(f32)
            for j in range(blocks):
                piece = wide[:, j * LANES : (j + 1) * LANES]
                if j < i - 1:
                    far_left = piece if far_left is None else far_left + piece
                elif j > i + 1:
                    far_right = piece if far_right is None else far_right + piece
                else:
                    at = j - i + 1
                    strip[at] = piece if strip[at] is None else strip[at] + piece
        part = slice(k * HEAD_DIM, (k + 1) * HEAD_DIM)
        dq.append(mm(ds_ref[k], keys))
        dkv_ref[part, :] = mm(query_t_ref[part, :], ds_ref[k]).astype(bf16)
        low_part = slice(LANES + k * HEAD_DIM, LANES + (k + 1) * HEAD_DIM)
        dkv_ref[low_part, :] = mm(grad_t[part, :], probs_ref[k]).astype(bf16)
        vec = unskew(jnp.concatenate(strip + [jnp.zeros((LANES, LANES), f32)], axis=1))
        left = jnp.sum(jnp.sum(far_left, axis=0, keepdims=True), axis=1, keepdims=True)
        right = jnp.sum(jnp.sum(far_right, axis=0, keepdims=True), axis=1, keepdims=True)
        vec = vec + jnp.where(lane == 0, left, 0.0) + jnp.where(lane == 510, right, 0.0)
        dvec_ref[pl.ds((pair + pairs_before) * 2 + k, 1), :] = vec
    dq_ref[...] = (jnp.where(low_half, dq[0], dq[1]) * HEAD_DIM ** (-0.5)).astype(bf16)
    half = keep_ref.shape[0]
    start = pl.multiple_of(pair * BLOCK, LANES)
    queries, rest = pl.ds(start, LANES), pl.ds(start + LANES, 2 * LANES)
    send_ref[:, queries] = mm(normed_t_ref[half:, :], dq_ref[...]).astype(bf16)
    send_ref[:, rest] = mm_nt(normed_t_ref[half:, :], dkv_ref[...]).astype(bf16)
    keep_ref[:, queries] = mm(normed_t_ref[:half, :], dq_ref[...])
    keep_ref[:, rest] = mm_nt(normed_t_ref[:half, :], dkv_ref[...])

    if vec_in is not None:

        @pl.when(pair == 0)
        def _():
            dvec_ref[: 2 * pairs_before, :] = vec_in[...]

    if not last:
        return

    @pl.when(pair == pl.num_programs(0) - 1)
    def _():
        table_col = table_column(
            jnp.concatenate([dvec_ref[...], jnp.zeros((16 - HEADS, 4 * LANES), f32)], axis=0),
            hmask_ref,
            umask_ref,
        )
        lane = lax.broadcasted_iota(jnp.int32, (2 * half, LANES), 1)
        packed = jnp.where(lane == 0, table_col, 0.0)
        end = keep_ref.shape[1] - LANES
        keep_ref[:, end:] = packed[:half]
        send_ref[:, end:] = packed[half:].astype(bf16)


def split_three(values):
    one, rest = split_two(values)
    two, three = split_two(values - one.astype(f32))
    return one, two, three


def table_column(vec, hmask_ref, umask_ref):
    offset = lax.broadcasted_iota(jnp.int32, (LANES, 4 * LANES), 1) - 255
    onehot = (
        lax.broadcasted_iota(jnp.int32, (LANES, 4 * LANES), 0) == buckets_of(offset)
    ).astype(f32).astype(bf16)
    one, two, three = split_three(vec)
    table = mm_nt(one, onehot) + (mm_nt(two, onehot) + mm_nt(three, onehot))
    heads = hmask_ref[:, :16]
    one, two, three = split_three(table)
    spread = mm(heads, one) + (mm(heads, two) + mm(heads, three))
    return jnp.sum(spread * umask_ref[...].astype(f32), axis=1, keepdims=True)


def last_kernel(own_get, oth_get, xperm_get, gain_get, perm_get, after_get, *refs):
    *gets, out_out, grads_ref = refs
    runs = len(gets) // 2
    at = 0
    for dq_get, dkv_get in zip(gets[:runs], gets[runs:]):
        dq, dkv_t = dq_get()[...], dkv_get()
        for c in range(dq.shape[1] // LANES):
            grads_ref[:, at : at + LANES] = dq[:, c * LANES : (c + 1) * LANES]
            moved = jnp.transpose(dkv_t[2 * c * LANES : 2 * (c + 1) * LANES, :].astype(f32))
            grads_ref[:, at + LANES : at + BLOCK] = moved.astype(bf16)
            at += BLOCK
    grads = grads_ref[...]
    cols = slice(0, at)
    grad = jnp.concatenate(
        [mm_nt(grads, own_get()[:, cols]), mm_nt(grads, oth_get()[:, cols])], axis=1
    )
    x = xperm_get()[...].astype(f32)
    inverse = inverse_rms(x)
    unit = x * inverse
    scaled = grad * gain_get()[0:1, :]
    back = inverse * (scaled - unit * jnp.mean(scaled * unit, axis=-1, keepdims=True))
    high, rest = split_two(back)
    perm = perm_get()[...]
    out_out.ref[...] = (after_get()[...] + (mm_nt(high, perm) + mm_nt(rest, perm))).astype(bf16)


def fold_kernel(plan, *refs):
    refs = list(refs)
    total_in = sum(1 + n for members, _ in plan for n in members)
    ins, outs = refs[:total_in], refs[total_in:]
    for members, parts in plan:
        outs_here = [outs.pop(0) for _ in range(parts)]
        at = 0
        for arrived in members:
            total = ins.pop(0)[...]
            for _ in range(arrived):
                total = total + ins.pop(0)[...].astype(f32)
            rows = total.shape[0] // parts
            cols = slice(at, at + total.shape[1])
            at += total.shape[1]
            for m, out in enumerate(outs_here):
                out[:, cols] = total[m * rows : (m + 1) * rows].astype(out.dtype)


def summed(first_ref, moved):
    total = first_ref[...]
    for piece in moved:
        total = total + piece[...].astype(f32)
    return total


def as_row(column):
    size = column.shape[0]
    same = lax.broadcasted_iota(jnp.int32, (size, size), 0) == lax.broadcasted_iota(
        jnp.int32, (size, size), 1
    )
    return jnp.sum(jnp.where(same, column, 0.0), axis=0, keepdims=True)


def finish_kernel(moved_group, gain_get, wq_get, wk_get, wv_get, first_group, first_last, *refs):
    *moved, wo_out, router_out, gain_two_out, wq_out, wk_out, wv_out, gain_out, table_out = refs
    total = summed(first_group, moved[:moved_group])
    width, experts = wo_out.ref.shape[1], router_out.ref.shape[1]
    wo_out.ref[...] = total[:, :width]
    wo_out.send()
    router_out.ref[...] = total[:, width : width + experts]
    gain_two_out.ref[...] = as_row(total[:, width + experts : width + experts + 1])
    early = RUNS[1]
    sources = [(total, total.shape[1] - early * BLOCK)]
    total = summed(first_last, moved[moved_group:])
    sources.append((total, -early * BLOCK))
    for c in range(PAIRS):
        source, base = sources[c >= early]
        for k, out in enumerate((wq_out, wk_out, wv_out)):
            at = base + c * BLOCK + k * LANES
            out.ref[:, c * LANES : (c + 1) * LANES] = source[:, at : at + LANES]
    for out in (wq_out, wk_out, wv_out):
        out.send()
    products = None
    for get, out in ((wq_get, wq_out), (wk_get, wk_out), (wv_get, wv_out)):
        part = get()[...].astype(bf16).astype(f32) * out.ref[...]
        products = part if products is None else products + part
    gain = gain_get()[...].astype(bf16).astype(f32)
    gain_out.ref[...] = as_row(jnp.sum(products, axis=1, keepdims=True)) / gain
    at = total.shape[1] - LANES
    entries = table_out.ref.shape[1]
    table_out.ref[...] = as_row(total[:, at : at + 1])[:, :entries]


def join_kernel(*refs):
    *pieces, out_ref, sems = refs
    rows = pieces[0].shape[0]
    copies = [
        pltpu.make_async_copy(p, out_ref.at[pl.ds(i * rows, rows), :], sems.at[i])
        for i, p in enumerate(pieces)
    ]
    for copy in copies:
        copy.start()
    for copy in copies:
        copy.wait()


def join(values, moved, space):
    pieces = [values, *moved]
    if values.shape[0] % 8:
        return jnp.concatenate(pieces, axis=0)
    shape = (len(pieces) * values.shape[0], values.shape[1])
    any_ref = pl.BlockSpec(memory_space=pl.ANY)
    return pl.pallas_call(
        join_kernel,
        out_shape=space(shape, values.dtype),
        in_specs=[any_ref] * len(pieces),
        out_specs=any_ref,
        scratch_shapes=[pltpu.SemaphoreType.DMA((len(pieces),))],
        **parameters(4, 1),
    )(*pieces)


def expert_call(experts, steps, slots, width, units, wide):
    slab = (slots * width // LANES, LANES)
    any_ref, vmem_ref = (pl.BlockSpec(memory_space=m) for m in (pl.ANY, pltpu.VMEM))
    outs = [slab, (slots, width), (slots, width), (slots, width), (slots, wide)]
    call = pl.pallas_call(
        functools.partial(expert_kernel, experts, steps),
        out_shape=[far(shape, bf16) for shape in outs] + [far((slots, LANES), f32)],
        in_specs=[pl.BlockSpec(memory_space=pltpu.SMEM), vmem_ref] + [any_ref] * 5,
        out_specs=[any_ref] * 6,
        scratch_shapes=[pltpu.VMEM(slab, f32)]
        + [
            pltpu.VMEM(shape, bf16)
            for shape in (
                (width, wide), (slots, width), (width, units), (units, width),
                (slots, units), (slots, units), (slots, units),
            )
        ]
        + [pltpu.VMEM(shape, bf16) for shape in outs]
        + [
            pltpu.VMEM((slots, LANES), f32),
            pltpu.SemaphoreType.DMA((2 + 3 * steps,)),
            pltpu.SemaphoreType.DMA((6,)),
        ],
        **parameters(52, 18),
    )
    return lambda me, recv, *rest: call(me, recv, *[place(Far(a)) for a in rest])


def shards(
    count,
    inputs,
    segment_ids,
    routes,
    cotangent,
    gain_attn,
    gain_ffn,
    bias_table,
    w_query,
    w_key,
    w_value,
    w_output,
    w_router,
    w_in,
    w_out,
):
    tokens, width = inputs.shape
    experts = w_router.shape[1]
    rows_local = w_query.shape[0]
    entries = bias_table.shape[0]
    hidden_units = w_in.shape[2]
    capacity = max(2, 5 * tokens // (4 * experts))
    slots = experts * capacity
    blocks = width // LANES
    half = width // 2
    wide = -(-(experts + 1) // LANES) * LANES
    me = lax.axis_index("seq").astype(jnp.int32).reshape(1)
    vmem = pl.BlockSpec(memory_space=pltpu.VMEM)

    groups = bit_groups(count)
    levels = list(reversed(groups[1:]))
    columns = PAIRS * BLOCK
    piece, tail = flat_call(
        functools.partial(pack_kernel, experts),
        [near((rows_local, columns + LANES), bf16), near((rows_local, width + wide), bf16)],
        us=1,
    )(
        *map(Far, (gain_attn[None, :], gain_ffn[None, :], bias_table[None, :])),
        *map(Far, (w_query, w_key, w_value, w_output, w_router)),
    )

    def reach(values, low_bit, bits):
        return [swap(values, m << low_bit, count) for m in range(1, 1 << bits)]

    order = np.asarray(relative_order(count), np.int32)
    rel_row = jnp.asarray(np.repeat(order, rows_local)[None, :])
    off_row = jnp.asarray(np.tile(np.arange(rows_local, dtype=np.int32), count)[None, :])
    slab = (slots * blocks, LANES)
    slab_stage = pltpu.VMEM(slab, f32)
    perm, xperm, segrow, segcol, hmask, umask, dt, dm = flat_call(
        functools.partial(prepare_kernel, rows_local, entries, experts, capacity),
        [
            far((width, width), bf16),
            far((tokens, width), bf16),
            far((8, tokens), f32),
            far((tokens, LANES), f32),
            far((width, LANES), bf16),
            far((width, LANES), bf16),
            far((tokens, slots), bf16),
            far((slots, tokens), bf16),
        ],
        us=8,
    )(me, Far(rel_row), Far(off_row), Far(inputs), Far(segment_ids), Far(routes))
    cot_send = flat_call(dispatch_kernel, [far(slab, bf16)], us=3, scratch=[slab_stage])(
        Far(dm), Far(cotangent)
    )[0]

    moved = reach(piece, *levels[0])
    beside = [perm]
    for k, level in enumerate(levels[1:]):
        moved = lax.optimization_barrier((*moved, *beside))[: len(moved)]
        piece = join(piece, moved, near)
        moved = reach(piece, *level)
        beside = [cot_send]
        tail_moved = reach(after(tail, piece, cot_send), *levels[k])
        moved = lax.optimization_barrier((*moved, *tail_moved))[: len(moved)]
        tail = join(tail, tail_moved, near)
    piece = join(piece, moved, far)
    other = swap(piece, 1, count)
    tail_moved = reach(after(tail, piece), *levels[-1])

    slab_split = (count, slots * blocks // count, LANES)

    def exchange(rows):
        return lax.all_to_all(
            rows.reshape(slab_split), "seq", split_axis=0, concat_axis=0, tiled=True
        ).reshape(slab)

    cot_recv = exchange(after(cot_send, tail))

    def whole(shape):
        return pl.BlockSpec(shape, lambda i: (0,) * len(shape))

    pair_probs = pl.BlockSpec((2, tokens, tokens), lambda i: (i, 0, 0))
    piece, other = Far(piece), Far(other)
    small_block = pl.BlockSpec((half, LANES), lambda i: (0, columns // LANES))
    pair_weights = pl.BlockSpec((half, BLOCK), lambda i: (0, i))
    qkv, probs, mixed, normed, gain_one = grid_call(
        attend_forward_kernel,
        [
            far((tokens, PAIRS * BLOCK), bf16),
            far((HEADS, tokens, tokens), bf16),
            near((tokens, width), bf16),
            far((tokens, width), bf16),
            far((8, width), f32),
        ],
        grid=(PAIRS,),
        in_specs=[whole((tokens, width))]
        + [pair_weights, pair_weights, small_block, small_block]
        + [whole(shape) for shape in ((width, LANES), (width, LANES), (8, tokens), (tokens, LANES))],
        out_specs=[
            pl.BlockSpec((tokens, BLOCK), lambda i: (0, i)),
            pair_probs,
            vmem,
            whole((tokens, width)),
            whole((8, width)),
        ],
        scratch=[
            pltpu.VMEM((16, 4 * LANES), f32),
            pltpu.VMEM((2, tokens, tokens), f32),
            pltpu.VMEM((2, LANES, 3 * LANES), f32),
        ],
        us=14,
    )(
        Far(after(xperm, tail)), piece, other, piece, other,
        *map(Far, (hmask, umask, segrow, segcol)),
    )
    tail_moved = lax.optimization_barrier((*tail_moved, mixed))[:-1]
    tail = join(tail, tail_moved, near)
    tail_other = swap(tail, 1, count)

    after_rows, low_two, row_send, gain_two, mixed_perm = flat_call(
        functools.partial(after_kernel, experts),
        [
            far((tokens, width), f32),
            far((tokens, width), bf16),
            far(slab, bf16),
            far((8, width), f32),
            far((tokens, width), bf16),
        ],
        us=6,
        scratch=[slab_stage],
    )(mixed, Far(perm), tail, tail_other, Far(inputs), Far(dm))
    row_recv = exchange(row_send)

    steps = 6
    units = hidden_units // steps
    weight_in = pl.BlockSpec((1, width, units), lambda i: (0, 0, i))
    weight_out = pl.BlockSpec((1, units, width), lambda i: (0, i, 0))

    low_in = pl.BlockSpec((width, units), lambda i: (0, i))
    low_out = pl.BlockSpec((units, width), lambda i: (i, 0))
    slot_units = pl.BlockSpec((slots, units), lambda i: (0, i))
    cot_rows, win_low, wout_low, grad_hidden = grid_call(
        early_expert_kernel,
        [
            far((slots, width), bf16),
            far((width, hidden_units), bf16),
            far((hidden_units, width), bf16),
            far((slots, hidden_units), bf16),
        ],
        grid=(steps,),
        in_specs=[whole(slab), weight_in, weight_out],
        out_specs=[whole((slots, width)), low_in, low_out, slot_units],
        us=13,
        scratch=[slab_stage],
    )(cot_recv, Far(w_in), Far(w_out))
    mixed_t, normed_t, output_w, router_w, query_t = flat_call(
        between_kernel,
        [
            far((width, tokens), bf16),
            far((width, tokens), bf16),
            far((width, width), bf16),
            far((width, wide), bf16),
            far((width, tokens), bf16),
        ],
        us=7,
    )(Far(mixed_perm), Far(normed), tail, tail_other, Far(perm), Far(qkv))
    back_send, made, x_rows, grad_rows, grad_logits, gates = expert_call(
        experts, steps, slots, width, hidden_units, wide
    )(me, row_recv, router_w, cot_rows, win_low, wout_low, grad_hidden)
    back_recv = exchange(back_send)
    grad_inner, grad_outer, grad_router, prod_send = grid_call(
        expert_weights_kernel,
        [
            far((1, width, hidden_units), f32),
            far((1, hidden_units, width), f32),
            far((width, wide), f32),
            far(slab, bf16),
        ],
        grid=(steps,),
        in_specs=[
            whole((slots, width)),
            whole((slots, width)),
            whole((slots, wide)),
            whole((slots, LANES)),
            whole((slots, width)),
            whole((width, width)),
            low_in,
            slot_units,
        ],
        out_specs=[weight_in, weight_out, whole((width, wide)), whole(slab)],
        us=19,
        scratch=[pltpu.VMEM((width, slots), bf16), slab_stage],
    )(*map(Far, (x_rows, grad_rows, grad_logits, gates, made, perm, win_low, grad_hidden)))
    prod_recv = exchange(prod_send)

    row_scratch = pltpu.VMEM((slots, width), bf16)
    grad_after, grad_mixed, keep_o, send_o = flat_call(
        functools.partial(norm_two_kernel, experts),
        [
            far((tokens, width), f32),
            near((tokens, width), bf16),
            near((half, width + wide), f32),
            near((half, width + wide), bf16),
        ],
        us=1,
        scratch=[slab_stage, row_scratch],
    )(
        back_recv,
        *map(Far, (dt, after_rows, gain_two, cotangent, output_w, mixed_t, perm, grad_router)),
    )

    def backward(run, ready):
        start, stop = RUNS[run], RUNS[run + 1]
        last = stop == PAIRS
        vec = before.get("vec")
        here = [Far(qkv), Far(query_t), Far(probs), after(grad_mixed, *ready), Far(normed_t)]
        specs = [
            pl.BlockSpec((tokens, BLOCK), lambda i: (0, i + start)),
            pl.BlockSpec((LANES, tokens), lambda i: (i + start, 0)),
            pl.BlockSpec((2, tokens, tokens), lambda i: (i + start, 0, 0)),
            vmem,
            whole((width, tokens)),
        ]
        if vec is not None:
            here.append(vec)
            specs.append(vmem)
        if last:
            here += [Far(hmask), Far(umask)]
            specs += [whole((width, LANES))] * 2
        pairs = stop - start
        cols = pairs * BLOCK + (LANES if last else 0)
        keep, send, vec, dq, dkv_t = grid_call(
            functools.partial(attend_backward_kernel, vec is not None, last),
            [
                near((half, cols), f32),
                near((half, cols), bf16),
                near((2 * stop, 4 * LANES), f32),
                far((tokens, pairs * LANES), bf16),
                far((2 * pairs * LANES, tokens), bf16),
            ],
            grid=(pairs,),
            in_specs=specs,
            out_specs=[
                vmem,
                vmem,
                vmem,
                pl.BlockSpec((tokens, LANES), lambda i: (0, i)),
                pl.BlockSpec((2 * LANES, tokens), lambda i: (i, 0)),
            ],
            scratch=[
                pltpu.VMEM((2, tokens, tokens), f32),
                pltpu.VMEM((2, tokens, tokens), bf16),
            ],
            us=(1, 4)[run],
            vmem=24,
        )(*here)
        before.update(vec=vec)
        born.append((keep, send))
        grads.append((dq, dkv_t))
        return keep

    def results(ready):
        return flat_call(
            functools.partial(output_kernel, experts),
            [far((tokens, width), bf16)],
            us=0.001,
            scratch=[slab_stage, row_scratch],
            vmem=20,
        )(after(prod_recv, *ready), *map(Far, (dt, low_two, router_w, routes, after_rows)))[0]

    def finish(ready):
        return flat_call(
            last_kernel,
            [far((tokens, width), bf16)],
            us=8,
            scratch=[pltpu.VMEM((tokens, columns), bf16)],
            vmem=32,
        )(
            piece, other, Far(after(xperm, *ready)),
            *map(Far, (gain_one, perm, grad_after)),
            *[Far(g[0]) for g in grads], *[Far(g[1]) for g in grads],
        )[0]

    before, born, grads = {}, [(keep_o, send_o)], []
    ups = groups[1:]
    core = (1, 2)
    first = (1 << ups[0][0], 1 << ups[0][1])
    direct = [(1 << low_bit, 1 << bits) for low_bit, bits in ups[1:]]
    halving = [(1 << (low_bit + b), 2) for low_bit, bits in ups[1:] for b in reversed(range(bits))]
    plans = {c: {c: core, c + 1: first} for c in range(3)}
    plans[2].update({4 + i: step for i, step in enumerate(direct)})
    plans[3] = {3 + i: step for i, step in enumerate(halving)}
    work = {run: [functools.partial(backward, run)] for run in range(2)}
    work.update({2: [finish], 3: [results]})
    own, going, flight, finished = {}, {}, {}, {}
    output = grad_inputs = None
    end = max(max(plan) for plan in plans.values())
    own[0], going[0] = born[0][0], [born[0][1]]
    for slot in range(end + 1):
        for c, plan in plans.items():
            if slot in plan:
                distance, parts = plan[slot]
                flight[c] = [swap(g, (m + 1) * distance, count) for m, g in enumerate(going[c])]
        ready = [own[c] for c in flight] + ([prod_recv] if slot == 2 else [])
        for step in work.get(slot, []):
            value = step(ready)
            ready = [value]
            if step is results:
                output = value
            if step is finish:
                grad_inputs = value
        if slot in work:
            for c in flight:
                flight[c] = list(lax.optimization_barrier((*flight[c], value))[:-1])
        folds, args, outs, cut = [], [], [], []

        def fold(members, following, name):
            parts = following[1]
            folds.append(([len(flight[c]) if c in flight else 0 for c in members], parts))
            rows = own[members[0]].shape[0] // parts
            cols = sum(own[c].shape[1] for c in members)
            for c in members:
                args.append(own[c])
                args.extend(flight.pop(c, []))
            outs.append(near((rows, cols), f32))
            outs.extend([near((rows, cols), bf16)] * (parts - 1))
            cut.append((name, parts))

        if slot == 2:
            fold([0, 1], plans[3][3], 3)
        for c in list(flight):
            following = plans[c].get(slot + 1)
            if following or c < 2:
                fold([c], following or (0, 1), c)
            else:
                finished[c] = [own[c], *flight.pop(c)]
        if folds:
            folded = list(
                flat_call(functools.partial(fold_kernel, folds), outs, us=1, vmem=16)(*args)
            )
            for c, parts in cut:
                own[c] = folded.pop(0)
                going[c] = [folded.pop(0) for _ in range(parts - 1)]
            if len(born) == slot + 2:
                own[slot + 1] = born[-1][0]
                going[slot + 1] = [after(born[-1][1], own[cut[0][0]])]

    def row(size):
        return far((1, size), f32)

    square = far((rows_local, width), f32)
    grad_wo, grad_wr, grad_gain_two, grad_q, grad_k, grad_v, grad_gain_one, grad_table = flat_call(
        functools.partial(finish_kernel, len(finished[3]) - 1),
        [square, far((rows_local, experts), f32), row(rows_local)]
        + [square, square, square, row(rows_local), row(entries)],
        us=2,
        vmem=16,
    )(
        *map(Far, (gain_attn[None, :], w_query, w_key, w_value)),
        finished[3][0], finished[2][0], *finished[3][1:], *finished[2][1:],
    )

    return (
        output,
        grad_inputs,
        grad_gain_one[0],
        grad_gain_two[0],
        grad_table[0],
        grad_q,
        grad_k,
        grad_v,
        grad_wo,
        grad_wr,
        grad_inner,
        grad_outer,
    )


def solution(mesh):
    row, flat, cube = P("seq", None), P("seq"), P("seq", None, None)
    in_specs = (row,) * 4 + (flat,) * 3 + (row,) * 5 + (cube,) * 2
    out_specs = (row,) * 2 + (flat,) * 3 + (row,) * 5 + (cube,) * 2
    return jax.shard_map(
        functools.partial(shards, mesh.shape["seq"]),
        mesh=mesh,
        in_specs=in_specs,
        out_specs=out_specs,
        check_vma=False,
    )
```

```python
import functools

import jax
import jax.numpy as jnp
import numpy as np
from jax import lax
from jax.experimental import pallas as pl
from jax.experimental.pallas import tpu as pltpu
from jax.sharding import PartitionSpec as P

HEADS = 12
HEAD_DIM = 64
BUCKETS = 32
PAIRS = HEADS // 2
RUNS = (0, 4, 6)
LANES = 128
BLOCK = 3 * LANES

epsilon = 1e-06
bucket_edges = (1, 2, 3, 4, 5, 6, 7, 8, 12, 16, 23, 32, 46, 64, 91)
gelu_coef = 0.7978845608028654
cubic_coef = 0.044715

f32 = jnp.float32
bf16 = jnp.bfloat16


def bit_groups(count):
    bits = count.bit_length() - 1
    groups, low = [(0, 1)], 1
    while low < bits:
        width = min(2, bits - low)
        groups.append((low, width))
        low += width
    return groups


def relative_order(count):
    order = [0]
    for low, width in bit_groups(count):
        order = [base + (m << low) for base in order for m in range(1 << width)]
    return order


def swap(values, distance, count):
    return lax.ppermute(values, "seq", [(i, i ^ distance) for i in range(count)])


def after(values, *others):
    return lax.optimization_barrier((values, *others))[0]


def mm(left, right):
    return jnp.dot(left, right, preferred_element_type=f32)


def mm_nt(left, right):
    return lax.dot_general(left, right, (((1,), (1,)), ((), ())), preferred_element_type=f32)


def mm_tn(left, right):
    return lax.dot_general(left, right, (((0,), (0,)), ((), ())), preferred_element_type=f32)


def split_two(values):
    high = values.astype(bf16)
    return high, (values - high.astype(f32)).astype(bf16)


class Far:
    def __init__(self, values):
        self.values = values


def near(shape, dtype):
    return pltpu.VMEM(shape, dtype)


def far(shape, dtype):
    return pltpu.HBM(shape, dtype)


class Fetched:
    def __init__(self, copy, ref):
        self.copy, self.ref, self.here = copy, ref, False

    def __call__(self):
        if not self.here:
            self.copy.wait()
            self.here = True
        return self.ref


class Stored:
    def __init__(self, copy, ref):
        self.copy, self.ref, self.sent = copy, ref, False

    def send(self):
        self.copy.start()
        self.sent = True


def place(a):
    if isinstance(a, Far):
        return pltpu.with_memory_space_constraint(a.values, pltpu.HBM)
    return a


def parameters(vmem, us):
    return dict(
        compiler_params=pltpu.CompilerParams(vmem_limit_bytes=vmem * 1024 * 1024),
        cost_estimate=pl.CostEstimate(
            flops=int(us * 10**9), bytes_accessed=int(us * 10**6), transcendentals=0
        ),
    )


def grid_call(body, outs, grid, in_specs, out_specs, us, scratch=(), vmem=40):
    call = pl.pallas_call(
        body,
        out_shape=list(outs),
        grid=grid,
        in_specs=in_specs,
        out_specs=out_specs,
        scratch_shapes=list(scratch),
        **parameters(vmem, us),
    )
    return lambda *args: call(*[place(a) for a in args])


def flat_call(body, outs, us, scratch=(), vmem=32):
    def run(*args):
        lazy = [isinstance(a, Far) for a in args]
        late = [o.memory_space == pltpu.HBM for o in outs]
        values = [a.values if f else a for a, f in zip(args, lazy)]
        n_in, n_out, n_scratch = len(args), len(outs), len(scratch)
        any_ref, vmem_ref, smem_ref = (
            pl.BlockSpec(memory_space=m) for m in (pl.ANY, pltpu.VMEM, pltpu.SMEM)
        )
        in_copies = [pltpu.VMEM(v.shape, v.dtype) for v, f in zip(values, lazy) if f]
        out_copies = [pltpu.VMEM(o.shape, o.dtype) for o, f in zip(outs, late) if f]

        def wrapped(*refs):
            ins, rest = refs[:n_in], refs[n_in:]
            results, rest = rest[:n_out], rest[n_out:]
            own, rest = rest[:n_scratch], rest[n_scratch:]
            fetched, rest = list(rest[: len(in_copies)]), rest[len(in_copies) :]
            stored, rest = list(rest[: len(out_copies)]), rest[len(out_copies) :]
            sems = list(rest)
            given, made = [], []
            for ref, f in zip(ins, lazy):
                if f:
                    copy = pltpu.make_async_copy(ref, fetched[0], sems.pop())
                    copy.start()
                    given.append(Fetched(copy, fetched.pop(0)))
                else:
                    given.append(ref)
            for ref, f in zip(results, late):
                if f:
                    made.append(
                        Stored(pltpu.make_async_copy(stored[0], ref, sems.pop()), stored[0])
                    )
                    stored.pop(0)
                else:
                    made.append(ref)
            body(*given, *made, *own)
            for item in given:
                if isinstance(item, Fetched):
                    item()
            for item in made:
                if isinstance(item, Stored):
                    if not item.sent:
                        item.send()
                    item.copy.wait()

        return pl.pallas_call(
            wrapped,
            out_shape=list(outs),
            in_specs=[
                any_ref if f else (smem_ref if v.size == 1 else vmem_ref)
                for v, f in zip(values, lazy)
            ],
            out_specs=[any_ref if f else vmem_ref for f in late],
            scratch_shapes=list(scratch)
            + in_copies
            + out_copies
            + [pltpu.SemaphoreType.DMA] * (len(in_copies) + len(out_copies)),
            **parameters(vmem, us),
        )(*[place(a) for a in args])

    return run


def to_slab(values, stage, out_ref):
    slots, width = values.shape
    blocks = width // LANES
    for c in range(blocks):
        stage[pl.ds(c, slots, stride=blocks), :] = values[:, c * LANES : (c + 1) * LANES]
    out_ref[...] = stage[...].astype(out_ref.dtype)


def from_slab(in_ref, stage, slots, put):
    stage[...] = in_ref[...].astype(f32)
    blocks = in_ref.shape[0] // slots
    for c in range(blocks):
        put(c, stage[pl.ds(c, slots, stride=blocks), :])


def to_column(row, width=LANES):
    return jnp.transpose(jnp.broadcast_to(row, (width, row.shape[1])))


def inverse_rms(values):
    return lax.rsqrt(jnp.mean(values * values, axis=-1, keepdims=True) + epsilon)


def buckets_of(offset):
    magnitude = jnp.abs(offset)
    bucket = jnp.zeros(offset.shape, jnp.int32)
    for edge in bucket_edges:
        bucket = bucket + (magnitude >= edge).astype(jnp.int32)
    return bucket + BUCKETS // 2 * (offset > 0).astype(jnp.int32)


def prepare_kernel(
    rows_local, entries, experts, capacity,
    me_ref, rel_ref, off_ref, x_get, seg_get, routes_get,
    perm_out, xperm_out, segrow_out, segcol_out, hmask_out, umask_out, dt_out, dm_out,
):
    perm_ref, xperm_ref, segrow_ref, segcol_ref, hmask_ref, umask_ref, dt_ref, dm_ref = (
        out.ref
        for out in (perm_out, xperm_out, segrow_out, segcol_out, hmask_out, umask_out, dt_out, dm_out)
    )
    x_ref, seg_ref, routes_ref = x_get(), seg_get(), routes_get()
    tokens, width = x_ref.shape
    slots = dm_ref.shape[0]
    me = me_ref[0]
    device_row = rel_ref()[...] ^ me
    off_row = off_ref()[...]
    true_row = device_row * rows_local + off_row
    perm = (lax.broadcasted_iota(jnp.int32, (width, width), 0) == true_row).astype(f32).astype(bf16)
    perm_ref[...] = perm
    perm_out.send()
    xperm_ref[...] = mm(x_ref[...], perm).astype(bf16)
    segments = seg_ref[...].astype(f32)
    segrow_ref[...] = jnp.broadcast_to(segments, segrow_ref.shape)
    segcol_ref[...] = to_column(segments)
    flat = device_row * entries + off_row
    bucket_row = ((flat.astype(f32) + 0.5) * (1.0 / HEADS)).astype(jnp.int32)
    head_row = jnp.where(off_row < entries, flat - bucket_row * HEADS, -1)
    bucket_col = to_column(bucket_row.astype(f32))
    head_col = to_column(head_row.astype(f32))
    lane = lax.broadcasted_iota(jnp.int32, (width, LANES), 1).astype(f32)
    hmask_ref[...] = (head_col == lane).astype(f32).astype(bf16)
    umask_ref[...] = (bucket_col == lane).astype(f32).astype(bf16)
    routes = routes_ref[...]
    labels = lax.broadcasted_iota(jnp.int32, (tokens, experts), 1)
    picked = (routes == labels).astype(f32)
    earlier = (
        lax.broadcasted_iota(jnp.int32, (tokens, tokens), 1)
        <= lax.broadcasted_iota(jnp.int32, (tokens, tokens), 0)
    ).astype(f32).astype(bf16)
    counts = mm(earlier, picked.astype(bf16))
    position = jnp.sum(counts * picked, axis=1, keepdims=True) - 1.0
    slot_col = jnp.where(
        position < capacity, routes.astype(f32) * capacity + position, -1.0
    )
    slot_lane = lax.broadcasted_iota(jnp.int32, (tokens, slots), 1).astype(f32)
    dt_ref[...] = (slot_col == slot_lane).astype(f32).astype(bf16)
    slot_row = jnp.transpose(jnp.broadcast_to(slot_col, (tokens, LANES)))[0:1, :]
    slot_sub = lax.broadcasted_iota(jnp.int32, (slots, tokens), 0).astype(f32)
    dm_ref[...] = (slot_sub == slot_row).astype(f32).astype(bf16)


def dispatch_kernel(dm_get, cot_get, send_out, stage):
    to_slab(mm(dm_get()[...], cot_get()[...]), stage, send_out.ref)


def pack_kernel(
    experts, gain_get, gain_two_get, table_get, wq_get, wk_get, wv_get, wo_get, router_get,
    piece, tail,
):
    gain_ref, gain_two_ref, table_ref = gain_get(), gain_two_get(), table_get()
    wq_ref, wk_ref, wv_ref, wo_ref, router_ref = (
        get() for get in (wq_get, wk_get, wv_get, wo_get, router_get)
    )
    rows, width = wq_ref.shape

    def column(ref):
        size = ref.shape[1]
        same = lax.broadcasted_iota(jnp.int32, (rows, size), 0) == lax.broadcasted_iota(
            jnp.int32, (rows, size), 1
        )
        return jnp.sum(jnp.where(same, ref[...], 0.0), axis=1, keepdims=True)

    for c in range(PAIRS):
        for k, w in enumerate((wq_ref, wk_ref, wv_ref)):
            at = c * BLOCK + k * LANES
            piece[:, at : at + LANES] = w[:, c * LANES : (c + 1) * LANES].astype(bf16)
    lane = lax.broadcasted_iota(jnp.int32, (rows, LANES), 1)
    small = jnp.where(lane == 0, column(gain_ref), jnp.where(lane == 1, column(table_ref), 0.0))
    piece[:, PAIRS * BLOCK :] = small.astype(bf16)
    tail[:, :width] = wo_ref[...].astype(bf16)
    lane = lax.broadcasted_iota(jnp.int32, (rows, tail.shape[1] - width), 1)
    tail[:, width:] = jnp.where(lane == experts, column(gain_two_ref), 0.0).astype(bf16)
    tail[:, width : width + experts] = router_ref[...].astype(bf16)


def attend_forward_kernel(
    xperm_ref, own_ref, oth_ref, own_small, oth_small, hmask_ref, umask_ref, segrow_ref, segcol_ref,
    qkv_ref, probs_ref, mixed_ref, normed_ref, gain_ref,
    vec_ref, score_ref, strip_ref,
):
    half = own_ref.shape[0]
    tokens = segcol_ref.shape[0]
    blocks = tokens // LANES
    pair = pl.program_id(0)

    @pl.when(pair == 0)
    def _():
        packed = jnp.concatenate([own_small[...].astype(f32), oth_small[...].astype(f32)], axis=0)
        gain = jnp.transpose(packed)[0:1, :]
        gain_ref[...] = jnp.broadcast_to(gain, gain_ref.shape)
        spread = (packed[:, 1:2] * hmask_ref[...].astype(f32)).astype(bf16)
        table = mm_tn(spread, umask_ref[...])[:16]
        offset = lax.broadcasted_iota(jnp.int32, (LANES, 4 * LANES), 1) - 255
        onehot = (
            lax.broadcasted_iota(jnp.int32, (LANES, 4 * LANES), 0) == buckets_of(offset)
        ).astype(f32).astype(bf16)
        vec_ref[...] = mm(table.astype(bf16), onehot)
        x = xperm_ref[...].astype(f32)
        normed_ref[...] = (x * inverse_rms(x) * gain).astype(bf16)

    qkv = mm(normed_ref[:, :half], own_ref[...]) + mm(normed_ref[:, half:], oth_ref[...])
    query = (qkv[:, :LANES].astype(bf16) * HEAD_DIM ** (-0.5)).astype(bf16)
    keys = qkv[:, LANES : 2 * LANES].astype(bf16)
    vals = qkv[:, 2 * LANES :].astype(bf16)
    qkv_ref[:, :LANES] = query
    qkv_ref[:, LANES : 2 * LANES] = keys
    qkv_ref[:, 2 * LANES :] = vals
    low_half = lax.broadcasted_iota(jnp.int32, (tokens, LANES), 1) < HEAD_DIM
    left, right = [], []
    for k in range(2):
        keep = low_half if k == 0 else jnp.logical_not(low_half)
        score_ref[k] = mm_nt(jnp.where(keep, query, jnp.zeros_like(query)), keys)
        row = vec_ref[pl.ds(pair * 2 + k, 1), :]
        left.append(row[:, 0:1])
        right.append(row[:, 510:511])
        rolled = pltpu.roll(
            jnp.broadcast_to(row, (LANES, 4 * LANES)), 3 * LANES + 1, 1, stride=1, stride_axis=0
        )
        strip_ref[k] = rolled[:, : 3 * LANES]
    for i in range(blocks):
        rows = slice(i * LANES, (i + 1) * LANES)
        same = segcol_ref[rows, 0:1] == segrow_ref[0:1, :]
        for k in range(2):
            bias = []
            for j in range(blocks):
                if j < i - 1:
                    bias.append(jnp.broadcast_to(left[k], (LANES, LANES)))
                elif j > i + 1:
                    bias.append(jnp.broadcast_to(right[k], (LANES, LANES)))
                else:
                    at = (j - i + 1) * LANES
                    bias.append(strip_ref[k, :, at : at + LANES])
            scores = score_ref[k, rows, :] + jnp.concatenate(bias, axis=1)
            scores = jnp.where(same, scores, -1000000000.0)
            top = jnp.max(scores, axis=-1, keepdims=True)
            weights = jnp.exp(scores - top)
            total = jnp.sum(weights, axis=-1, keepdims=True)
            probs_ref[k, rows, :] = (weights * (1.0 / total)).astype(bf16)
    mixed = [mm(probs_ref[k], vals) for k in range(2)]
    mixed_ref[:, pl.ds(pl.multiple_of(pair * LANES, LANES), LANES)] = jnp.where(
        low_half, mixed[0], mixed[1]
    ).astype(bf16)


def after_kernel(
    experts, mixed_ref, perm_get, own_ref, oth_ref, x_get, dm_get,
    after_out, low_out, send_out, gain_out, mixed_out,
    stage,
):
    half = own_ref.shape[0]
    width = mixed_ref.shape[1]
    perm = perm_get()[...]
    mixed = mm(mixed_ref[...], perm).astype(bf16)
    mixed_out.ref[...] = mixed
    mixed_out.send()
    block = width + (experts // LANES) * LANES
    lanes = jnp.transpose(
        jnp.concatenate(
            [own_ref[:, block : block + LANES].astype(f32), oth_ref[:, block : block + LANES].astype(f32)],
            axis=0,
        )
    )
    at = experts % LANES
    gain = mm_nt(jnp.broadcast_to(lanes[at : at + 1, :], (8, width)).astype(bf16), perm)
    gain_out.ref[...] = gain
    gain_out.send()
    after = x_get()[...].astype(f32) + (
        mm(mixed[:, :half], own_ref[:, :width]) + mm(mixed[:, half:], oth_ref[:, :width])
    )
    after_out.ref[...] = after
    after_out.send()
    low = (after * inverse_rms(after) * gain[0:1, :]).astype(bf16)
    low_out.ref[...] = low
    low_out.send()
    to_slab(mm(dm_get()[...], low), stage, send_out.ref)


def between_kernel(
    mixed_get, normed_get, own_ref, oth_ref, perm_get, qkv_get,
    mixed_t_out, normed_t_out, wo_out, router_out, query_t_out,
):
    mixed_t_out.ref[...] = jnp.transpose(mixed_get()[...].astype(f32)).astype(bf16)
    mixed_t_out.send()
    normed_t_out.ref[...] = jnp.transpose(normed_get()[...].astype(f32)).astype(bf16)
    normed_t_out.send()
    half = own_ref.shape[0]
    perm = perm_get()[...]
    rest = (mm(perm[:, :half], own_ref[...]) + mm(perm[:, half:], oth_ref[...])).astype(bf16)
    width = wo_out.ref.shape[1]
    wo_out.ref[...] = rest[:, :width]
    router_out.ref[...] = rest[:, width:]
    wo_out.send()
    qkv_ref = qkv_get()
    for c in range(PAIRS):
        query = qkv_ref[:, c * BLOCK : c * BLOCK + LANES].astype(f32)
        query_t_out.ref[c * LANES : (c + 1) * LANES, :] = jnp.transpose(query).astype(bf16)


def early_expert_kernel(recv_ref, win_ref, wout_ref, cot_ref, win_low_ref, wout_low_ref, g_ref, stage):
    slots = cot_ref.shape[0]

    @pl.when(pl.program_id(0) == 0)
    def _():
        def put(c, values):
            cot_ref[:, c * LANES : (c + 1) * LANES] = values.astype(bf16)

        from_slab(recv_ref, stage, slots, put)

    win_low_ref[...] = win_ref[0].astype(bf16)
    wout = wout_ref[0].astype(bf16)
    wout_low_ref[...] = wout
    g_ref[...] = mm_nt(cot_ref[...], wout).astype(bf16)


def activate(pre):
    squared = pre * pre
    bent = jnp.tanh(pre * (gelu_coef + (gelu_coef * cubic_coef) * squared))
    rise = 0.5 + 0.5 * bent
    value = pre * rise
    slope = rise + (value - value * rise) * (
        2.0 * gelu_coef + (6.0 * gelu_coef * cubic_coef) * squared
    )
    return value, slope


def expert_kernel(
    experts, steps,
    me_ref, recv_ref, router_hbm, cot_hbm, win_hbm, wout_hbm, g_hbm,
    back_hbm, made_hbm, x_hbm, rows_hbm, glog_hbm, gate_hbm,
    stage, router_ref, cot_ref, win_ref, wout_ref, g_ref, hidden_ref, act_ref,
    back_ref, made_ref, x_ref, rows_ref, glog_ref, gate_ref, in_sems, out_sems,
):
    slots, width = x_ref.shape
    units = win_ref.shape[1] // steps
    parts = [slice(i * units, (i + 1) * units) for i in range(steps)]
    fetch = [(router_hbm, router_ref), (cot_hbm, cot_ref)]
    fetch += [(win_hbm.at[:, p], win_ref.at[:, p]) for p in parts]
    fetch += [(g_hbm.at[:, p], g_ref.at[:, p]) for p in parts]
    fetch += [(wout_hbm.at[p, :], wout_ref.at[p, :]) for p in parts]
    copies = [pltpu.make_async_copy(a, b, in_sems.at[i]) for i, (a, b) in enumerate(fetch)]
    stores = [
        pltpu.make_async_copy(a, b, out_sems.at[i])
        for i, (a, b) in enumerate(
            (
                (back_ref, back_hbm), (made_ref, made_hbm), (x_ref, x_hbm),
                (rows_ref, rows_hbm), (glog_ref, glog_hbm), (gate_ref, gate_hbm),
            )
        )
    ]
    sequence = [0, 2, 2 + steps, 3, 3 + steps]
    for i in sequence:
        copies[i].start()

    def put(c, values):
        x_ref[:, c * LANES : (c + 1) * LANES] = values.astype(bf16)

    from_slab(recv_ref, stage, slots, put)
    stores[2].start()
    copies[0].wait()
    router = router_ref[...]
    wide = router.shape[1]
    logits = mm(x_ref[...], router)
    for step, part in enumerate(parts):
        if step + 2 < steps:
            copies[4 + step].start()
            copies[4 + step + steps].start()
        else:
            for i in range(steps // 2):
                copies[2 + 2 * steps + (step + 2 - steps) * (steps // 2) + i].start()
        if step == steps - 1:
            copies[1].start()
        copies[2 + step].wait()
        copies[2 + step + steps].wait()
        value, slope = activate(mm(x_ref[...], win_ref[:, part]))
        hidden_ref[:, part] = value.astype(bf16)
        act_ref[:, part] = (g_ref[:, part].astype(f32) * slope).astype(bf16)
    for step in range(steps):
        copies[2 + 2 * steps + step].wait()
    produced = mm(hidden_ref[...], wout_ref[...]).astype(bf16)
    made_ref[...] = produced
    stores[1].start()
    lane = lax.broadcasted_iota(jnp.int32, (slots, wide), 1)
    logits = jnp.where(lane < experts, logits, -jnp.inf)
    weights = jnp.exp(logits - jnp.max(logits, axis=-1, keepdims=True))
    probs = weights / jnp.sum(weights, axis=-1, keepdims=True)
    own = (lane == me_ref[0]).astype(f32)
    gate = jnp.sum(probs * own, axis=-1, keepdims=True)
    gate_ref[...] = jnp.broadcast_to(gate, (slots, LANES))
    stores[5].start()
    copies[1].wait()
    cot = cot_ref[...].astype(f32)
    rows_ref[...] = (gate * cot).astype(bf16)
    stores[3].start()
    grad_gate = jnp.sum(cot * produced.astype(f32), axis=-1, keepdims=True)
    grad_logits = (probs * (own - gate) * grad_gate).astype(bf16)
    glog_ref[...] = grad_logits
    stores[4].start()
    back = (gate * mm_nt(act_ref[...], win_ref[...])).astype(bf16).astype(f32)
    to_slab(back + mm_nt(grad_logits, router), stage, back_ref)
    stores[0].start()
    for copy in stores:
        copy.wait()


def expert_weights_kernel(
    x_ref, rows_ref, glog_ref, gate_ref, made_ref, perm_ref, win_ref, g_ref,
    gin_ref, gout_ref, grouter_ref, prod_ref,
    xt, stage,
):
    @pl.when(pl.program_id(0) == 0)
    def _():
        to_slab(made_ref[...].astype(f32), stage, prod_ref)
        x = x_ref[...]
        xt[...] = jnp.transpose(gate_ref[:, 0:1] * x.astype(f32)).astype(bf16)
        moved = mm(x, perm_ref[...]).astype(bf16)
        grouter_ref[...] = mm_tn(moved, glog_ref[...])

    value, slope = activate(mm(x_ref[...], win_ref[...]))
    act = (g_ref[...].astype(f32) * slope).astype(bf16)
    gout_ref[0] = mm_tn(value.astype(bf16), rows_ref[...])
    gin_ref[0] = mm(xt[...], act)


def output_kernel(experts, recv_ref, dt_get, low_get, router_get, routes_get, after_get, out_out, stage, rows):
    def put(c, values):
        rows[:, c * LANES : (c + 1) * LANES] = values.astype(bf16)

    dt = dt_get()[...]
    from_slab(recv_ref, stage, dt.shape[1], put)
    produced = mm(dt, rows[...])
    logits = mm(low_get()[...], router_get()[...])
    lane = lax.broadcasted_iota(jnp.int32, logits.shape, 1)
    logits = jnp.where(lane < experts, logits, -jnp.inf)
    weights = jnp.exp(logits - jnp.max(logits, axis=-1, keepdims=True))
    own = (lane == routes_get()[...]).astype(f32)
    gate = jnp.sum(weights * own, axis=-1, keepdims=True) / jnp.sum(weights, axis=-1, keepdims=True)
    out_out.ref[...] = (after_get()[...] + gate * produced).astype(bf16)


def norm_two_kernel(
    experts,
    recv_ref, dt_get, after_get, gain_get, cot_get, wo_get, mixed_t_get, perm_get, grouter_get,
    grad_after_out, grad_mixed_ref, keep_ref, send_ref,
    stage, rows,
):
    def put(c, values):
        rows[:, c * LANES : (c + 1) * LANES] = values.astype(bf16)

    slots = recv_ref.shape[0] * LANES // grad_mixed_ref.shape[1]
    from_slab(recv_ref, stage, slots, put)
    grad = mm(dt_get()[...], rows[...])
    after = after_get()[...]
    inverse = inverse_rms(after)
    unit = after * inverse
    scaled = grad * gain_get()[0:1, :]
    back = inverse * (scaled - unit * jnp.mean(scaled * unit, axis=-1, keepdims=True))
    grad_after = cot_get()[...].astype(f32) + back
    grad_after_out.ref[...] = grad_after
    grad_after_out.send()
    low = grad_after.astype(bf16)
    grad_mixed_ref[...] = mm_nt(low, wo_get()[...]).astype(bf16)
    half = keep_ref.shape[0]
    width = low.shape[1]
    mixed_t_ref = mixed_t_get()
    keep_ref[:, :width] = mm(mixed_t_ref[:half, :], low)
    send_ref[:, :width] = mm(mixed_t_ref[half:, :], low).astype(bf16)
    gain_row = jnp.sum(grad * unit, axis=0, keepdims=True)
    high, rest = split_two(jnp.broadcast_to(gain_row, (8, width)))
    perm = perm_get()[...]
    gain_row = (mm(high, perm) + mm(rest, perm))[0:1, :]
    grouter = grouter_get()[...]
    lane = lax.broadcasted_iota(jnp.int32, grouter.shape, 1)
    packed = jnp.where(
        lane < experts, grouter, jnp.where(lane == experts, to_column(gain_row, grouter.shape[1]), 0.0)
    )
    keep_ref[:, width:] = packed[:half]
    send_ref[:, width:] = packed[half:].astype(bf16)


def unskew(skewed):
    span = 4 * LANES
    total = None
    for g in range(LANES // 8):
        moved = pltpu.roll(skewed[8 * g : 8 * g + 8, :], (LANES - 1 - 8 * g) % span, 1)
        total = moved if total is None else total + moved
    turned = jnp.concatenate([total[7 - s : 8 - s, :] for s in range(8)], axis=0)
    turned = pltpu.roll(turned, span - 7, 1, stride=1, stride_axis=0)
    return jnp.sum(turned, axis=0, keepdims=True)


def attend_backward_kernel(
    before, last, qkv_ref, query_t_ref, probs_ref, gm_ref, normed_t_ref, *refs
):
    refs = list(refs)
    vec_in = refs.pop(0) if before else None
    if last:
        hmask_ref, umask_ref = refs.pop(0), refs.pop(0)
    keep_ref, send_ref, dvec_ref, dq_ref, dkv_ref, dp_ref, ds_ref = refs
    pairs_before = 0 if vec_in is None else vec_in.shape[0] // 2
    pair = pl.program_id(0)
    tokens = qkv_ref.shape[0]
    blocks = tokens // LANES
    low_half = lax.broadcasted_iota(jnp.int32, (tokens, LANES), 1) < HEAD_DIM
    lane = lax.broadcasted_iota(jnp.int32, (1, 4 * LANES), 1)
    keys, vals = (qkv_ref[:, k * LANES : (k + 1) * LANES] for k in (1, 2))
    grad = gm_ref[:, pl.ds(pl.multiple_of((pair + pairs_before) * LANES, LANES), LANES)]
    grad_t = jnp.transpose(grad.astype(f32)).astype(bf16)
    dq = []
    for k in range(2):
        keep = low_half if k == 0 else jnp.logical_not(low_half)
        dp_ref[k] = mm_nt(jnp.where(keep, grad, jnp.zeros_like(grad)), vals)
    for k in range(2):
        strip = [None] * 3
        far_left = far_right = None
        for i in range(blocks):
            rows = slice(i * LANES, (i + 1) * LANES)
            dp = dp_ref[k, rows, :]
            probs = probs_ref[k, rows, :].astype(f32)
            delta = jnp.sum(probs * dp, axis=-1, keepdims=True)
            ds = (probs * (dp - delta)).astype(bf16)
            ds_ref[k, rows, :] = ds
            wide = ds.astype(f32)
            for j in range(blocks):
                piece = wide[:, j * LANES : (j + 1) * LANES]
                if j < i - 1:
                    far_left = piece if far_left is None else far_left + piece
                elif j > i + 1:
                    far_right = piece if far_right is None else far_right + piece
                else:
                    at = j - i + 1
                    strip[at] = piece if strip[at] is None else strip[at] + piece
        part = slice(k * HEAD_DIM, (k + 1) * HEAD_DIM)
        dq.append(mm(ds_ref[k], keys))
        dkv_ref[part, :] = mm(query_t_ref[part, :], ds_ref[k]).astype(bf16)
        low_part = slice(LANES + k * HEAD_DIM, LANES + (k + 1) * HEAD_DIM)
        dkv_ref[low_part, :] = mm(grad_t[part, :], probs_ref[k]).astype(bf16)
        vec = unskew(jnp.concatenate(strip + [jnp.zeros((LANES, LANES), f32)], axis=1))
        left = jnp.sum(jnp.sum(far_left, axis=0, keepdims=True), axis=1, keepdims=True)
        right = jnp.sum(jnp.sum(far_right, axis=0, keepdims=True), axis=1, keepdims=True)
        vec = vec + jnp.where(lane == 0, left, 0.0) + jnp.where(lane == 510, right, 0.0)
        dvec_ref[pl.ds((pair + pairs_before) * 2 + k, 1), :] = vec
    dq_ref[...] = (jnp.where(low_half, dq[0], dq[1]) * HEAD_DIM ** (-0.5)).astype(bf16)
    half = keep_ref.shape[0]
    start = pl.multiple_of(pair * BLOCK, LANES)
    queries, rest = pl.ds(start, LANES), pl.ds(start + LANES, 2 * LANES)
    send_ref[:, queries] = mm(normed_t_ref[half:, :], dq_ref[...]).astype(bf16)
    send_ref[:, rest] = mm_nt(normed_t_ref[half:, :], dkv_ref[...]).astype(bf16)
    keep_ref[:, queries] = mm(normed_t_ref[:half, :], dq_ref[...])
    keep_ref[:, rest] = mm_nt(normed_t_ref[:half, :], dkv_ref[...])

    if vec_in is not None:

        @pl.when(pair == 0)
        def _():
            dvec_ref[: 2 * pairs_before, :] = vec_in[...]

    if not last:
        return

    @pl.when(pair == pl.num_programs(0) - 1)
    def _():
        table_col = table_column(
            jnp.concatenate([dvec_ref[...], jnp.zeros((16 - HEADS, 4 * LANES), f32)], axis=0),
            hmask_ref,
            umask_ref,
        )
        lane = lax.broadcasted_iota(jnp.int32, (2 * half, LANES), 1)
        packed = jnp.where(lane == 0, table_col, 0.0)
        end = keep_ref.shape[1] - LANES
        keep_ref[:, end:] = packed[:half]
        send_ref[:, end:] = packed[half:].astype(bf16)


def split_three(values):
    one, rest = split_two(values)
    two, three = split_two(values - one.astype(f32))
    return one, two, three


def table_column(vec, hmask_ref, umask_ref):
    offset = lax.broadcasted_iota(jnp.int32, (LANES, 4 * LANES), 1) - 255
    onehot = (
        lax.broadcasted_iota(jnp.int32, (LANES, 4 * LANES), 0) == buckets_of(offset)
    ).astype(f32).astype(bf16)
    one, two, three = split_three(vec)
    table = mm_nt(one, onehot) + (mm_nt(two, onehot) + mm_nt(three, onehot))
    heads = hmask_ref[:, :16]
    one, two, three = split_three(table)
    spread = mm(heads, one) + (mm(heads, two) + mm(heads, three))
    return jnp.sum(spread * umask_ref[...].astype(f32), axis=1, keepdims=True)


def last_kernel(own_get, oth_get, xperm_get, gain_get, perm_get, after_get, *refs):
    *gets, out_out, grads_ref = refs
    runs = len(gets) // 2
    at = 0
    for dq_get, dkv_get in zip(gets[:runs], gets[runs:]):
        dq, dkv_t = dq_get()[...], dkv_get()
        for c in range(dq.shape[1] // LANES):
            grads_ref[:, at : at + LANES] = dq[:, c * LANES : (c + 1) * LANES]
            moved = jnp.transpose(dkv_t[2 * c * LANES : 2 * (c + 1) * LANES, :].astype(f32))
            grads_ref[:, at + LANES : at + BLOCK] = moved.astype(bf16)
            at += BLOCK
    grads = grads_ref[...]
    cols = slice(0, at)
    grad = jnp.concatenate(
        [mm_nt(grads, own_get()[:, cols]), mm_nt(grads, oth_get()[:, cols])], axis=1
    )
    x = xperm_get()[...].astype(f32)
    inverse = inverse_rms(x)
    unit = x * inverse
    scaled = grad * gain_get()[0:1, :]
    back = inverse * (scaled - unit * jnp.mean(scaled * unit, axis=-1, keepdims=True))
    high, rest = split_two(back)
    perm = perm_get()[...]
    out_out.ref[...] = (after_get()[...] + (mm_nt(high, perm) + mm_nt(rest, perm))).astype(bf16)


def fold_kernel(plan, *refs):
    refs = list(refs)
    total_in = sum(1 + n for members, _ in plan for n in members)
    ins, outs = refs[:total_in], refs[total_in:]
    for members, parts in plan:
        outs_here = [outs.pop(0) for _ in range(parts)]
        at = 0
        for arrived in members:
            total = ins.pop(0)[...]
            for _ in range(arrived):
                total = total + ins.pop(0)[...].astype(f32)
            rows = total.shape[0] // parts
            cols = slice(at, at + total.shape[1])
            at += total.shape[1]
            for m, out in enumerate(outs_here):
                out[:, cols] = total[m * rows : (m + 1) * rows].astype(out.dtype)


def summed(first_ref, moved):
    total = first_ref[...]
    for piece in moved:
        total = total + piece[...].astype(f32)
    return total


def as_row(column):
    size = column.shape[0]
    same = lax.broadcasted_iota(jnp.int32, (size, size), 0) == lax.broadcasted_iota(
        jnp.int32, (size, size), 1
    )
    return jnp.sum(jnp.where(same, column, 0.0), axis=0, keepdims=True)


def finish_kernel(moved_group, gain_get, wq_get, wk_get, wv_get, first_group, first_last, *refs):
    *moved, wo_out, router_out, gain_two_out, wq_out, wk_out, wv_out, gain_out, table_out = refs
    total = summed(first_group, moved[:moved_group])
    width, experts = wo_out.ref.shape[1], router_out.ref.shape[1]
    wo_out.ref[...] = total[:, :width]
    wo_out.send()
    router_out.ref[...] = total[:, width : width + experts]
    gain_two_out.ref[...] = as_row(total[:, width + experts : width + experts + 1])
    early = RUNS[1]
    sources = [(total, total.shape[1] - early * BLOCK)]
    total = summed(first_last, moved[moved_group:])
    sources.append((total, -early * BLOCK))
    for c in range(PAIRS):
        source, base = sources[c >= early]
        for k, out in enumerate((wq_out, wk_out, wv_out)):
            at = base + c * BLOCK + k * LANES
            out.ref[:, c * LANES : (c + 1) * LANES] = source[:, at : at + LANES]
    for out in (wq_out, wk_out, wv_out):
        out.send()
    products = None
    for get, out in ((wq_get, wq_out), (wk_get, wk_out), (wv_get, wv_out)):
        part = get()[...].astype(bf16).astype(f32) * out.ref[...]
        products = part if products is None else products + part
    gain = gain_get()[...].astype(bf16).astype(f32)
    gain_out.ref[...] = as_row(jnp.sum(products, axis=1, keepdims=True)) / gain
    at = total.shape[1] - LANES
    entries = table_out.ref.shape[1]
    table_out.ref[...] = as_row(total[:, at : at + 1])[:, :entries]


def join_kernel(*refs):
    *pieces, out_ref, sems = refs
    rows = pieces[0].shape[0]
    copies = [
        pltpu.make_async_copy(p, out_ref.at[pl.ds(i * rows, rows), :], sems.at[i])
        for i, p in enumerate(pieces)
    ]
    for copy in copies:
        copy.start()
    for copy in copies:
        copy.wait()


def join(values, moved, space):
    pieces = [values, *moved]
    if values.shape[0] % 8:
        return jnp.concatenate(pieces, axis=0)
    shape = (len(pieces) * values.shape[0], values.shape[1])
    any_ref = pl.BlockSpec(memory_space=pl.ANY)
    return pl.pallas_call(
        join_kernel,
        out_shape=space(shape, values.dtype),
        in_specs=[any_ref] * len(pieces),
        out_specs=any_ref,
        scratch_shapes=[pltpu.SemaphoreType.DMA((len(pieces),))],
        **parameters(4, 1),
    )(*pieces)


def assemble_kernel(moves, count, *refs):
    sources, outs, sems = refs[:count], refs[count:-1], refs[-1]
    copies = []
    for i, (source, row, rows, col, cols, out, to_row, to_col) in enumerate(moves):
        copies.append(
            pltpu.make_async_copy(
                sources[source].at[pl.ds(row, rows), pl.ds(col, cols)],
                outs[out].at[pl.ds(to_row, rows), pl.ds(to_col, cols)],
                sems.at[i],
            )
        )
    for copy in copies:
        copy.start()
    for copy in copies:
        copy.wait()


def assemble(arrays, outs, moves):
    if any(m[i] % 8 for m in moves for i in (1, 2, 6)):
        made = [jnp.zeros(o.shape, o.dtype) for o in outs]
        for a, row, rows, col, cols, out, to_row, to_col in moves:
            block = arrays[a][row : row + rows, col : col + cols]
            made[out] = lax.dynamic_update_slice(made[out], block, (to_row, to_col))
        return made
    any_ref = pl.BlockSpec(memory_space=pl.ANY)
    return pl.pallas_call(
        functools.partial(assemble_kernel, moves, len(arrays)),
        out_shape=list(outs),
        in_specs=[any_ref] * len(arrays),
        out_specs=[any_ref] * len(outs),
        scratch_shapes=[pltpu.SemaphoreType.DMA((len(moves),))],
        **parameters(4, 1),
    )(*arrays)


def expert_call(experts, steps, slots, width, units, wide):
    slab = (slots * width // LANES, LANES)
    any_ref, vmem_ref = (pl.BlockSpec(memory_space=m) for m in (pl.ANY, pltpu.VMEM))
    outs = [slab, (slots, width), (slots, width), (slots, width), (slots, wide)]
    call = pl.pallas_call(
        functools.partial(expert_kernel, experts, steps),
        out_shape=[far(shape, bf16) for shape in outs] + [far((slots, LANES), f32)],
        in_specs=[pl.BlockSpec(memory_space=pltpu.SMEM), vmem_ref] + [any_ref] * 5,
        out_specs=[any_ref] * 6,
        scratch_shapes=[pltpu.VMEM(slab, f32)]
        + [
            pltpu.VMEM(shape, bf16)
            for shape in (
                (width, wide), (slots, width), (width, units), (units, width),
                (slots, units), (slots, units), (slots, units),
            )
        ]
        + [pltpu.VMEM(shape, bf16) for shape in outs]
        + [
            pltpu.VMEM((slots, LANES), f32),
            pltpu.SemaphoreType.DMA((2 + 3 * steps,)),
            pltpu.SemaphoreType.DMA((6,)),
        ],
        **parameters(52, 18),
    )
    return lambda me, recv, *rest: call(me, recv, *[place(Far(a)) for a in rest])


def shards(
    count,
    inputs,
    segment_ids,
    routes,
    cotangent,
    gain_attn,
    gain_ffn,
    bias_table,
    w_query,
    w_key,
    w_value,
    w_output,
    w_router,
    w_in,
    w_out,
):
    tokens, width = inputs.shape
    experts = w_router.shape[1]
    rows_local = w_query.shape[0]
    entries = bias_table.shape[0]
    hidden_units = w_in.shape[2]
    capacity = max(2, 5 * tokens // (4 * experts))
    slots = experts * capacity
    blocks = width // LANES
    half = width // 2
    wide = -(-(experts + 1) // LANES) * LANES
    me = lax.axis_index("seq").astype(jnp.int32).reshape(1)
    vmem = pl.BlockSpec(memory_space=pltpu.VMEM)

    groups = bit_groups(count)
    levels = list(reversed(groups[1:]))
    columns = PAIRS * BLOCK
    piece, tail = flat_call(
        functools.partial(pack_kernel, experts),
        [near((rows_local, columns + LANES), bf16), near((rows_local, width + wide), bf16)],
        us=1,
    )(
        *map(Far, (gain_attn[None, :], gain_ffn[None, :], bias_table[None, :])),
        *map(Far, (w_query, w_key, w_value, w_output, w_router)),
    )

    def reach(values, low_bit, bits):
        return [swap(values, m << low_bit, count) for m in range(1, 1 << bits)]

    order = np.asarray(relative_order(count), np.int32)
    rel_row = jnp.asarray(np.repeat(order, rows_local)[None, :])
    off_row = jnp.asarray(np.tile(np.arange(rows_local, dtype=np.int32), count)[None, :])
    slab = (slots * blocks, LANES)
    slab_stage = pltpu.VMEM(slab, f32)
    perm, xperm, segrow, segcol, hmask, umask, dt, dm = flat_call(
        functools.partial(prepare_kernel, rows_local, entries, experts, capacity),
        [
            far((width, width), bf16),
            far((tokens, width), bf16),
            far((8, tokens), f32),
            far((tokens, LANES), f32),
            far((width, LANES), bf16),
            far((width, LANES), bf16),
            far((tokens, slots), bf16),
            far((slots, tokens), bf16),
        ],
        us=8,
    )(me, Far(rel_row), Far(off_row), Far(inputs), Far(segment_ids), Far(routes))
    cot_send = flat_call(dispatch_kernel, [far(slab, bf16)], us=3, scratch=[slab_stage])(
        Far(dm), Far(cotangent)
    )[0]

    moved = reach(piece, *levels[0])
    moved = lax.optimization_barrier((*moved, perm))[:-1]
    total = columns + LANES
    sizes = (columns // 2, total - columns // 2)
    starts = (0, sizes[0])
    rows = rows_local
    pieces = [piece, *moved]
    moves = [
        (i, 0, rows, starts[p], sizes[p], p, i * rows, 0) for i in range(len(pieces)) for p in range(2)
    ]
    rows *= len(pieces)
    parts = assemble(pieces, [near((rows, size), bf16) for size in sizes], moves)
    for k, (low_bit, _) in enumerate(levels[1:]):
        steps_of = ((2 << low_bit, 1 << low_bit), (1 << low_bit, 2 << low_bit))
        got = [swap(part, d[0], count) for part, d in zip(parts, steps_of)]
        tail_moved = reach(after(tail, *parts, cot_send), *levels[k])
        got = lax.optimization_barrier((*got, cot_send))[:-1]
        moves = [(p + 2 * i, 0, rows, 0, sizes[p], p, i * rows, 0) for i in range(2) for p in range(2)]
        parts = assemble(
            [*parts, *got], [near((2 * rows, size), bf16) for size in sizes], moves
        )
        got = [swap(part, d[1], count) for part, d in zip(parts, steps_of)]
        got = lax.optimization_barrier((*got, *tail_moved))[:2]
        tail = join(tail, tail_moved, near)
        final = k == len(levels) - 2
        order_of = (((0, 2), (1, 3)), ((0, 1), (2, 3)))
        moves = [
            (p + 2 * i, b * rows, rows, 0, sizes[p], 0 if final else p, order_of[p][i][b] * rows,
             starts[p] if final else 0)
            for i in range(2) for p in range(2) for b in range(2)
        ]
        outs = [far((4 * rows, total), bf16)] if final else [near((4 * rows, size), bf16) for size in sizes]
        parts = assemble([*parts, *got], outs, moves)
        rows *= 4
    piece = parts[0]
    other = swap(piece, 1, count)
    tail_moved = reach(after(tail, piece), *levels[-1])

    slab_split = (count, slots * blocks // count, LANES)

    def exchange(rows):
        return lax.all_to_all(
            rows.reshape(slab_split), "seq", split_axis=0, concat_axis=0, tiled=True
        ).reshape(slab)

    cot_recv = exchange(after(cot_send, tail))

    def whole(shape):
        return pl.BlockSpec(shape, lambda i: (0,) * len(shape))

    pair_probs = pl.BlockSpec((2, tokens, tokens), lambda i: (i, 0, 0))
    piece, other = Far(piece), Far(other)
    small_block = pl.BlockSpec((half, LANES), lambda i: (0, columns // LANES))
    pair_weights = pl.BlockSpec((half, BLOCK), lambda i: (0, i))
    qkv, probs, mixed, normed, gain_one = grid_call(
        attend_forward_kernel,
        [
            far((tokens, PAIRS * BLOCK), bf16),
            far((HEADS, tokens, tokens), bf16),
            near((tokens, width), bf16),
            far((tokens, width), bf16),
            far((8, width), f32),
        ],
        grid=(PAIRS,),
        in_specs=[whole((tokens, width))]
        + [pair_weights, pair_weights, small_block, small_block]
        + [whole(shape) for shape in ((width, LANES), (width, LANES), (8, tokens), (tokens, LANES))],
        out_specs=[
            pl.BlockSpec((tokens, BLOCK), lambda i: (0, i)),
            pair_probs,
            vmem,
            whole((tokens, width)),
            whole((8, width)),
        ],
        scratch=[
            pltpu.VMEM((16, 4 * LANES), f32),
            pltpu.VMEM((2, tokens, tokens), f32),
            pltpu.VMEM((2, LANES, 3 * LANES), f32),
        ],
        us=14,
    )(
        Far(after(xperm, tail)), piece, other, piece, other,
        *map(Far, (hmask, umask, segrow, segcol)),
    )
    tail_moved = lax.optimization_barrier((*tail_moved, mixed))[:-1]
    tail = join(tail, tail_moved, near)
    tail_other = swap(tail, 1, count)

    after_rows, low_two, row_send, gain_two, mixed_perm = flat_call(
        functools.partial(after_kernel, experts),
        [
            far((tokens, width), f32),
            far((tokens, width), bf16),
            far(slab, bf16),
            far((8, width), f32),
            far((tokens, width), bf16),
        ],
        us=6,
        scratch=[slab_stage],
    )(mixed, Far(perm), tail, tail_other, Far(inputs), Far(dm))
    row_recv = exchange(row_send)

    steps = 6
    units = hidden_units // steps
    weight_in = pl.BlockSpec((1, width, units), lambda i: (0, 0, i))
    weight_out = pl.BlockSpec((1, units, width), lambda i: (0, i, 0))

    low_in = pl.BlockSpec((width, units), lambda i: (0, i))
    low_out = pl.BlockSpec((units, width), lambda i: (i, 0))
    slot_units = pl.BlockSpec((slots, units), lambda i: (0, i))
    cot_rows, win_low, wout_low, grad_hidden = grid_call(
        early_expert_kernel,
        [
            far((slots, width), bf16),
            far((width, hidden_units), bf16),
            far((hidden_units, width), bf16),
            far((slots, hidden_units), bf16),
        ],
        grid=(steps,),
        in_specs=[whole(slab), weight_in, weight_out],
        out_specs=[whole((slots, width)), low_in, low_out, slot_units],
        us=13,
        scratch=[slab_stage],
    )(cot_recv, Far(w_in), Far(w_out))
    mixed_t, normed_t, output_w, router_w, query_t = flat_call(
        between_kernel,
        [
            far((width, tokens), bf16),
            far((width, tokens), bf16),
            far((width, width), bf16),
            far((width, wide), bf16),
            far((width, tokens), bf16),
        ],
        us=7,
    )(Far(mixed_perm), Far(normed), tail, tail_other, Far(perm), Far(qkv))
    back_send, made, x_rows, grad_rows, grad_logits, gates = expert_call(
        experts, steps, slots, width, hidden_units, wide
    )(me, row_recv, router_w, cot_rows, win_low, wout_low, grad_hidden)
    back_recv = exchange(back_send)
    grad_inner, grad_outer, grad_router, prod_send = grid_call(
        expert_weights_kernel,
        [
            far((1, width, hidden_units), f32),
            far((1, hidden_units, width), f32),
            far((width, wide), f32),
            far(slab, bf16),
        ],
        grid=(steps,),
        in_specs=[
            whole((slots, width)),
            whole((slots, width)),
            whole((slots, wide)),
            whole((slots, LANES)),
            whole((slots, width)),
            whole((width, width)),
            low_in,
            slot_units,
        ],
        out_specs=[weight_in, weight_out, whole((width, wide)), whole(slab)],
        us=19,
        scratch=[pltpu.VMEM((width, slots), bf16), slab_stage],
    )(*map(Far, (x_rows, grad_rows, grad_logits, gates, made, perm, win_low, grad_hidden)))
    prod_recv = exchange(prod_send)

    row_scratch = pltpu.VMEM((slots, width), bf16)
    grad_after, grad_mixed, keep_o, send_o = flat_call(
        functools.partial(norm_two_kernel, experts),
        [
            far((tokens, width), f32),
            near((tokens, width), bf16),
            near((half, width + wide), f32),
            near((half, width + wide), bf16),
        ],
        us=1,
        scratch=[slab_stage, row_scratch],
    )(
        back_recv,
        *map(Far, (dt, after_rows, gain_two, cotangent, output_w, mixed_t, perm, grad_router)),
    )

    def backward(run, ready):
        start, stop = RUNS[run], RUNS[run + 1]
        last = stop == PAIRS
        vec = before.get("vec")
        here = [Far(qkv), Far(query_t), Far(probs), after(grad_mixed, *ready), Far(normed_t)]
        specs = [
            pl.BlockSpec((tokens, BLOCK), lambda i: (0, i + start)),
            pl.BlockSpec((LANES, tokens), lambda i: (i + start, 0)),
            pl.BlockSpec((2, tokens, tokens), lambda i: (i + start, 0, 0)),
            vmem,
            whole((width, tokens)),
        ]
        if vec is not None:
            here.append(vec)
            specs.append(vmem)
        if last:
            here += [Far(hmask), Far(umask)]
            specs += [whole((width, LANES))] * 2
        pairs = stop - start
        cols = pairs * BLOCK + (LANES if last else 0)
        keep, send, vec, dq, dkv_t = grid_call(
            functools.partial(attend_backward_kernel, vec is not None, last),
            [
                near((half, cols), f32),
                near((half, cols), bf16),
                near((2 * stop, 4 * LANES), f32),
                far((tokens, pairs * LANES), bf16),
                far((2 * pairs * LANES, tokens), bf16),
            ],
            grid=(pairs,),
            in_specs=specs,
            out_specs=[
                vmem,
                vmem,
                vmem,
                pl.BlockSpec((tokens, LANES), lambda i: (0, i)),
                pl.BlockSpec((2 * LANES, tokens), lambda i: (i, 0)),
            ],
            scratch=[
                pltpu.VMEM((2, tokens, tokens), f32),
                pltpu.VMEM((2, tokens, tokens), bf16),
            ],
            us=(1, 4)[run],
            vmem=24,
        )(*here)
        before.update(vec=vec)
        born.append((keep, send))
        grads.append((dq, dkv_t))
        return keep

    def results(ready):
        return flat_call(
            functools.partial(output_kernel, experts),
            [far((tokens, width), bf16)],
            us=0.001,
            scratch=[slab_stage, row_scratch],
            vmem=20,
        )(after(prod_recv, *ready), *map(Far, (dt, low_two, router_w, routes, after_rows)))[0]

    def finish(ready):
        return flat_call(
            last_kernel,
            [far((tokens, width), bf16)],
            us=8,
            scratch=[pltpu.VMEM((tokens, columns), bf16)],
            vmem=32,
        )(
            piece, other, Far(after(xperm, *ready)),
            *map(Far, (gain_one, perm, grad_after)),
            *[Far(g[0]) for g in grads], *[Far(g[1]) for g in grads],
        )[0]

    before, born, grads = {}, [(keep_o, send_o)], []
    ups = groups[1:]
    core = (1, 2)
    first = (1 << ups[0][0], 1 << ups[0][1])
    direct = [(1 << low_bit, 1 << bits) for low_bit, bits in ups[1:]]
    halving = [(1 << (low_bit + b), 2) for low_bit, bits in ups[1:] for b in reversed(range(bits))]
    plans = {c: {c: core, c + 1: first} for c in range(3)}
    plans[2].update({4 + i: step for i, step in enumerate(direct)})
    plans[3] = {3 + i: step for i, step in enumerate(halving)}
    work = {run: [functools.partial(backward, run)] for run in range(2)}
    work.update({2: [finish], 3: [results]})
    own, going, flight, finished = {}, {}, {}, {}
    output = grad_inputs = None
    end = max(max(plan) for plan in plans.values())
    own[0], going[0] = born[0][0], [born[0][1]]
    for slot in range(end + 1):
        for c, plan in plans.items():
            if slot in plan:
                distance, parts = plan[slot]
                flight[c] = [swap(g, (m + 1) * distance, count) for m, g in enumerate(going[c])]
        ready = [own[c] for c in flight] + ([prod_recv] if slot == 2 else [])
        for step in work.get(slot, []):
            value = step(ready)
            ready = [value]
            if step is results:
                output = value
            if step is finish:
                grad_inputs = value
        if slot in work:
            for c in flight:
                flight[c] = list(lax.optimization_barrier((*flight[c], value))[:-1])
        folds, args, outs, cut = [], [], [], []

        def fold(members, following, name):
            parts = following[1]
            folds.append(([len(flight[c]) if c in flight else 0 for c in members], parts))
            rows = own[members[0]].shape[0] // parts
            cols = sum(own[c].shape[1] for c in members)
            for c in members:
                args.append(own[c])
                args.extend(flight.pop(c, []))
            outs.append(near((rows, cols), f32))
            outs.extend([near((rows, cols), bf16)] * (parts - 1))
            cut.append((name, parts))

        if slot == 2:
            fold([0, 1], plans[3][3], 3)
        for c in list(flight):
            following = plans[c].get(slot + 1)
            if following or c < 2:
                fold([c], following or (0, 1), c)
            else:
                finished[c] = [own[c], *flight.pop(c)]
        if folds:
            folded = list(
                flat_call(functools.partial(fold_kernel, folds), outs, us=1, vmem=16)(*args)
            )
            for c, parts in cut:
                own[c] = folded.pop(0)
                going[c] = [folded.pop(0) for _ in range(parts - 1)]
            if len(born) == slot + 2:
                own[slot + 1] = born[-1][0]
                going[slot + 1] = [after(born[-1][1], own[cut[0][0]])]

    def row(size):
        return far((1, size), f32)

    square = far((rows_local, width), f32)
    grad_wo, grad_wr, grad_gain_two, grad_q, grad_k, grad_v, grad_gain_one, grad_table = flat_call(
        functools.partial(finish_kernel, len(finished[3]) - 1),
        [square, far((rows_local, experts), f32), row(rows_local)]
        + [square, square, square, row(rows_local), row(entries)],
        us=2,
        vmem=16,
    )(
        *map(Far, (gain_attn[None, :], w_query, w_key, w_value)),
        finished[3][0], finished[2][0], *finished[3][1:], *finished[2][1:],
    )

    return (
        output,
        grad_inputs,
        grad_gain_one[0],
        grad_gain_two[0],
        grad_table[0],
        grad_q,
        grad_k,
        grad_v,
        grad_wo,
        grad_wr,
        grad_inner,
        grad_outer,
    )


def solution(mesh):
    row, flat, cube = P("seq", None), P("seq"), P("seq", None, None)
    in_specs = (row,) * 4 + (flat,) * 3 + (row,) * 5 + (cube,) * 2
    out_specs = (row,) * 2 + (flat,) * 3 + (row,) * 5 + (cube,) * 2
    return jax.shard_map(
        functools.partial(shards, mesh.shape["seq"]),
        mesh=mesh,
        in_specs=in_specs,
        out_specs=out_specs,
        check_vma=False,
    )
```

```python
import functools

import jax
import jax.numpy as jnp
import numpy as np
from jax import lax
from jax.experimental import pallas as pl
from jax.experimental.pallas import tpu as pltpu
from jax.sharding import PartitionSpec as P

HEADS = 12
HEAD_DIM = 64
BUCKETS = 32
PAIRS = HEADS // 2
RUNS = (0, 4, 6)
ABREAST = 1
LANES = 128
BLOCK = 3 * LANES

epsilon = 1e-06
bucket_edges = (1, 2, 3, 4, 5, 6, 7, 8, 12, 16, 23, 32, 46, 64, 91)
gelu_coef = 0.7978845608028654
cubic_coef = 0.044715

f32 = jnp.float32
bf16 = jnp.bfloat16


def bit_groups(count):
    bits = count.bit_length() - 1
    groups, low = [(0, 1)], 1
    while low < bits:
        width = min(2, bits - low)
        groups.append((low, width))
        low += width
    return groups


def relative_order(count):
    order = [0]
    for low, width in bit_groups(count):
        order = [base + (m << low) for base in order for m in range(1 << width)]
    return order


def swap(values, distance, count):
    return lax.ppermute(values, "seq", [(i, i ^ distance) for i in range(count)])


def after(values, *others):
    return lax.optimization_barrier((values, *others))[0]


def mm(left, right):
    return jnp.dot(left, right, preferred_element_type=f32)


def mm_nt(left, right):
    return lax.dot_general(left, right, (((1,), (1,)), ((), ())), preferred_element_type=f32)


def mm_tn(left, right):
    return lax.dot_general(left, right, (((0,), (0,)), ((), ())), preferred_element_type=f32)


def split_two(values):
    high = values.astype(bf16)
    return high, (values - high.astype(f32)).astype(bf16)


class Far:
    def __init__(self, values):
        self.values = values


def near(shape, dtype):
    return pltpu.VMEM(shape, dtype)


def far(shape, dtype):
    return pltpu.HBM(shape, dtype)


class Fetched:
    def __init__(self, copy, ref):
        self.copy, self.ref, self.here = copy, ref, False

    def __call__(self):
        if not self.here:
            self.copy.wait()
            self.here = True
        return self.ref


class Stored:
    def __init__(self, copy, ref):
        self.copy, self.ref, self.sent = copy, ref, False

    def send(self):
        self.copy.start()
        self.sent = True


def place(a):
    if isinstance(a, Far):
        return pltpu.with_memory_space_constraint(a.values, pltpu.HBM)
    return a


def parameters(vmem, us):
    return dict(
        compiler_params=pltpu.CompilerParams(vmem_limit_bytes=vmem * 1024 * 1024),
        cost_estimate=pl.CostEstimate(
            flops=int(us * 10**9), bytes_accessed=int(us * 10**6), transcendentals=0
        ),
    )


def grid_call(body, outs, grid, in_specs, out_specs, us, scratch=(), vmem=40):
    call = pl.pallas_call(
        body,
        out_shape=list(outs),
        grid=grid,
        in_specs=in_specs,
        out_specs=out_specs,
        scratch_shapes=list(scratch),
        **parameters(vmem, us),
    )
    return lambda *args: call(*[place(a) for a in args])


def flat_call(body, outs, us, scratch=(), vmem=32):
    def run(*args):
        lazy = [isinstance(a, Far) for a in args]
        late = [o.memory_space == pltpu.HBM for o in outs]
        values = [a.values if f else a for a, f in zip(args, lazy)]
        n_in, n_out, n_scratch = len(args), len(outs), len(scratch)
        any_ref, vmem_ref, smem_ref = (
            pl.BlockSpec(memory_space=m) for m in (pl.ANY, pltpu.VMEM, pltpu.SMEM)
        )
        in_copies = [pltpu.VMEM(v.shape, v.dtype) for v, f in zip(values, lazy) if f]
        out_copies = [pltpu.VMEM(o.shape, o.dtype) for o, f in zip(outs, late) if f]

        def wrapped(*refs):
            ins, rest = refs[:n_in], refs[n_in:]
            results, rest = rest[:n_out], rest[n_out:]
            own, rest = rest[:n_scratch], rest[n_scratch:]
            fetched, rest = list(rest[: len(in_copies)]), rest[len(in_copies) :]
            stored, rest = list(rest[: len(out_copies)]), rest[len(out_copies) :]
            sems = list(rest)
            given, made = [], []
            for ref, f in zip(ins, lazy):
                if f:
                    copy = pltpu.make_async_copy(ref, fetched[0], sems.pop())
                    copy.start()
                    given.append(Fetched(copy, fetched.pop(0)))
                else:
                    given.append(ref)
            for ref, f in zip(results, late):
                if f:
                    made.append(
                        Stored(pltpu.make_async_copy(stored[0], ref, sems.pop()), stored[0])
                    )
                    stored.pop(0)
                else:
                    made.append(ref)
            body(*given, *made, *own)
            for item in given:
                if isinstance(item, Fetched):
                    item()
            for item in made:
                if isinstance(item, Stored):
                    if not item.sent:
                        item.send()
                    item.copy.wait()

        return pl.pallas_call(
            wrapped,
            out_shape=list(outs),
            in_specs=[
                any_ref if f else (smem_ref if v.size == 1 else vmem_ref)
                for v, f in zip(values, lazy)
            ],
            out_specs=[any_ref if f else vmem_ref for f in late],
            scratch_shapes=list(scratch)
            + in_copies
            + out_copies
            + [pltpu.SemaphoreType.DMA] * (len(in_copies) + len(out_copies)),
            **parameters(vmem, us),
        )(*[place(a) for a in args])

    return run


def to_slab(values, stage, out_ref):
    slots, width = values.shape
    blocks = width // LANES
    for c in range(blocks):
        stage[pl.ds(c, slots, stride=blocks), :] = values[:, c * LANES : (c + 1) * LANES]
    out_ref[...] = stage[...].astype(out_ref.dtype)


def from_slab(in_ref, stage, slots, put):
    stage[...] = in_ref[...].astype(f32)
    blocks = in_ref.shape[0] // slots
    for c in range(blocks):
        put(c, stage[pl.ds(c, slots, stride=blocks), :])


def to_column(row, width=LANES):
    return jnp.transpose(jnp.broadcast_to(row, (width, row.shape[1])))


def inverse_rms(values):
    return lax.rsqrt(jnp.mean(values * values, axis=-1, keepdims=True) + epsilon)


def buckets_of(offset):
    magnitude = jnp.abs(offset)
    bucket = jnp.zeros(offset.shape, jnp.int32)
    for edge in bucket_edges:
        bucket = bucket + (magnitude >= edge).astype(jnp.int32)
    return bucket + BUCKETS // 2 * (offset > 0).astype(jnp.int32)


def prepare_kernel(
    rows_local, entries, experts, capacity,
    me_ref, rel_ref, off_ref, x_get, seg_get, routes_get,
    perm_out, xperm_out, segrow_out, segcol_out, hmask_out, umask_out, dt_out, dm_out,
):
    perm_ref, xperm_ref, segrow_ref, segcol_ref, hmask_ref, umask_ref, dt_ref, dm_ref = (
        out.ref
        for out in (perm_out, xperm_out, segrow_out, segcol_out, hmask_out, umask_out, dt_out, dm_out)
    )
    x_ref, seg_ref, routes_ref = x_get(), seg_get(), routes_get()
    tokens, width = x_ref.shape
    slots = dm_ref.shape[0]
    me = me_ref[0]
    device_row = rel_ref()[...] ^ me
    off_row = off_ref()[...]
    true_row = device_row * rows_local + off_row
    perm = (lax.broadcasted_iota(jnp.int32, (width, width), 0) == true_row).astype(f32).astype(bf16)
    perm_ref[...] = perm
    perm_out.send()
    xperm_ref[...] = mm(x_ref[...], perm).astype(bf16)
    segments = seg_ref[...].astype(f32)
    segrow_ref[...] = jnp.broadcast_to(segments, segrow_ref.shape)
    segcol_ref[...] = to_column(segments)
    flat = device_row * entries + off_row
    bucket_row = ((flat.astype(f32) + 0.5) * (1.0 / HEADS)).astype(jnp.int32)
    head_row = jnp.where(off_row < entries, flat - bucket_row * HEADS, -1)
    bucket_col = to_column(bucket_row.astype(f32))
    head_col = to_column(head_row.astype(f32))
    lane = lax.broadcasted_iota(jnp.int32, (width, LANES), 1).astype(f32)
    hmask_ref[...] = (head_col == lane).astype(f32).astype(bf16)
    umask_ref[...] = (bucket_col == lane).astype(f32).astype(bf16)
    routes = routes_ref[...]
    labels = lax.broadcasted_iota(jnp.int32, (tokens, experts), 1)
    picked = (routes == labels).astype(f32)
    earlier = (
        lax.broadcasted_iota(jnp.int32, (tokens, tokens), 1)
        <= lax.broadcasted_iota(jnp.int32, (tokens, tokens), 0)
    ).astype(f32).astype(bf16)
    counts = mm(earlier, picked.astype(bf16))
    position = jnp.sum(counts * picked, axis=1, keepdims=True) - 1.0
    slot_col = jnp.where(
        position < capacity, routes.astype(f32) * capacity + position, -1.0
    )
    slot_lane = lax.broadcasted_iota(jnp.int32, (tokens, slots), 1).astype(f32)
    dt_ref[...] = (slot_col == slot_lane).astype(f32).astype(bf16)
    slot_row = jnp.transpose(jnp.broadcast_to(slot_col, (tokens, LANES)))[0:1, :]
    slot_sub = lax.broadcasted_iota(jnp.int32, (slots, tokens), 0).astype(f32)
    dm_ref[...] = (slot_sub == slot_row).astype(f32).astype(bf16)


def dispatch_kernel(dm_get, cot_get, send_out, stage):
    to_slab(mm(dm_get()[...], cot_get()[...]), stage, send_out.ref)


def pack_kernel(
    experts, gain_get, gain_two_get, table_get, wq_get, wk_get, wv_get, wo_get, router_get,
    piece, tail,
):
    gain_ref, gain_two_ref, table_ref = gain_get(), gain_two_get(), table_get()
    wq_ref, wk_ref, wv_ref, wo_ref, router_ref = (
        get() for get in (wq_get, wk_get, wv_get, wo_get, router_get)
    )
    rows, width = wq_ref.shape

    def column(ref):
        size = ref.shape[1]
        same = lax.broadcasted_iota(jnp.int32, (rows, size), 0) == lax.broadcasted_iota(
            jnp.int32, (rows, size), 1
        )
        return jnp.sum(jnp.where(same, ref[...], 0.0), axis=1, keepdims=True)

    for c in range(PAIRS):
        for k, w in enumerate((wq_ref, wk_ref, wv_ref)):
            at = c * BLOCK + k * LANES
            piece[:, at : at + LANES] = w[:, c * LANES : (c + 1) * LANES].astype(bf16)
    lane = lax.broadcasted_iota(jnp.int32, (rows, LANES), 1)
    small = jnp.where(lane == 0, column(gain_ref), jnp.where(lane == 1, column(table_ref), 0.0))
    piece[:, PAIRS * BLOCK :] = small.astype(bf16)
    tail[:, :width] = wo_ref[...].astype(bf16)
    lane = lax.broadcasted_iota(jnp.int32, (rows, tail.shape[1] - width), 1)
    tail[:, width:] = jnp.where(lane == experts, column(gain_two_ref), 0.0).astype(bf16)
    tail[:, width : width + experts] = router_ref[...].astype(bf16)


def attend_forward_kernel(
    xperm_ref, own_ref, oth_ref, own_small, oth_small, hmask_ref, umask_ref, segrow_ref, segcol_ref,
    qkv_ref, probs_ref, mixed_ref, normed_ref, gain_ref,
    vec_ref, score_ref, strip_ref,
):
    half = own_ref.shape[0]
    tokens = segcol_ref.shape[0]
    blocks = tokens // LANES
    pair = pl.program_id(0)

    @pl.when(pair == 0)
    def _():
        packed = jnp.concatenate([own_small[...].astype(f32), oth_small[...].astype(f32)], axis=0)
        gain = jnp.transpose(packed)[0:1, :]
        gain_ref[...] = jnp.broadcast_to(gain, gain_ref.shape)
        spread = (packed[:, 1:2] * hmask_ref[...].astype(f32)).astype(bf16)
        table = mm_tn(spread, umask_ref[...])[:16]
        offset = lax.broadcasted_iota(jnp.int32, (LANES, 4 * LANES), 1) - 255
        onehot = (
            lax.broadcasted_iota(jnp.int32, (LANES, 4 * LANES), 0) == buckets_of(offset)
        ).astype(f32).astype(bf16)
        vec_ref[...] = mm(table.astype(bf16), onehot)
        x = xperm_ref[...].astype(f32)
        normed_ref[...] = (x * inverse_rms(x) * gain).astype(bf16)

    low_half = lax.broadcasted_iota(jnp.int32, (tokens, LANES), 1) < HEAD_DIM
    left, right, vals = {}, {}, []
    for sub in range(ABREAST):
        cols = slice(sub * BLOCK, (sub + 1) * BLOCK)
        qkv = mm(normed_ref[:, :half], own_ref[:, cols]) + mm(normed_ref[:, half:], oth_ref[:, cols])
        query = (qkv[:, :LANES].astype(bf16) * HEAD_DIM ** (-0.5)).astype(bf16)
        keys = qkv[:, LANES : 2 * LANES].astype(bf16)
        vals.append(qkv[:, 2 * LANES :].astype(bf16))
        at = sub * BLOCK
        qkv_ref[:, at : at + LANES] = query
        qkv_ref[:, at + LANES : at + 2 * LANES] = keys
        qkv_ref[:, at + 2 * LANES : at + BLOCK] = vals[sub]
        for k in range(2):
            head = 2 * sub + k
            keep = low_half if k == 0 else jnp.logical_not(low_half)
            score_ref[head] = mm_nt(jnp.where(keep, query, jnp.zeros_like(query)), keys)
            row = vec_ref[pl.ds(pair * 2 * ABREAST + head, 1), :]
            left[head] = row[:, 0:1]
            right[head] = row[:, 510:511]
            rolled = pltpu.roll(
                jnp.broadcast_to(row, (LANES, 4 * LANES)), 3 * LANES + 1, 1, stride=1, stride_axis=0
            )
            strip_ref[head] = rolled[:, : 3 * LANES]
    for sub in range(ABREAST):
        for i in range(blocks):
            rows = slice(i * LANES, (i + 1) * LANES)
            same = segcol_ref[rows, 0:1] == segrow_ref[0:1, :]
            for head in (2 * sub, 2 * sub + 1):
                bias = []
                for j in range(blocks):
                    if j < i - 1:
                        bias.append(jnp.broadcast_to(left[head], (LANES, LANES)))
                    elif j > i + 1:
                        bias.append(jnp.broadcast_to(right[head], (LANES, LANES)))
                    else:
                        at = (j - i + 1) * LANES
                        bias.append(strip_ref[head, :, at : at + LANES])
                scores = score_ref[head, rows, :] + jnp.concatenate(bias, axis=1)
                scores = jnp.where(same, scores, -1000000000.0)
                top = jnp.max(scores, axis=-1, keepdims=True)
                weights = jnp.exp(scores - top)
                total = jnp.sum(weights, axis=-1, keepdims=True)
                probs_ref[head, rows, :] = (weights * (1.0 / total)).astype(bf16)
        mixed = [mm(probs_ref[2 * sub + k], vals[sub]) for k in range(2)]
        at = pl.multiple_of((pair * ABREAST + sub) * LANES, LANES)
        mixed_ref[:, pl.ds(at, LANES)] = jnp.where(low_half, mixed[0], mixed[1]).astype(bf16)


def after_kernel(
    experts, mixed_ref, perm_get, own_ref, oth_ref, x_get, dm_get,
    after_out, low_out, send_out, gain_out, mixed_out,
    stage,
):
    half = own_ref.shape[0]
    width = mixed_ref.shape[1]
    perm = perm_get()[...]
    mixed = mm(mixed_ref[...], perm).astype(bf16)
    mixed_out.ref[...] = mixed
    mixed_out.send()
    block = width + (experts // LANES) * LANES
    lanes = jnp.transpose(
        jnp.concatenate(
            [own_ref[:, block : block + LANES].astype(f32), oth_ref[:, block : block + LANES].astype(f32)],
            axis=0,
        )
    )
    at = experts % LANES
    gain = mm_nt(jnp.broadcast_to(lanes[at : at + 1, :], (8, width)).astype(bf16), perm)
    gain_out.ref[...] = gain
    gain_out.send()
    after = x_get()[...].astype(f32) + (
        mm(mixed[:, :half], own_ref[:, :width]) + mm(mixed[:, half:], oth_ref[:, :width])
    )
    after_out.ref[...] = after
    after_out.send()
    low = (after * inverse_rms(after) * gain[0:1, :]).astype(bf16)
    low_out.ref[...] = low
    low_out.send()
    to_slab(mm(dm_get()[...], low), stage, send_out.ref)


def between_kernel(
    mixed_get, normed_get, own_ref, oth_ref, perm_get, qkv_get,
    mixed_t_out, normed_t_out, wo_out, router_out, query_t_out,
):
    mixed_t_out.ref[...] = jnp.transpose(mixed_get()[...].astype(f32)).astype(bf16)
    mixed_t_out.send()
    normed_t_out.ref[...] = jnp.transpose(normed_get()[...].astype(f32)).astype(bf16)
    normed_t_out.send()
    half = own_ref.shape[0]
    perm = perm_get()[...]
    rest = (mm(perm[:, :half], own_ref[...]) + mm(perm[:, half:], oth_ref[...])).astype(bf16)
    width = wo_out.ref.shape[1]
    wo_out.ref[...] = rest[:, :width]
    router_out.ref[...] = rest[:, width:]
    wo_out.send()
    qkv_ref = qkv_get()
    for c in range(PAIRS):
        query = qkv_ref[:, c * BLOCK : c * BLOCK + LANES].astype(f32)
        query_t_out.ref[c * LANES : (c + 1) * LANES, :] = jnp.transpose(query).astype(bf16)


def early_expert_kernel(recv_ref, win_ref, wout_ref, cot_ref, win_low_ref, wout_low_ref, g_ref, stage):
    slots = cot_ref.shape[0]

    @pl.when(pl.program_id(0) == 0)
    def _():
        def put(c, values):
            cot_ref[:, c * LANES : (c + 1) * LANES] = values.astype(bf16)

        from_slab(recv_ref, stage, slots, put)

    win_low_ref[0] = win_ref[0].astype(bf16)
    wout = wout_ref[0].astype(bf16)
    wout_low_ref[...] = wout
    g_ref[0] = mm_nt(cot_ref[...], wout).astype(bf16)


def activate(pre):
    squared = pre * pre
    bent = jnp.tanh(pre * (gelu_coef + (gelu_coef * cubic_coef) * squared))
    rise = 0.5 + 0.5 * bent
    value = pre * rise
    slope = rise + (value - value * rise) * (
        2.0 * gelu_coef + (6.0 * gelu_coef * cubic_coef) * squared
    )
    return value, slope


def expert_kernel(
    experts, steps,
    me_ref, recv_ref, router_hbm, cot_hbm, win_hbm, wout_hbm, g_hbm,
    back_hbm, made_hbm, x_hbm, rows_hbm, glog_hbm, gate_hbm,
    stage, router_ref, cot_ref, win_ref, wout_ref, g_ref, hidden_ref, act_ref,
    back_ref, made_ref, x_ref, rows_ref, glog_ref, gate_ref, in_sems, out_sems,
):
    slots, width = x_ref.shape
    units = win_ref.shape[1] // steps
    parts = [slice(i * units, (i + 1) * units) for i in range(steps)]
    fetch = [(router_hbm, router_ref), (cot_hbm, cot_ref)]
    fetch += [(win_hbm.at[i], win_ref.at[:, p]) for i, p in enumerate(parts)]
    fetch += [(g_hbm.at[i], g_ref.at[:, p]) for i, p in enumerate(parts)]
    fetch += [(wout_hbm.at[p, :], wout_ref.at[p, :]) for p in parts]
    copies = [pltpu.make_async_copy(a, b, in_sems.at[i]) for i, (a, b) in enumerate(fetch)]
    stores = [
        pltpu.make_async_copy(a, b, out_sems.at[i])
        for i, (a, b) in enumerate(
            (
                (back_ref, back_hbm), (made_ref, made_hbm), (x_ref, x_hbm),
                (rows_ref, rows_hbm), (glog_ref, glog_hbm), (gate_ref, gate_hbm),
            )
        )
    ]
    sequence = [0, 2, 2 + steps, 3, 3 + steps]
    for i in sequence:
        copies[i].start()

    def put(c, values):
        x_ref[:, c * LANES : (c + 1) * LANES] = values.astype(bf16)

    from_slab(recv_ref, stage, slots, put)
    stores[2].start()
    copies[0].wait()
    router = router_ref[...]
    wide = router.shape[1]
    logits = mm(x_ref[...], router)
    for step, part in enumerate(parts):
        if step + 2 < steps:
            copies[4 + step].start()
            copies[4 + step + steps].start()
        else:
            for i in range(steps // 2):
                copies[2 + 2 * steps + (step + 2 - steps) * (steps // 2) + i].start()
        if step == steps - 1:
            copies[1].start()
        copies[2 + step].wait()
        copies[2 + step + steps].wait()
        value, slope = activate(mm(x_ref[...], win_ref[:, part]))
        hidden_ref[:, part] = value.astype(bf16)
        act_ref[:, part] = (g_ref[:, part].astype(f32) * slope).astype(bf16)
    for step in range(steps):
        copies[2 + 2 * steps + step].wait()
    produced = mm(hidden_ref[...], wout_ref[...]).astype(bf16)
    made_ref[...] = produced
    stores[1].start()
    lane = lax.broadcasted_iota(jnp.int32, (slots, wide), 1)
    logits = jnp.where(lane < experts, logits, -jnp.inf)
    weights = jnp.exp(logits - jnp.max(logits, axis=-1, keepdims=True))
    probs = weights / jnp.sum(weights, axis=-1, keepdims=True)
    own = (lane == me_ref[0]).astype(f32)
    gate = jnp.sum(probs * own, axis=-1, keepdims=True)
    gate_ref[...] = jnp.broadcast_to(gate, (slots, LANES))
    stores[5].start()
    copies[1].wait()
    cot = cot_ref[...].astype(f32)
    rows_ref[...] = (gate * cot).astype(bf16)
    stores[3].start()
    grad_gate = jnp.sum(cot * produced.astype(f32), axis=-1, keepdims=True)
    grad_logits = (probs * (own - gate) * grad_gate).astype(bf16)
    glog_ref[...] = grad_logits
    stores[4].start()
    back = (gate * mm_nt(act_ref[...], win_ref[...])).astype(bf16).astype(f32)
    to_slab(back + mm_nt(grad_logits, router), stage, back_ref)
    stores[0].start()
    for copy in stores:
        copy.wait()


def expert_weights_kernel(
    x_ref, rows_ref, glog_ref, gate_ref, made_ref, perm_ref, win_ref, g_ref,
    gin_ref, gout_ref, grouter_ref, prod_ref,
    xt, stage,
):
    @pl.when(pl.program_id(0) == 0)
    def _():
        to_slab(made_ref[...].astype(f32), stage, prod_ref)
        x = x_ref[...]
        xt[...] = jnp.transpose(gate_ref[:, 0:1] * x.astype(f32)).astype(bf16)
        moved = mm(x, perm_ref[...]).astype(bf16)
        grouter_ref[...] = mm_tn(moved, glog_ref[...])

    value, slope = activate(mm(x_ref[...], win_ref[0]))
    act = (g_ref[0].astype(f32) * slope).astype(bf16)
    gout_ref[0] = mm_tn(value.astype(bf16), rows_ref[...])
    gin_ref[0] = mm(xt[...], act)


def output_kernel(experts, recv_ref, dt_get, low_get, router_get, routes_get, after_get, out_out, stage, rows):
    def put(c, values):
        rows[:, c * LANES : (c + 1) * LANES] = values.astype(bf16)

    dt = dt_get()[...]
    from_slab(recv_ref, stage, dt.shape[1], put)
    produced = mm(dt, rows[...])
    logits = mm(low_get()[...], router_get()[...])
    lane = lax.broadcasted_iota(jnp.int32, logits.shape, 1)
    logits = jnp.where(lane < experts, logits, -jnp.inf)
    weights = jnp.exp(logits - jnp.max(logits, axis=-1, keepdims=True))
    own = (lane == routes_get()[...]).astype(f32)
    gate = jnp.sum(weights * own, axis=-1, keepdims=True) / jnp.sum(weights, axis=-1, keepdims=True)
    out_out.ref[...] = (after_get()[...] + gate * produced).astype(bf16)


def norm_two_kernel(
    experts,
    recv_ref, dt_get, after_get, gain_get, cot_get, wo_get, mixed_t_get, perm_get, grouter_get,
    grad_after_out, grad_mixed_ref, keep_ref, send_ref,
    stage, rows,
):
    def put(c, values):
        rows[:, c * LANES : (c + 1) * LANES] = values.astype(bf16)

    slots = recv_ref.shape[0] * LANES // grad_mixed_ref.shape[1]
    from_slab(recv_ref, stage, slots, put)
    grad = mm(dt_get()[...], rows[...])
    after = after_get()[...]
    inverse = inverse_rms(after)
    unit = after * inverse
    scaled = grad * gain_get()[0:1, :]
    back = inverse * (scaled - unit * jnp.mean(scaled * unit, axis=-1, keepdims=True))
    grad_after = cot_get()[...].astype(f32) + back
    grad_after_out.ref[...] = grad_after
    grad_after_out.send()
    low = grad_after.astype(bf16)
    grad_mixed_ref[...] = mm_nt(low, wo_get()[...]).astype(bf16)
    half = keep_ref.shape[0]
    width = low.shape[1]
    mixed_t_ref = mixed_t_get()
    keep_ref[:, :width] = mm(mixed_t_ref[:half, :], low)
    send_ref[:, :width] = mm(mixed_t_ref[half:, :], low).astype(bf16)
    gain_row = jnp.sum(grad * unit, axis=0, keepdims=True)
    high, rest = split_two(jnp.broadcast_to(gain_row, (8, width)))
    perm = perm_get()[...]
    gain_row = (mm(high, perm) + mm(rest, perm))[0:1, :]
    grouter = grouter_get()[...]
    lane = lax.broadcasted_iota(jnp.int32, grouter.shape, 1)
    packed = jnp.where(
        lane < experts, grouter, jnp.where(lane == experts, to_column(gain_row, grouter.shape[1]), 0.0)
    )
    keep_ref[:, width:] = packed[:half]
    send_ref[:, width:] = packed[half:].astype(bf16)


def unskew(skewed):
    span = 4 * LANES
    total = None
    for g in range(LANES // 8):
        moved = pltpu.roll(skewed[8 * g : 8 * g + 8, :], (LANES - 1 - 8 * g) % span, 1)
        total = moved if total is None else total + moved
    turned = jnp.concatenate([total[7 - s : 8 - s, :] for s in range(8)], axis=0)
    turned = pltpu.roll(turned, span - 7, 1, stride=1, stride_axis=0)
    return jnp.sum(turned, axis=0, keepdims=True)


def attend_backward_kernel(
    before, last, qkv_ref, query_t_ref, probs_ref, gm_ref, normed_t_ref, *refs
):
    refs = list(refs)
    vec_in = refs.pop(0) if before else None
    if last:
        hmask_ref, umask_ref = refs.pop(0), refs.pop(0)
    keep_ref, send_ref, dvec_ref, dq_ref, dkv_ref, dp_ref, ds_ref = refs
    pairs_before = 0 if vec_in is None else vec_in.shape[0] // 2
    pair = pl.program_id(0)
    tokens = qkv_ref.shape[0]
    blocks = tokens // LANES
    low_half = lax.broadcasted_iota(jnp.int32, (tokens, LANES), 1) < HEAD_DIM
    lane = lax.broadcasted_iota(jnp.int32, (1, 4 * LANES), 1)
    keys, vals = (qkv_ref[:, k * LANES : (k + 1) * LANES] for k in (1, 2))
    grad = gm_ref[:, pl.ds(pl.multiple_of((pair + pairs_before) * LANES, LANES), LANES)]
    grad_t = jnp.transpose(grad.astype(f32)).astype(bf16)
    dq = []
    for k in range(2):
        keep = low_half if k == 0 else jnp.logical_not(low_half)
        dp_ref[k] = mm_nt(jnp.where(keep, grad, jnp.zeros_like(grad)), vals)
    for k in range(2):
        strip = [None] * 3
        far_left = far_right = None
        for i in range(blocks):
            rows = slice(i * LANES, (i + 1) * LANES)
            dp = dp_ref[k, rows, :]
            probs = probs_ref[k, rows, :].astype(f32)
            delta = jnp.sum(probs * dp, axis=-1, keepdims=True)
            ds = (probs * (dp - delta)).astype(bf16)
            ds_ref[k, rows, :] = ds
            wide = ds.astype(f32)
            for j in range(blocks):
                piece = wide[:, j * LANES : (j + 1) * LANES]
                if j < i - 1:
                    far_left = piece if far_left is None else far_left + piece
                elif j > i + 1:
                    far_right = piece if far_right is None else far_right + piece
                else:
                    at = j - i + 1
                    strip[at] = piece if strip[at] is None else strip[at] + piece
        part = slice(k * HEAD_DIM, (k + 1) * HEAD_DIM)
        dq.append(mm(ds_ref[k], keys))
        dkv_ref[part, :] = mm(query_t_ref[part, :], ds_ref[k]).astype(bf16)
        low_part = slice(LANES + k * HEAD_DIM, LANES + (k + 1) * HEAD_DIM)
        dkv_ref[low_part, :] = mm(grad_t[part, :], probs_ref[k]).astype(bf16)
        vec = unskew(jnp.concatenate(strip + [jnp.zeros((LANES, LANES), f32)], axis=1))
        left = jnp.sum(jnp.sum(far_left, axis=0, keepdims=True), axis=1, keepdims=True)
        right = jnp.sum(jnp.sum(far_right, axis=0, keepdims=True), axis=1, keepdims=True)
        vec = vec + jnp.where(lane == 0, left, 0.0) + jnp.where(lane == 510, right, 0.0)
        dvec_ref[pl.ds((pair + pairs_before) * 2 + k, 1), :] = vec
    dq_ref[...] = (jnp.where(low_half, dq[0], dq[1]) * HEAD_DIM ** (-0.5)).astype(bf16)
    half = keep_ref.shape[0]
    start = pl.multiple_of(pair * BLOCK, LANES)
    queries, rest = pl.ds(start, LANES), pl.ds(start + LANES, 2 * LANES)
    send_ref[:, queries] = mm(normed_t_ref[half:, :], dq_ref[...]).astype(bf16)
    send_ref[:, rest] = mm_nt(normed_t_ref[half:, :], dkv_ref[...]).astype(bf16)
    keep_ref[:, queries] = mm(normed_t_ref[:half, :], dq_ref[...])
    keep_ref[:, rest] = mm_nt(normed_t_ref[:half, :], dkv_ref[...])

    if vec_in is not None:

        @pl.when(pair == 0)
        def _():
            dvec_ref[: 2 * pairs_before, :] = vec_in[...]

    if not last:
        return

    @pl.when(pair == pl.num_programs(0) - 1)
    def _():
        table_col = table_column(
            jnp.concatenate([dvec_ref[...], jnp.zeros((16 - HEADS, 4 * LANES), f32)], axis=0),
            hmask_ref,
            umask_ref,
        )
        lane = lax.broadcasted_iota(jnp.int32, (2 * half, LANES), 1)
        packed = jnp.where(lane == 0, table_col, 0.0)
        end = keep_ref.shape[1] - LANES
        keep_ref[:, end:] = packed[:half]
        send_ref[:, end:] = packed[half:].astype(bf16)


def split_three(values):
    one, rest = split_two(values)
    two, three = split_two(values - one.astype(f32))
    return one, two, three


def table_column(vec, hmask_ref, umask_ref):
    offset = lax.broadcasted_iota(jnp.int32, (LANES, 4 * LANES), 1) - 255
    onehot = (
        lax.broadcasted_iota(jnp.int32, (LANES, 4 * LANES), 0) == buckets_of(offset)
    ).astype(f32).astype(bf16)
    one, two, three = split_three(vec)
    table = mm_nt(one, onehot) + (mm_nt(two, onehot) + mm_nt(three, onehot))
    heads = hmask_ref[:, :16]
    one, two, three = split_three(table)
    spread = mm(heads, one) + (mm(heads, two) + mm(heads, three))
    return jnp.sum(spread * umask_ref[...].astype(f32), axis=1, keepdims=True)


def last_kernel(own_get, oth_get, xperm_get, gain_get, perm_get, after_get, *refs):
    *gets, out_out, grads_ref = refs
    runs = len(gets) // 2
    at = 0
    for dq_get, dkv_get in zip(gets[:runs], gets[runs:]):
        dq, dkv_t = dq_get()[...], dkv_get()
        for c in range(dq.shape[1] // LANES):
            grads_ref[:, at : at + LANES] = dq[:, c * LANES : (c + 1) * LANES]
            moved = jnp.transpose(dkv_t[2 * c * LANES : 2 * (c + 1) * LANES, :].astype(f32))
            grads_ref[:, at + LANES : at + BLOCK] = moved.astype(bf16)
            at += BLOCK
    grads = grads_ref[...]
    cols = slice(0, at)
    grad = jnp.concatenate(
        [mm_nt(grads, own_get()[:, cols]), mm_nt(grads, oth_get()[:, cols])], axis=1
    )
    x = xperm_get()[...].astype(f32)
    inverse = inverse_rms(x)
    unit = x * inverse
    scaled = grad * gain_get()[0:1, :]
    back = inverse * (scaled - unit * jnp.mean(scaled * unit, axis=-1, keepdims=True))
    high, rest = split_two(back)
    perm = perm_get()[...]
    out_out.ref[...] = (after_get()[...] + (mm_nt(high, perm) + mm_nt(rest, perm))).astype(bf16)


def fold_kernel(plan, *refs):
    refs = list(refs)
    total_in = sum(1 + n for members, _ in plan for n in members)
    ins, outs = refs[:total_in], refs[total_in:]
    for members, parts in plan:
        outs_here = [outs.pop(0) for _ in range(parts)]
        at = 0
        for arrived in members:
            total = ins.pop(0)[...]
            for _ in range(arrived):
                total = total + ins.pop(0)[...].astype(f32)
            rows = total.shape[0] // parts
            cols = slice(at, at + total.shape[1])
            at += total.shape[1]
            for m, out in enumerate(outs_here):
                out[:, cols] = total[m * rows : (m + 1) * rows].astype(out.dtype)


def summed(first_ref, moved):
    total = first_ref[...]
    for piece in moved:
        total = total + piece[...].astype(f32)
    return total


def as_row(column):
    size = column.shape[0]
    same = lax.broadcasted_iota(jnp.int32, (size, size), 0) == lax.broadcasted_iota(
        jnp.int32, (size, size), 1
    )
    return jnp.sum(jnp.where(same, column, 0.0), axis=0, keepdims=True)


def finish_kernel(moved_group, gain_get, wq_get, wk_get, wv_get, first_group, first_last, *refs):
    *moved, wo_out, router_out, gain_two_out, wq_out, wk_out, wv_out, gain_out, table_out = refs
    total = summed(first_group, moved[:moved_group])
    width, experts = wo_out.ref.shape[1], router_out.ref.shape[1]
    wo_out.ref[...] = total[:, :width]
    wo_out.send()
    router_out.ref[...] = total[:, width : width + experts]
    gain_two_out.ref[...] = as_row(total[:, width + experts : width + experts + 1])
    early = RUNS[1]
    sources = [(total, total.shape[1] - early * BLOCK)]
    total = summed(first_last, moved[moved_group:])
    sources.append((total, -early * BLOCK))
    for c in range(PAIRS):
        source, base = sources[c >= early]
        for k, out in enumerate((wq_out, wk_out, wv_out)):
            at = base + c * BLOCK + k * LANES
            out.ref[:, c * LANES : (c + 1) * LANES] = source[:, at : at + LANES]
    for out in (wq_out, wk_out, wv_out):
        out.send()
    products = None
    for get, out in ((wq_get, wq_out), (wk_get, wk_out), (wv_get, wv_out)):
        part = get()[...].astype(bf16).astype(f32) * out.ref[...]
        products = part if products is None else products + part
    gain = gain_get()[...].astype(bf16).astype(f32)
    gain_out.ref[...] = as_row(jnp.sum(products, axis=1, keepdims=True)) / gain
    at = total.shape[1] - LANES
    entries = table_out.ref.shape[1]
    table_out.ref[...] = as_row(total[:, at : at + 1])[:, :entries]


def join_kernel(*refs):
    *pieces, out_ref, sems = refs
    rows = pieces[0].shape[0]
    copies = [
        pltpu.make_async_copy(p, out_ref.at[pl.ds(i * rows, rows), :], sems.at[i])
        for i, p in enumerate(pieces)
    ]
    for copy in copies:
        copy.start()
    for copy in copies:
        copy.wait()


def join(values, moved, space):
    pieces = [values, *moved]
    if values.shape[0] % 8:
        return jnp.concatenate(pieces, axis=0)
    shape = (len(pieces) * values.shape[0], values.shape[1])
    any_ref = pl.BlockSpec(memory_space=pl.ANY)
    return pl.pallas_call(
        join_kernel,
        out_shape=space(shape, values.dtype),
        in_specs=[any_ref] * len(pieces),
        out_specs=any_ref,
        scratch_shapes=[pltpu.SemaphoreType.DMA((len(pieces),))],
        **parameters(4, 1),
    )(*pieces)


def assemble_kernel(moves, count, *refs):
    sources, outs, sems = refs[:count], refs[count:-1], refs[-1]
    copies = []
    for i, (source, row, rows, col, cols, out, to_row, to_col) in enumerate(moves):
        copies.append(
            pltpu.make_async_copy(
                sources[source].at[pl.ds(row, rows), pl.ds(col, cols)],
                outs[out].at[pl.ds(to_row, rows), pl.ds(to_col, cols)],
                sems.at[i],
            )
        )
    for copy in copies:
        copy.start()
    for copy in copies:
        copy.wait()


def assemble(arrays, outs, moves):
    if any(m[i] % 8 for m in moves for i in (1, 2, 6)):
        made = [jnp.zeros(o.shape, o.dtype) for o in outs]
        for a, row, rows, col, cols, out, to_row, to_col in moves:
            block = arrays[a][row : row + rows, col : col + cols]
            made[out] = lax.dynamic_update_slice(made[out], block, (to_row, to_col))
        return made
    any_ref = pl.BlockSpec(memory_space=pl.ANY)
    return pl.pallas_call(
        functools.partial(assemble_kernel, moves, len(arrays)),
        out_shape=list(outs),
        in_specs=[any_ref] * len(arrays),
        out_specs=[any_ref] * len(outs),
        scratch_shapes=[pltpu.SemaphoreType.DMA((len(moves),))],
        **parameters(4, 1),
    )(*arrays)


def expert_call(experts, steps, slots, width, units, wide):
    slab = (slots * width // LANES, LANES)
    any_ref, vmem_ref = (pl.BlockSpec(memory_space=m) for m in (pl.ANY, pltpu.VMEM))
    outs = [slab, (slots, width), (slots, width), (slots, width), (slots, wide)]
    call = pl.pallas_call(
        functools.partial(expert_kernel, experts, steps),
        out_shape=[far(shape, bf16) for shape in outs] + [far((slots, LANES), f32)],
        in_specs=[pl.BlockSpec(memory_space=pltpu.SMEM), vmem_ref] + [any_ref] * 5,
        out_specs=[any_ref] * 6,
        scratch_shapes=[pltpu.VMEM(slab, f32)]
        + [
            pltpu.VMEM(shape, bf16)
            for shape in (
                (width, wide), (slots, width), (width, units), (units, width),
                (slots, units), (slots, units), (slots, units),
            )
        ]
        + [pltpu.VMEM(shape, bf16) for shape in outs]
        + [
            pltpu.VMEM((slots, LANES), f32),
            pltpu.SemaphoreType.DMA((2 + 3 * steps,)),
            pltpu.SemaphoreType.DMA((6,)),
        ],
        **parameters(52, 18),
    )
    return lambda me, recv, *rest: call(me, recv, *[place(Far(a)) for a in rest])


def shards(
    count,
    inputs,
    segment_ids,
    routes,
    cotangent,
    gain_attn,
    gain_ffn,
    bias_table,
    w_query,
    w_key,
    w_value,
    w_output,
    w_router,
    w_in,
    w_out,
):
    tokens, width = inputs.shape
    experts = w_router.shape[1]
    rows_local = w_query.shape[0]
    entries = bias_table.shape[0]
    hidden_units = w_in.shape[2]
    capacity = max(2, 5 * tokens // (4 * experts))
    slots = experts * capacity
    blocks = width // LANES
    half = width // 2
    wide = -(-(experts + 1) // LANES) * LANES
    me = lax.axis_index("seq").astype(jnp.int32).reshape(1)
    vmem = pl.BlockSpec(memory_space=pltpu.VMEM)

    groups = bit_groups(count)
    levels = list(reversed(groups[1:]))
    columns = PAIRS * BLOCK
    piece, tail = flat_call(
        functools.partial(pack_kernel, experts),
        [near((rows_local, columns + LANES), bf16), near((rows_local, width + wide), bf16)],
        us=1,
    )(
        *map(Far, (gain_attn[None, :], gain_ffn[None, :], bias_table[None, :])),
        *map(Far, (w_query, w_key, w_value, w_output, w_router)),
    )

    def reach(values, low_bit, bits):
        return [swap(values, m << low_bit, count) for m in range(1, 1 << bits)]

    order = np.asarray(relative_order(count), np.int32)
    rel_row = jnp.asarray(np.repeat(order, rows_local)[None, :])
    off_row = jnp.asarray(np.tile(np.arange(rows_local, dtype=np.int32), count)[None, :])
    slab = (slots * blocks, LANES)
    slab_stage = pltpu.VMEM(slab, f32)
    perm, xperm, segrow, segcol, hmask, umask, dt, dm = flat_call(
        functools.partial(prepare_kernel, rows_local, entries, experts, capacity),
        [
            far((width, width), bf16),
            far((tokens, width), bf16),
            far((8, tokens), f32),
            far((tokens, LANES), f32),
            far((width, LANES), bf16),
            far((width, LANES), bf16),
            far((tokens, slots), bf16),
            far((slots, tokens), bf16),
        ],
        us=8,
    )(me, Far(rel_row), Far(off_row), Far(inputs), Far(segment_ids), Far(routes))
    cot_send = flat_call(dispatch_kernel, [far(slab, bf16)], us=3, scratch=[slab_stage])(
        Far(dm), Far(cotangent)
    )[0]

    moved = reach(piece, *levels[0])
    moved = lax.optimization_barrier((*moved, perm))[:-1]
    total = columns + LANES
    sizes = (columns // 2, total - columns // 2)
    starts = (0, sizes[0])
    rows = rows_local
    pieces = [piece, *moved]
    moves = [
        (i, 0, rows, starts[p], sizes[p], p, i * rows, 0) for i in range(len(pieces)) for p in range(2)
    ]
    rows *= len(pieces)
    parts = assemble(pieces, [near((rows, size), bf16) for size in sizes], moves)
    for k, (low_bit, _) in enumerate(levels[1:]):
        steps_of = ((2 << low_bit, 1 << low_bit), (1 << low_bit, 2 << low_bit))
        got = [swap(part, d[0], count) for part, d in zip(parts, steps_of)]
        tail_moved = reach(after(tail, *parts, cot_send), *levels[k])
        got = lax.optimization_barrier((*got, cot_send))[:-1]
        moves = [(p + 2 * i, 0, rows, 0, sizes[p], p, i * rows, 0) for i in range(2) for p in range(2)]
        parts = assemble(
            [*parts, *got], [near((2 * rows, size), bf16) for size in sizes], moves
        )
        got = [swap(part, d[1], count) for part, d in zip(parts, steps_of)]
        got = lax.optimization_barrier((*got, *tail_moved))[:2]
        tail = join(tail, tail_moved, near)
        final = k == len(levels) - 2
        order_of = (((0, 2), (1, 3)), ((0, 1), (2, 3)))
        moves = [
            (p + 2 * i, b * rows, rows, 0, sizes[p], 0 if final else p, order_of[p][i][b] * rows,
             starts[p] if final else 0)
            for i in range(2) for p in range(2) for b in range(2)
        ]
        outs = [far((4 * rows, total), bf16)] if final else [near((4 * rows, size), bf16) for size in sizes]
        parts = assemble([*parts, *got], outs, moves)
        rows *= 4
    piece = parts[0]
    other = swap(piece, 1, count)
    tail_moved = reach(after(tail, piece), *levels[-1])

    slab_split = (count, slots * blocks // count, LANES)

    def exchange(rows):
        return lax.all_to_all(
            rows.reshape(slab_split), "seq", split_axis=0, concat_axis=0, tiled=True
        ).reshape(slab)

    cot_recv = exchange(after(cot_send, other))

    def whole(shape):
        return pl.BlockSpec(shape, lambda i: (0,) * len(shape))

    pair_probs = pl.BlockSpec((2 * ABREAST, tokens, tokens), lambda i: (i, 0, 0))
    piece, other = Far(piece), Far(other)
    small_block = pl.BlockSpec((half, LANES), lambda i: (0, columns // LANES))
    pair_weights = pl.BlockSpec((half, ABREAST * BLOCK), lambda i: (0, i))
    qkv, probs, mixed, normed, gain_one = grid_call(
        attend_forward_kernel,
        [
            far((tokens, PAIRS * BLOCK), bf16),
            far((HEADS, tokens, tokens), bf16),
            near((tokens, width), bf16),
            far((tokens, width), bf16),
            far((8, width), f32),
        ],
        grid=(PAIRS // ABREAST,),
        in_specs=[whole((tokens, width))]
        + [pair_weights, pair_weights, small_block, small_block]
        + [whole(shape) for shape in ((width, LANES), (width, LANES), (8, tokens), (tokens, LANES))],
        out_specs=[
            pl.BlockSpec((tokens, ABREAST * BLOCK), lambda i: (0, i)),
            pair_probs,
            vmem,
            whole((tokens, width)),
            whole((8, width)),
        ],
        scratch=[
            pltpu.VMEM((16, 4 * LANES), f32),
            pltpu.VMEM((2 * ABREAST, tokens, tokens), f32),
            pltpu.VMEM((2 * ABREAST, LANES, 3 * LANES), f32),
        ],
        us=14,
    )(
        Far(after(xperm, tail)), piece, other, piece, other,
        *map(Far, (hmask, umask, segrow, segcol)),
    )
    tail_moved = lax.optimization_barrier((*tail_moved, mixed))[:-1]
    tail = join(tail, tail_moved, near)
    tail_other = swap(tail, 1, count)

    after_rows, low_two, row_send, gain_two, mixed_perm = flat_call(
        functools.partial(after_kernel, experts),
        [
            far((tokens, width), f32),
            far((tokens, width), bf16),
            far(slab, bf16),
            far((8, width), f32),
            far((tokens, width), bf16),
        ],
        us=6,
        scratch=[slab_stage],
    )(mixed, Far(perm), tail, tail_other, Far(inputs), Far(dm))
    row_recv = exchange(row_send)

    steps = 6
    units = hidden_units // steps
    weight_in = pl.BlockSpec((1, width, units), lambda i: (0, 0, i))
    weight_out = pl.BlockSpec((1, units, width), lambda i: (0, i, 0))

    low_in = pl.BlockSpec((1, width, units), lambda i: (i, 0, 0))
    low_out = pl.BlockSpec((units, width), lambda i: (i, 0))
    slot_units = pl.BlockSpec((1, slots, units), lambda i: (i, 0, 0))
    cot_rows, win_low, wout_low, grad_hidden = grid_call(
        early_expert_kernel,
        [
            far((slots, width), bf16),
            far((steps, width, units), bf16),
            far((hidden_units, width), bf16),
            far((steps, slots, units), bf16),
        ],
        grid=(steps,),
        in_specs=[whole(slab), weight_in, weight_out],
        out_specs=[whole((slots, width)), low_in, low_out, slot_units],
        us=13,
        scratch=[slab_stage],
    )(cot_recv, Far(w_in), Far(w_out))
    mixed_t, normed_t, output_w, router_w, query_t = flat_call(
        between_kernel,
        [
            far((width, tokens), bf16),
            far((width, tokens), bf16),
            far((width, width), bf16),
            far((width, wide), bf16),
            far((width, tokens), bf16),
        ],
        us=7,
    )(Far(mixed_perm), Far(normed), tail, tail_other, Far(perm), Far(qkv))
    back_send, made, x_rows, grad_rows, grad_logits, gates = expert_call(
        experts, steps, slots, width, hidden_units, wide
    )(me, row_recv, router_w, cot_rows, win_low, wout_low, grad_hidden)
    back_recv = exchange(back_send)
    grad_inner, grad_outer, grad_router, prod_send = grid_call(
        expert_weights_kernel,
        [
            far((1, width, hidden_units), f32),
            far((1, hidden_units, width), f32),
            far((width, wide), f32),
            far(slab, bf16),
        ],
        grid=(steps,),
        in_specs=[
            whole((slots, width)),
            whole((slots, width)),
            whole((slots, wide)),
            whole((slots, LANES)),
            whole((slots, width)),
            whole((width, width)),
            low_in,
            slot_units,
        ],
        out_specs=[weight_in, weight_out, whole((width, wide)), whole(slab)],
        us=19,
        scratch=[pltpu.VMEM((width, slots), bf16), slab_stage],
    )(*map(Far, (x_rows, grad_rows, grad_logits, gates, made, perm, win_low, grad_hidden)))
    prod_recv = exchange(prod_send)

    row_scratch = pltpu.VMEM((slots, width), bf16)
    grad_after, grad_mixed, keep_o, send_o = flat_call(
        functools.partial(norm_two_kernel, experts),
        [
            far((tokens, width), f32),
            near((tokens, width), bf16),
            near((half, width + wide), f32),
            near((half, width + wide), bf16),
        ],
        us=1,
        scratch=[slab_stage, row_scratch],
    )(
        back_recv,
        *map(Far, (dt, after_rows, gain_two, cotangent, output_w, mixed_t, perm, grad_router)),
    )

    def backward(run, ready):
        start, stop = RUNS[run], RUNS[run + 1]
        last = stop == PAIRS
        vec = before.get("vec")
        here = [Far(qkv), Far(query_t), Far(probs), after(grad_mixed, *ready), Far(normed_t)]
        specs = [
            pl.BlockSpec((tokens, BLOCK), lambda i: (0, i + start)),
            pl.BlockSpec((LANES, tokens), lambda i: (i + start, 0)),
            pl.BlockSpec((2, tokens, tokens), lambda i: (i + start, 0, 0)),
            vmem,
            whole((width, tokens)),
        ]
        if vec is not None:
            here.append(vec)
            specs.append(vmem)
        if last:
            here += [Far(hmask), Far(umask)]
            specs += [whole((width, LANES))] * 2
        pairs = stop - start
        cols = pairs * BLOCK + (LANES if last else 0)
        keep, send, vec, dq, dkv_t = grid_call(
            functools.partial(attend_backward_kernel, vec is not None, last),
            [
                near((half, cols), f32),
                near((half, cols), bf16),
                near((2 * stop, 4 * LANES), f32),
                far((tokens, pairs * LANES), bf16),
                far((2 * pairs * LANES, tokens), bf16),
            ],
            grid=(pairs,),
            in_specs=specs,
            out_specs=[
                vmem,
                vmem,
                vmem,
                pl.BlockSpec((tokens, LANES), lambda i: (0, i)),
                pl.BlockSpec((2 * LANES, tokens), lambda i: (i, 0)),
            ],
            scratch=[
                pltpu.VMEM((2, tokens, tokens), f32),
                pltpu.VMEM((2, tokens, tokens), bf16),
            ],
            us=(1, 4)[run],
            vmem=24,
        )(*here)
        before.update(vec=vec)
        born.append((keep, send))
        grads.append((dq, dkv_t))
        return keep

    def results(ready):
        return flat_call(
            functools.partial(output_kernel, experts),
            [far((tokens, width), bf16)],
            us=0.001,
            scratch=[slab_stage, row_scratch],
            vmem=20,
        )(after(prod_recv, *ready), *map(Far, (dt, low_two, router_w, routes, after_rows)))[0]

    def finish(ready):
        return flat_call(
            last_kernel,
            [far((tokens, width), bf16)],
            us=8,
            scratch=[pltpu.VMEM((tokens, columns), bf16)],
            vmem=32,
        )(
            piece, other, Far(after(xperm, *ready)),
            *map(Far, (gain_one, perm, grad_after)),
            *[Far(g[0]) for g in grads], *[Far(g[1]) for g in grads],
        )[0]

    before, born, grads = {}, [(keep_o, send_o)], []
    ups = groups[1:]
    core = (1, 2)
    first = (1 << ups[0][0], 1 << ups[0][1])
    direct = [(1 << low_bit, 1 << bits) for low_bit, bits in ups[1:]]
    halving = [(1 << (low_bit + b), 2) for low_bit, bits in ups[1:] for b in reversed(range(bits))]
    plans = {c: {c: core, c + 1: first} for c in range(3)}
    plans[2].update({4 + i: step for i, step in enumerate(direct)})
    plans[3] = {3 + i: step for i, step in enumerate(halving)}
    work = {run: [functools.partial(backward, run)] for run in range(2)}
    work.update({2: [finish], 3: [results]})
    own, going, flight, finished = {}, {}, {}, {}
    output = grad_inputs = None
    end = max(max(plan) for plan in plans.values())
    own[0], going[0] = born[0][0], [born[0][1]]
    for slot in range(end + 1):
        for c, plan in plans.items():
            if slot in plan:
                distance, parts = plan[slot]
                flight[c] = [swap(g, (m + 1) * distance, count) for m, g in enumerate(going[c])]
        ready = [own[c] for c in flight] + ([prod_recv] if slot == 2 else [])
        for step in work.get(slot, []):
            value = step(ready)
            ready = [value]
            if step is results:
                output = value
            if step is finish:
                grad_inputs = value
        if slot in work:
            for c in flight:
                flight[c] = list(lax.optimization_barrier((*flight[c], value))[:-1])
        folds, args, outs, cut = [], [], [], []

        def fold(members, following, name):
            parts = following[1]
            folds.append(([len(flight[c]) if c in flight else 0 for c in members], parts))
            rows = own[members[0]].shape[0] // parts
            cols = sum(own[c].shape[1] for c in members)
            for c in members:
                args.append(own[c])
                args.extend(flight.pop(c, []))
            outs.append(near((rows, cols), f32))
            outs.extend([near((rows, cols), bf16)] * (parts - 1))
            cut.append((name, parts))

        if slot == 2:
            fold([0, 1], plans[3][3], 3)
        for c in list(flight):
            following = plans[c].get(slot + 1)
            if following or c < 2:
                fold([c], following or (0, 1), c)
            else:
                finished[c] = [own[c], *flight.pop(c)]
        if folds:
            folded = list(
                flat_call(functools.partial(fold_kernel, folds), outs, us=1, vmem=16)(*args)
            )
            for c, parts in cut:
                own[c] = folded.pop(0)
                going[c] = [folded.pop(0) for _ in range(parts - 1)]
            if len(born) == slot + 2:
                own[slot + 1] = born[-1][0]
                going[slot + 1] = [after(born[-1][1], own[cut[0][0]])]

    def row(size):
        return far((1, size), f32)

    square = far((rows_local, width), f32)
    grad_wo, grad_wr, grad_gain_two, grad_q, grad_k, grad_v, grad_gain_one, grad_table = flat_call(
        functools.partial(finish_kernel, len(finished[3]) - 1),
        [square, far((rows_local, experts), f32), row(rows_local)]
        + [square, square, square, row(rows_local), row(entries)],
        us=2,
        vmem=16,
    )(
        *map(Far, (gain_attn[None, :], w_query, w_key, w_value)),
        finished[3][0], finished[2][0], *finished[3][1:], *finished[2][1:],
    )

    return (
        output,
        grad_inputs,
        grad_gain_one[0],
        grad_gain_two[0],
        grad_table[0],
        grad_q,
        grad_k,
        grad_v,
        grad_wo,
        grad_wr,
        grad_inner,
        grad_outer,
    )


def solution(mesh):
    row, flat, cube = P("seq", None), P("seq"), P("seq", None, None)
    in_specs = (row,) * 4 + (flat,) * 3 + (row,) * 5 + (cube,) * 2
    out_specs = (row,) * 2 + (flat,) * 3 + (row,) * 5 + (cube,) * 2
    return jax.shard_map(
        functools.partial(shards, mesh.shape["seq"]),
        mesh=mesh,
        in_specs=in_specs,
        out_specs=out_specs,
        check_vma=False,
    )
```

```python
import functools

import jax
import jax.numpy as jnp
import numpy as np
from jax import lax
from jax.experimental import pallas as pl
from jax.experimental.pallas import tpu as pltpu
from jax.sharding import PartitionSpec as P

HEADS = 12
HEAD_DIM = 64
BUCKETS = 32
PAIRS = HEADS // 2
RUNS = (0, 4, 6)
ABREAST = 1
LANES = 128
BLOCK = 3 * LANES

epsilon = 1e-06
bucket_edges = (1, 2, 3, 4, 5, 6, 7, 8, 12, 16, 23, 32, 46, 64, 91)
gelu_coef = 0.7978845608028654
cubic_coef = 0.044715

f32 = jnp.float32
bf16 = jnp.bfloat16


def bit_groups(count):
    bits = count.bit_length() - 1
    groups, low = [(0, 1)], 1
    while low < bits:
        width = min(2, bits - low)
        groups.append((low, width))
        low += width
    return groups


def relative_order(count):
    order = [0]
    for low, width in bit_groups(count):
        order = [base + (m << low) for base in order for m in range(1 << width)]
    return order


def swap(values, distance, count):
    return lax.ppermute(values, "seq", [(i, i ^ distance) for i in range(count)])


def after(values, *others):
    return lax.optimization_barrier((values, *others))[0]


def mm(left, right):
    return jnp.dot(left, right, preferred_element_type=f32)


def mm_nt(left, right):
    return lax.dot_general(left, right, (((1,), (1,)), ((), ())), preferred_element_type=f32)


def mm_tn(left, right):
    return lax.dot_general(left, right, (((0,), (0,)), ((), ())), preferred_element_type=f32)


def split_two(values):
    high = values.astype(bf16)
    return high, (values - high.astype(f32)).astype(bf16)


class Far:
    def __init__(self, values, turn=0):
        self.values, self.turn = values, turn


def near(shape, dtype):
    return pltpu.VMEM(shape, dtype)


def far(shape, dtype):
    return pltpu.HBM(shape, dtype)


class Fetched:
    def __init__(self, copy, ref, following=()):
        self.copy, self.ref, self.here, self.following = copy, ref, False, following

    def __call__(self):
        if not self.here:
            self.copy.wait()
            self.here = True
            while self.following:
                self.following.pop().start()
        return self.ref


class Stored:
    def __init__(self, copy, ref):
        self.copy, self.ref, self.sent = copy, ref, False

    def send(self):
        self.copy.start()
        self.sent = True


def place(a):
    if isinstance(a, Far):
        return pltpu.with_memory_space_constraint(a.values, pltpu.HBM)
    return a


def parameters(vmem, us):
    return dict(
        compiler_params=pltpu.CompilerParams(vmem_limit_bytes=vmem * 1024 * 1024),
        cost_estimate=pl.CostEstimate(
            flops=int(us * 10**9), bytes_accessed=int(us * 10**6), transcendentals=0
        ),
    )


def grid_call(body, outs, grid, in_specs, out_specs, us, scratch=(), vmem=40):
    call = pl.pallas_call(
        body,
        out_shape=list(outs),
        grid=grid,
        in_specs=in_specs,
        out_specs=out_specs,
        scratch_shapes=list(scratch),
        **parameters(vmem, us),
    )
    return lambda *args: call(*[place(a) for a in args])


def flat_call(body, outs, us, scratch=(), vmem=32):
    def run(*args):
        lazy = [isinstance(a, Far) for a in args]
        late = [o.memory_space == pltpu.HBM for o in outs]
        values = [a.values if f else a for a, f in zip(args, lazy)]
        n_in, n_out, n_scratch = len(args), len(outs), len(scratch)
        any_ref, vmem_ref, smem_ref = (
            pl.BlockSpec(memory_space=m) for m in (pl.ANY, pltpu.VMEM, pltpu.SMEM)
        )
        in_copies = [pltpu.VMEM(v.shape, v.dtype) for v, f in zip(values, lazy) if f]
        out_copies = [pltpu.VMEM(o.shape, o.dtype) for o, f in zip(outs, late) if f]

        def wrapped(*refs):
            ins, rest = refs[:n_in], refs[n_in:]
            results, rest = rest[:n_out], rest[n_out:]
            own, rest = rest[:n_scratch], rest[n_scratch:]
            fetched, rest = list(rest[: len(in_copies)]), rest[len(in_copies) :]
            stored, rest = list(rest[: len(out_copies)]), rest[len(out_copies) :]
            sems = list(rest)
            given, made = [], []
            turns = {}
            for ref, a, f in zip(ins, args, lazy):
                if f:
                    copy = pltpu.make_async_copy(ref, fetched[0], sems.pop())
                    if a.turn:
                        turns.setdefault(a.turn, []).append(copy)
                    else:
                        copy.start()
                    given.append(Fetched(copy, fetched.pop(0), turns.setdefault(a.turn + 1, [])))
                else:
                    given.append(ref)
            for ref, f in zip(results, late):
                if f:
                    made.append(
                        Stored(pltpu.make_async_copy(stored[0], ref, sems.pop()), stored[0])
                    )
                    stored.pop(0)
                else:
                    made.append(ref)
            body(*given, *made, *own)
            for item in given:
                if isinstance(item, Fetched):
                    item()
            for item in made:
                if isinstance(item, Stored):
                    if not item.sent:
                        item.send()
                    item.copy.wait()

        return pl.pallas_call(
            wrapped,
            out_shape=list(outs),
            in_specs=[
                any_ref if f else (smem_ref if v.size == 1 else vmem_ref)
                for v, f in zip(values, lazy)
            ],
            out_specs=[any_ref if f else vmem_ref for f in late],
            scratch_shapes=list(scratch)
            + in_copies
            + out_copies
            + [pltpu.SemaphoreType.DMA] * (len(in_copies) + len(out_copies)),
            **parameters(vmem, us),
        )(*[place(a) for a in args])

    return run


def to_slab(values, stage, out_ref):
    slots, width = values.shape
    blocks = width // LANES
    for c in range(blocks):
        stage[pl.ds(c, slots, stride=blocks), :] = values[:, c * LANES : (c + 1) * LANES]
    out_ref[...] = stage[...].astype(out_ref.dtype)


def from_slab(in_ref, stage, slots, put):
    stage[...] = in_ref[...].astype(f32)
    blocks = in_ref.shape[0] // slots
    for c in range(blocks):
        put(c, stage[pl.ds(c, slots, stride=blocks), :])


def to_column(row, width=LANES):
    return jnp.transpose(jnp.broadcast_to(row, (width, row.shape[1])))


def inverse_rms(values):
    return lax.rsqrt(jnp.mean(values * values, axis=-1, keepdims=True) + epsilon)


def buckets_of(offset):
    magnitude = jnp.abs(offset)
    bucket = jnp.zeros(offset.shape, jnp.int32)
    for edge in bucket_edges:
        bucket = bucket + (magnitude >= edge).astype(jnp.int32)
    return bucket + BUCKETS // 2 * (offset > 0).astype(jnp.int32)


def prepare_kernel(
    rows_local, entries, experts, capacity,
    me_ref, rel_ref, off_ref, x_get, seg_get, routes_get,
    perm_out, xperm_out, segrow_out, segcol_out, hmask_out, umask_out, dt_out, dm_out,
):
    perm_ref, xperm_ref, segrow_ref, segcol_ref, hmask_ref, umask_ref, dt_ref, dm_ref = (
        out.ref
        for out in (perm_out, xperm_out, segrow_out, segcol_out, hmask_out, umask_out, dt_out, dm_out)
    )
    x_ref, seg_ref, routes_ref = x_get(), seg_get(), routes_get()
    tokens, width = x_ref.shape
    slots = dm_ref.shape[0]
    me = me_ref[0]
    device_row = rel_ref()[...] ^ me
    off_row = off_ref()[...]
    true_row = device_row * rows_local + off_row
    perm = (lax.broadcasted_iota(jnp.int32, (width, width), 0) == true_row).astype(f32).astype(bf16)
    perm_ref[...] = perm
    perm_out.send()
    xperm_ref[...] = mm(x_ref[...], perm).astype(bf16)
    xperm_out.send()
    segments = seg_ref[...].astype(f32)
    segrow_ref[...] = jnp.broadcast_to(segments, segrow_ref.shape)
    segcol_ref[...] = to_column(segments)
    flat = device_row * entries + off_row
    bucket_row = ((flat.astype(f32) + 0.5) * (1.0 / HEADS)).astype(jnp.int32)
    head_row = jnp.where(off_row < entries, flat - bucket_row * HEADS, -1)
    bucket_col = to_column(bucket_row.astype(f32))
    head_col = to_column(head_row.astype(f32))
    lane = lax.broadcasted_iota(jnp.int32, (width, LANES), 1).astype(f32)
    hmask_ref[...] = (head_col == lane).astype(f32).astype(bf16)
    umask_ref[...] = (bucket_col == lane).astype(f32).astype(bf16)
    for out in (segrow_out, segcol_out, hmask_out, umask_out):
        out.send()
    routes = routes_ref[...]
    labels = lax.broadcasted_iota(jnp.int32, (tokens, experts), 1)
    picked = (routes == labels).astype(f32)
    earlier = (
        lax.broadcasted_iota(jnp.int32, (tokens, tokens), 1)
        <= lax.broadcasted_iota(jnp.int32, (tokens, tokens), 0)
    ).astype(f32).astype(bf16)
    counts = mm(earlier, picked.astype(bf16))
    position = jnp.sum(counts * picked, axis=1, keepdims=True) - 1.0
    slot_col = jnp.where(
        position < capacity, routes.astype(f32) * capacity + position, -1.0
    )
    slot_lane = lax.broadcasted_iota(jnp.int32, (tokens, slots), 1).astype(f32)
    dt_ref[...] = (slot_col == slot_lane).astype(f32).astype(bf16)
    dt_out.send()
    slot_row = jnp.transpose(jnp.broadcast_to(slot_col, (tokens, LANES)))[0:1, :]
    slot_sub = lax.broadcasted_iota(jnp.int32, (slots, tokens), 0).astype(f32)
    dm_ref[...] = (slot_sub == slot_row).astype(f32).astype(bf16)


def dispatch_kernel(dm_get, cot_get, send_out, stage):
    to_slab(mm(dm_get()[...], cot_get()[...]), stage, send_out.ref)


def pack_kernel(
    experts, gain_get, gain_two_get, table_get, wq_get, wk_get, wv_get, wo_get, router_get,
    piece, tail,
):
    gain_ref, gain_two_ref, table_ref = gain_get(), gain_two_get(), table_get()
    wq_ref, wk_ref, wv_ref, wo_ref, router_ref = (
        get() for get in (wq_get, wk_get, wv_get, wo_get, router_get)
    )
    rows, width = wq_ref.shape

    def column(ref):
        size = ref.shape[1]
        same = lax.broadcasted_iota(jnp.int32, (rows, size), 0) == lax.broadcasted_iota(
            jnp.int32, (rows, size), 1
        )
        return jnp.sum(jnp.where(same, ref[...], 0.0), axis=1, keepdims=True)

    for c in range(PAIRS):
        for k, w in enumerate((wq_ref, wk_ref, wv_ref)):
            at = c * BLOCK + k * LANES
            piece[:, at : at + LANES] = w[:, c * LANES : (c + 1) * LANES].astype(bf16)
    lane = lax.broadcasted_iota(jnp.int32, (rows, LANES), 1)
    small = jnp.where(lane == 0, column(gain_ref), jnp.where(lane == 1, column(table_ref), 0.0))
    piece[:, PAIRS * BLOCK :] = small.astype(bf16)
    tail[:, :width] = wo_ref[...].astype(bf16)
    lane = lax.broadcasted_iota(jnp.int32, (rows, tail.shape[1] - width), 1)
    tail[:, width:] = jnp.where(lane == experts, column(gain_two_ref), 0.0).astype(bf16)
    tail[:, width : width + experts] = router_ref[...].astype(bf16)


def attend_forward_kernel(
    xperm_ref, own_ref, oth_ref, own_small, oth_small, hmask_ref, umask_ref, segrow_ref, segcol_ref,
    qkv_ref, probs_ref, mixed_ref, normed_ref, gain_ref,
    vec_ref, score_ref, strip_ref,
):
    half = own_ref.shape[0]
    tokens = segcol_ref.shape[0]
    blocks = tokens // LANES
    pair = pl.program_id(0)

    @pl.when(pair == 0)
    def _():
        packed = jnp.concatenate([own_small[...].astype(f32), oth_small[...].astype(f32)], axis=0)
        gain = jnp.transpose(packed)[0:1, :]
        gain_ref[...] = jnp.broadcast_to(gain, gain_ref.shape)
        spread = (packed[:, 1:2] * hmask_ref[...].astype(f32)).astype(bf16)
        table = mm_tn(spread, umask_ref[...])[:16]
        offset = lax.broadcasted_iota(jnp.int32, (LANES, 4 * LANES), 1) - 255
        onehot = (
            lax.broadcasted_iota(jnp.int32, (LANES, 4 * LANES), 0) == buckets_of(offset)
        ).astype(f32).astype(bf16)
        vec_ref[...] = mm(table.astype(bf16), onehot)
        x = xperm_ref[...].astype(f32)
        normed_ref[...] = (x * inverse_rms(x) * gain).astype(bf16)

    low_half = lax.broadcasted_iota(jnp.int32, (tokens, LANES), 1) < HEAD_DIM
    left, right, vals = {}, {}, []
    for sub in range(ABREAST):
        cols = slice(sub * BLOCK, (sub + 1) * BLOCK)
        qkv = mm(normed_ref[:, :half], own_ref[:, cols]) + mm(normed_ref[:, half:], oth_ref[:, cols])
        query = (qkv[:, :LANES].astype(bf16) * HEAD_DIM ** (-0.5)).astype(bf16)
        keys = qkv[:, LANES : 2 * LANES].astype(bf16)
        vals.append(qkv[:, 2 * LANES :].astype(bf16))
        at = sub * BLOCK
        qkv_ref[:, at : at + LANES] = query
        qkv_ref[:, at + LANES : at + 2 * LANES] = keys
        qkv_ref[:, at + 2 * LANES : at + BLOCK] = vals[sub]
        for k in range(2):
            head = 2 * sub + k
            keep = low_half if k == 0 else jnp.logical_not(low_half)
            score_ref[head] = mm_nt(jnp.where(keep, query, jnp.zeros_like(query)), keys)
            row = vec_ref[pl.ds(pair * 2 * ABREAST + head, 1), :]
            left[head] = row[:, 0:1]
            right[head] = row[:, 510:511]
            rolled = pltpu.roll(
                jnp.broadcast_to(row, (LANES, 4 * LANES)), 3 * LANES + 1, 1, stride=1, stride_axis=0
            )
            strip_ref[head] = rolled[:, : 3 * LANES]
    for sub in range(ABREAST):
        for i in range(blocks):
            rows = slice(i * LANES, (i + 1) * LANES)
            same = segcol_ref[rows, 0:1] == segrow_ref[0:1, :]
            for head in (2 * sub, 2 * sub + 1):
                bias = []
                for j in range(blocks):
                    if j < i - 1:
                        bias.append(jnp.broadcast_to(left[head], (LANES, LANES)))
                    elif j > i + 1:
                        bias.append(jnp.broadcast_to(right[head], (LANES, LANES)))
                    else:
                        at = (j - i + 1) * LANES
                        bias.append(strip_ref[head, :, at : at + LANES])
                scores = score_ref[head, rows, :] + jnp.concatenate(bias, axis=1)
                scores = jnp.where(same, scores, -1000000000.0)
                top = jnp.max(scores, axis=-1, keepdims=True)
                weights = jnp.exp(scores - top)
                total = jnp.sum(weights, axis=-1, keepdims=True)
                probs_ref[head, rows, :] = (weights * (1.0 / total)).astype(bf16)
        mixed = [mm(probs_ref[2 * sub + k], vals[sub]) for k in range(2)]
        at = pl.multiple_of((pair * ABREAST + sub) * LANES, LANES)
        mixed_ref[:, pl.ds(at, LANES)] = jnp.where(low_half, mixed[0], mixed[1]).astype(bf16)


def after_kernel(
    experts, mixed_ref, perm_get, own_ref, oth_ref, x_get, dm_get,
    after_out, low_out, send_out, gain_out, mixed_out,
    stage,
):
    half = own_ref.shape[0]
    width = mixed_ref.shape[1]
    perm = perm_get()[...]
    mixed = mm(mixed_ref[...], perm).astype(bf16)
    mixed_out.ref[...] = mixed
    mixed_out.send()
    block = width + (experts // LANES) * LANES
    lanes = jnp.transpose(
        jnp.concatenate(
            [own_ref[:, block : block + LANES].astype(f32), oth_ref[:, block : block + LANES].astype(f32)],
            axis=0,
        )
    )
    at = experts % LANES
    gain = mm_nt(jnp.broadcast_to(lanes[at : at + 1, :], (8, width)).astype(bf16), perm)
    gain_out.ref[...] = gain
    gain_out.send()
    after = x_get()[...].astype(f32) + (
        mm(mixed[:, :half], own_ref[:, :width]) + mm(mixed[:, half:], oth_ref[:, :width])
    )
    after_out.ref[...] = after
    after_out.send()
    low = (after * inverse_rms(after) * gain[0:1, :]).astype(bf16)
    low_out.ref[...] = low
    low_out.send()
    to_slab(mm(dm_get()[...], low), stage, send_out.ref)


def between_kernel(
    mixed_get, normed_get, own_ref, oth_ref, perm_get, qkv_get,
    mixed_t_out, normed_t_out, wo_out, router_out, query_t_out,
):
    mixed_t_out.ref[...] = jnp.transpose(mixed_get()[...].astype(f32)).astype(bf16)
    mixed_t_out.send()
    normed_t_out.ref[...] = jnp.transpose(normed_get()[...].astype(f32)).astype(bf16)
    normed_t_out.send()
    half = own_ref.shape[0]
    perm = perm_get()[...]
    rest = (mm(perm[:, :half], own_ref[...]) + mm(perm[:, half:], oth_ref[...])).astype(bf16)
    width = wo_out.ref.shape[1]
    wo_out.ref[...] = rest[:, :width]
    router_out.ref[...] = rest[:, width:]
    wo_out.send()
    qkv_ref = qkv_get()
    for c in range(PAIRS):
        query = qkv_ref[:, c * BLOCK : c * BLOCK + LANES].astype(f32)
        query_t_out.ref[c * LANES : (c + 1) * LANES, :] = jnp.transpose(query).astype(bf16)


def early_expert_kernel(recv_ref, win_ref, wout_ref, cot_ref, win_low_ref, wout_low_ref, g_ref, stage):
    slots = cot_ref.shape[0]

    @pl.when(pl.program_id(0) == 0)
    def _():
        def put(c, values):
            cot_ref[:, c * LANES : (c + 1) * LANES] = values.astype(bf16)

        from_slab(recv_ref, stage, slots, put)

    win_low_ref[0] = win_ref[0].astype(bf16)
    wout = wout_ref[0].astype(bf16)
    wout_low_ref[...] = wout
    g_ref[0] = mm_nt(cot_ref[...], wout).astype(bf16)


def activate(pre):
    squared = pre * pre
    bent = jnp.tanh(pre * (gelu_coef + (gelu_coef * cubic_coef) * squared))
    rise = 0.5 + 0.5 * bent
    value = pre * rise
    slope = rise + (value - value * rise) * (
        2.0 * gelu_coef + (6.0 * gelu_coef * cubic_coef) * squared
    )
    return value, slope


def expert_kernel(
    experts, steps,
    me_ref, recv_ref, router_hbm, cot_hbm, win_hbm, wout_hbm, g_hbm,
    back_hbm, made_hbm, x_hbm, rows_hbm, glog_hbm, gate_hbm,
    stage, router_ref, cot_ref, win_ref, wout_ref, g_ref, hidden_ref, act_ref,
    back_ref, made_ref, x_ref, rows_ref, glog_ref, gate_ref, in_sems, out_sems,
):
    slots, width = x_ref.shape
    units = win_ref.shape[1] // steps
    parts = [slice(i * units, (i + 1) * units) for i in range(steps)]
    fetch = [(router_hbm, router_ref), (cot_hbm, cot_ref)]
    fetch += [(win_hbm.at[i], win_ref.at[:, p]) for i, p in enumerate(parts)]
    fetch += [(g_hbm.at[i], g_ref.at[:, p]) for i, p in enumerate(parts)]
    fetch += [(wout_hbm.at[p, :], wout_ref.at[p, :]) for p in parts]
    copies = [pltpu.make_async_copy(a, b, in_sems.at[i]) for i, (a, b) in enumerate(fetch)]
    stores = [
        pltpu.make_async_copy(a, b, out_sems.at[i])
        for i, (a, b) in enumerate(
            (
                (back_ref, back_hbm), (made_ref, made_hbm), (x_ref, x_hbm),
                (rows_ref, rows_hbm), (glog_ref, glog_hbm), (gate_ref, gate_hbm),
            )
        )
    ]
    sequence = [0, 2, 2 + steps, 3, 3 + steps]
    for i in sequence:
        copies[i].start()

    def put(c, values):
        x_ref[:, c * LANES : (c + 1) * LANES] = values.astype(bf16)

    from_slab(recv_ref, stage, slots, put)
    stores[2].start()
    copies[0].wait()
    router = router_ref[...]
    wide = router.shape[1]
    logits = mm(x_ref[...], router)
    for step, part in enumerate(parts):
        if step + 2 < steps:
            copies[4 + step].start()
            copies[4 + step + steps].start()
        else:
            for i in range(steps // 2):
                copies[2 + 2 * steps + (step + 2 - steps) * (steps // 2) + i].start()
        if step == steps - 1:
            copies[1].start()
        copies[2 + step].wait()
        copies[2 + step + steps].wait()
        value, slope = activate(mm(x_ref[...], win_ref[:, part]))
        hidden_ref[:, part] = value.astype(bf16)
        act_ref[:, part] = (g_ref[:, part].astype(f32) * slope).astype(bf16)
    for step in range(steps):
        copies[2 + 2 * steps + step].wait()
    produced = mm(hidden_ref[...], wout_ref[...]).astype(bf16)
    made_ref[...] = produced
    stores[1].start()
    lane = lax.broadcasted_iota(jnp.int32, (slots, wide), 1)
    logits = jnp.where(lane < experts, logits, -jnp.inf)
    weights = jnp.exp(logits - jnp.max(logits, axis=-1, keepdims=True))
    probs = weights / jnp.sum(weights, axis=-1, keepdims=True)
    own = (lane == me_ref[0]).astype(f32)
    gate = jnp.sum(probs * own, axis=-1, keepdims=True)
    gate_ref[...] = jnp.broadcast_to(gate, (slots, LANES))
    stores[5].start()
    copies[1].wait()
    cot = cot_ref[...].astype(f32)
    rows_ref[...] = (gate * cot).astype(bf16)
    stores[3].start()
    grad_gate = jnp.sum(cot * produced.astype(f32), axis=-1, keepdims=True)
    grad_logits = (probs * (own - gate) * grad_gate).astype(bf16)
    glog_ref[...] = grad_logits
    stores[4].start()
    back = (gate * mm_nt(act_ref[...], win_ref[...])).astype(bf16).astype(f32)
    to_slab(back + mm_nt(grad_logits, router), stage, back_ref)
    stores[0].start()
    for copy in stores:
        copy.wait()


def expert_weights_kernel(
    x_ref, rows_ref, glog_ref, gate_ref, made_ref, perm_ref, win_ref, g_ref,
    gin_ref, gout_ref, grouter_ref, prod_ref,
    xt, stage,
):
    @pl.when(pl.program_id(0) == 0)
    def _():
        to_slab(made_ref[...].astype(f32), stage, prod_ref)
        x = x_ref[...]
        xt[...] = jnp.transpose(gate_ref[:, 0:1] * x.astype(f32)).astype(bf16)
        moved = mm(x, perm_ref[...]).astype(bf16)
        grouter_ref[...] = mm_tn(moved, glog_ref[...])

    value, slope = activate(mm(x_ref[...], win_ref[0]))
    act = (g_ref[0].astype(f32) * slope).astype(bf16)
    gout_ref[0] = mm_tn(value.astype(bf16), rows_ref[...])
    gin_ref[0] = mm(xt[...], act)


def output_kernel(experts, recv_ref, dt_get, low_get, router_get, routes_get, after_get, out_out, stage, rows):
    def put(c, values):
        rows[:, c * LANES : (c + 1) * LANES] = values.astype(bf16)

    dt = dt_get()[...]
    from_slab(recv_ref, stage, dt.shape[1], put)
    produced = mm(dt, rows[...])
    logits = mm(low_get()[...], router_get()[...])
    lane = lax.broadcasted_iota(jnp.int32, logits.shape, 1)
    logits = jnp.where(lane < experts, logits, -jnp.inf)
    weights = jnp.exp(logits - jnp.max(logits, axis=-1, keepdims=True))
    own = (lane == routes_get()[...]).astype(f32)
    gate = jnp.sum(weights * own, axis=-1, keepdims=True) / jnp.sum(weights, axis=-1, keepdims=True)
    out_out.ref[...] = (after_get()[...] + gate * produced).astype(bf16)


def norm_two_kernel(
    experts,
    recv_ref, dt_get, after_get, gain_get, cot_get, wo_get, mixed_t_get, perm_get, grouter_get,
    grad_after_out, grad_mixed_ref, keep_ref, send_ref,
    stage, rows,
):
    def put(c, values):
        rows[:, c * LANES : (c + 1) * LANES] = values.astype(bf16)

    slots = recv_ref.shape[0] * LANES // grad_mixed_ref.shape[1]
    from_slab(recv_ref, stage, slots, put)
    grad = mm(dt_get()[...], rows[...])
    after = after_get()[...]
    inverse = inverse_rms(after)
    unit = after * inverse
    scaled = grad * gain_get()[0:1, :]
    back = inverse * (scaled - unit * jnp.mean(scaled * unit, axis=-1, keepdims=True))
    grad_after = cot_get()[...].astype(f32) + back
    grad_after_out.ref[...] = grad_after
    grad_after_out.send()
    low = grad_after.astype(bf16)
    grad_mixed_ref[...] = mm_nt(low, wo_get()[...]).astype(bf16)
    half = keep_ref.shape[0]
    width = low.shape[1]
    mixed_t_ref = mixed_t_get()
    keep_ref[:, :width] = mm(mixed_t_ref[:half, :], low)
    send_ref[:, :width] = mm(mixed_t_ref[half:, :], low).astype(bf16)
    gain_row = jnp.sum(grad * unit, axis=0, keepdims=True)
    high, rest = split_two(jnp.broadcast_to(gain_row, (8, width)))
    perm = perm_get()[...]
    gain_row = (mm(high, perm) + mm(rest, perm))[0:1, :]
    grouter = grouter_get()[...]
    lane = lax.broadcasted_iota(jnp.int32, grouter.shape, 1)
    packed = jnp.where(
        lane < experts, grouter, jnp.where(lane == experts, to_column(gain_row, grouter.shape[1]), 0.0)
    )
    keep_ref[:, width:] = packed[:half]
    send_ref[:, width:] = packed[half:].astype(bf16)


def unskew(skewed):
    span = 4 * LANES
    total = None
    for g in range(LANES // 8):
        moved = pltpu.roll(skewed[8 * g : 8 * g + 8, :], (LANES - 1 - 8 * g) % span, 1)
        total = moved if total is None else total + moved
    turned = jnp.concatenate([total[7 - s : 8 - s, :] for s in range(8)], axis=0)
    turned = pltpu.roll(turned, span - 7, 1, stride=1, stride_axis=0)
    return jnp.sum(turned, axis=0, keepdims=True)


def attend_backward_kernel(
    before, last, qkv_ref, query_t_ref, probs_ref, gm_ref, normed_t_ref, *refs
):
    refs = list(refs)
    vec_in = refs.pop(0) if before else None
    if last:
        hmask_ref, umask_ref = refs.pop(0), refs.pop(0)
    keep_ref, send_ref, dvec_ref, dq_ref, dkv_ref, dp_ref, ds_ref = refs
    pairs_before = 0 if vec_in is None else vec_in.shape[0] // 2
    pair = pl.program_id(0)
    tokens = qkv_ref.shape[0]
    blocks = tokens // LANES
    low_half = lax.broadcasted_iota(jnp.int32, (tokens, LANES), 1) < HEAD_DIM
    lane = lax.broadcasted_iota(jnp.int32, (1, 4 * LANES), 1)
    keys, vals = (qkv_ref[:, k * LANES : (k + 1) * LANES] for k in (1, 2))
    grad = gm_ref[:, pl.ds(pl.multiple_of((pair + pairs_before) * LANES, LANES), LANES)]
    grad_t = jnp.transpose(grad.astype(f32)).astype(bf16)
    dq = []
    for k in range(2):
        keep = low_half if k == 0 else jnp.logical_not(low_half)
        dp_ref[k] = mm_nt(jnp.where(keep, grad, jnp.zeros_like(grad)), vals)
    for k in range(2):
        strip = [None] * 3
        far_left = far_right = None
        for i in range(blocks):
            rows = slice(i * LANES, (i + 1) * LANES)
            dp = dp_ref[k, rows, :]
            probs = probs_ref[k, rows, :].astype(f32)
            delta = jnp.sum(probs * dp, axis=-1, keepdims=True)
            ds = (probs * (dp - delta)).astype(bf16)
            ds_ref[k, rows, :] = ds
            wide = ds.astype(f32)
            for j in range(blocks):
                piece = wide[:, j * LANES : (j + 1) * LANES]
                if j < i - 1:
                    far_left = piece if far_left is None else far_left + piece
                elif j > i + 1:
                    far_right = piece if far_right is None else far_right + piece
                else:
                    at = j - i + 1
                    strip[at] = piece if strip[at] is None else strip[at] + piece
        part = slice(k * HEAD_DIM, (k + 1) * HEAD_DIM)
        dq.append(mm(ds_ref[k], keys))
        dkv_ref[part, :] = mm(query_t_ref[part, :], ds_ref[k]).astype(bf16)
        low_part = slice(LANES + k * HEAD_DIM, LANES + (k + 1) * HEAD_DIM)
        dkv_ref[low_part, :] = mm(grad_t[part, :], probs_ref[k]).astype(bf16)
        vec = unskew(jnp.concatenate(strip + [jnp.zeros((LANES, LANES), f32)], axis=1))
        left = jnp.sum(jnp.sum(far_left, axis=0, keepdims=True), axis=1, keepdims=True)
        right = jnp.sum(jnp.sum(far_right, axis=0, keepdims=True), axis=1, keepdims=True)
        vec = vec + jnp.where(lane == 0, left, 0.0) + jnp.where(lane == 510, right, 0.0)
        dvec_ref[pl.ds((pair + pairs_before) * 2 + k, 1), :] = vec
    dq_ref[...] = (jnp.where(low_half, dq[0], dq[1]) * HEAD_DIM ** (-0.5)).astype(bf16)
    half = keep_ref.shape[0]
    start = pl.multiple_of(pair * BLOCK, LANES)
    queries, rest = pl.ds(start, LANES), pl.ds(start + LANES, 2 * LANES)
    send_ref[:, queries] = mm(normed_t_ref[half:, :], dq_ref[...]).astype(bf16)
    send_ref[:, rest] = mm_nt(normed_t_ref[half:, :], dkv_ref[...]).astype(bf16)
    keep_ref[:, queries] = mm(normed_t_ref[:half, :], dq_ref[...])
    keep_ref[:, rest] = mm_nt(normed_t_ref[:half, :], dkv_ref[...])

    if vec_in is not None:

        @pl.when(pair == 0)
        def _():
            dvec_ref[: 2 * pairs_before, :] = vec_in[...]

    if not last:
        return

    @pl.when(pair == pl.num_programs(0) - 1)
    def _():
        table_col = table_column(
            jnp.concatenate([dvec_ref[...], jnp.zeros((16 - HEADS, 4 * LANES), f32)], axis=0),
            hmask_ref,
            umask_ref,
        )
        lane = lax.broadcasted_iota(jnp.int32, (2 * half, LANES), 1)
        packed = jnp.where(lane == 0, table_col, 0.0)
        end = keep_ref.shape[1] - LANES
        keep_ref[:, end:] = packed[:half]
        send_ref[:, end:] = packed[half:].astype(bf16)


def split_three(values):
    one, rest = split_two(values)
    two, three = split_two(values - one.astype(f32))
    return one, two, three


def table_column(vec, hmask_ref, umask_ref):
    offset = lax.broadcasted_iota(jnp.int32, (LANES, 4 * LANES), 1) - 255
    onehot = (
        lax.broadcasted_iota(jnp.int32, (LANES, 4 * LANES), 0) == buckets_of(offset)
    ).astype(f32).astype(bf16)
    one, two, three = split_three(vec)
    table = mm_nt(one, onehot) + (mm_nt(two, onehot) + mm_nt(three, onehot))
    heads = hmask_ref[:, :16]
    one, two, three = split_three(table)
    spread = mm(heads, one) + (mm(heads, two) + mm(heads, three))
    return jnp.sum(spread * umask_ref[...].astype(f32), axis=1, keepdims=True)


def last_kernel(own_get, oth_get, xperm_get, gain_get, perm_get, after_get, *refs):
    *gets, out_out, grads_ref = refs
    runs = len(gets) // 2
    at = 0
    for dq_get, dkv_get in zip(gets[:runs], gets[runs:]):
        dq, dkv_t = dq_get()[...], dkv_get()
        for c in range(dq.shape[1] // LANES):
            grads_ref[:, at : at + LANES] = dq[:, c * LANES : (c + 1) * LANES]
            moved = jnp.transpose(dkv_t[2 * c * LANES : 2 * (c + 1) * LANES, :].astype(f32))
            grads_ref[:, at + LANES : at + BLOCK] = moved.astype(bf16)
            at += BLOCK
    grads = grads_ref[...]
    cols = slice(0, at)
    grad = jnp.concatenate(
        [mm_nt(grads, own_get()[:, cols]), mm_nt(grads, oth_get()[:, cols])], axis=1
    )
    x = xperm_get()[...].astype(f32)
    inverse = inverse_rms(x)
    unit = x * inverse
    scaled = grad * gain_get()[0:1, :]
    back = inverse * (scaled - unit * jnp.mean(scaled * unit, axis=-1, keepdims=True))
    high, rest = split_two(back)
    perm = perm_get()[...]
    out_out.ref[...] = (after_get()[...] + (mm_nt(high, perm) + mm_nt(rest, perm))).astype(bf16)


def fold_kernel(plan, *refs):
    refs = list(refs)
    total_in = sum(1 + n for members, _ in plan for n in members)
    ins, outs = refs[:total_in], refs[total_in:]
    for members, parts in plan:
        outs_here = [outs.pop(0) for _ in range(parts)]
        at = 0
        for arrived in members:
            total = ins.pop(0)[...]
            for _ in range(arrived):
                total = total + ins.pop(0)[...].astype(f32)
            rows = total.shape[0] // parts
            cols = slice(at, at + total.shape[1])
            at += total.shape[1]
            for m, out in enumerate(outs_here):
                out[:, cols] = total[m * rows : (m + 1) * rows].astype(out.dtype)


def summed(first_ref, moved):
    total = first_ref[...]
    for piece in moved:
        total = total + piece[...].astype(f32)
    return total


def as_row(column):
    size = column.shape[0]
    same = lax.broadcasted_iota(jnp.int32, (size, size), 0) == lax.broadcasted_iota(
        jnp.int32, (size, size), 1
    )
    return jnp.sum(jnp.where(same, column, 0.0), axis=0, keepdims=True)


def finish_kernel(moved_group, gain_get, wq_get, wk_get, wv_get, first_group, first_last, *refs):
    *moved, wo_out, router_out, gain_two_out, wq_out, wk_out, wv_out, gain_out, table_out = refs
    total = summed(first_group, moved[:moved_group])
    width, experts = wo_out.ref.shape[1], router_out.ref.shape[1]
    wo_out.ref[...] = total[:, :width]
    wo_out.send()
    router_out.ref[...] = total[:, width : width + experts]
    router_out.send()
    gain_two_out.ref[...] = as_row(total[:, width + experts : width + experts + 1])
    gain_two_out.send()
    early = RUNS[1]
    sources = [(total, total.shape[1] - early * BLOCK)]
    total = summed(first_last, moved[moved_group:])
    sources.append((total, -early * BLOCK))
    for c in range(PAIRS):
        source, base = sources[c >= early]
        for k, out in enumerate((wq_out, wk_out, wv_out)):
            at = base + c * BLOCK + k * LANES
            out.ref[:, c * LANES : (c + 1) * LANES] = source[:, at : at + LANES]
    for out in (wq_out, wk_out, wv_out):
        out.send()
    products = None
    for get, out in ((wq_get, wq_out), (wk_get, wk_out), (wv_get, wv_out)):
        part = get()[...].astype(bf16).astype(f32) * out.ref[...]
        products = part if products is None else products + part
    gain = gain_get()[...].astype(bf16).astype(f32)
    gain_out.ref[...] = as_row(jnp.sum(products, axis=1, keepdims=True)) / gain
    at = total.shape[1] - LANES
    entries = table_out.ref.shape[1]
    table_out.ref[...] = as_row(total[:, at : at + 1])[:, :entries]


def join_kernel(*refs):
    *pieces, out_ref, sems = refs
    rows = pieces[0].shape[0]
    copies = [
        pltpu.make_async_copy(p, out_ref.at[pl.ds(i * rows, rows), :], sems.at[i])
        for i, p in enumerate(pieces)
    ]
    for copy in copies:
        copy.start()
    for copy in copies:
        copy.wait()


def join(values, moved, space):
    pieces = [values, *moved]
    if values.shape[0] % 8:
        return jnp.concatenate(pieces, axis=0)
    shape = (len(pieces) * values.shape[0], values.shape[1])
    any_ref = pl.BlockSpec(memory_space=pl.ANY)
    return pl.pallas_call(
        join_kernel,
        out_shape=space(shape, values.dtype),
        in_specs=[any_ref] * len(pieces),
        out_specs=any_ref,
        scratch_shapes=[pltpu.SemaphoreType.DMA((len(pieces),))],
        **parameters(4, 1),
    )(*pieces)


def assemble_kernel(moves, count, *refs):
    sources, outs, sems = refs[:count], refs[count:-1], refs[-1]
    copies = []
    for i, (source, row, rows, col, cols, out, to_row, to_col) in enumerate(moves):
        copies.append(
            pltpu.make_async_copy(
                sources[source].at[pl.ds(row, rows), pl.ds(col, cols)],
                outs[out].at[pl.ds(to_row, rows), pl.ds(to_col, cols)],
                sems.at[i],
            )
        )
    for copy in copies:
        copy.start()
    for copy in copies:
        copy.wait()


def assemble(arrays, outs, moves):
    if any(m[i] % 8 for m in moves for i in (1, 2, 6)):
        made = [jnp.zeros(o.shape, o.dtype) for o in outs]
        for a, row, rows, col, cols, out, to_row, to_col in moves:
            block = arrays[a][row : row + rows, col : col + cols]
            made[out] = lax.dynamic_update_slice(made[out], block, (to_row, to_col))
        return made
    any_ref = pl.BlockSpec(memory_space=pl.ANY)
    return pl.pallas_call(
        functools.partial(assemble_kernel, moves, len(arrays)),
        out_shape=list(outs),
        in_specs=[any_ref] * len(arrays),
        out_specs=[any_ref] * len(outs),
        scratch_shapes=[pltpu.SemaphoreType.DMA((len(moves),))],
        **parameters(4, 1),
    )(*arrays)


def expert_call(experts, steps, slots, width, units, wide):
    slab = (slots * width // LANES, LANES)
    any_ref, vmem_ref = (pl.BlockSpec(memory_space=m) for m in (pl.ANY, pltpu.VMEM))
    outs = [slab, (slots, width), (slots, width), (slots, width), (slots, wide)]
    call = pl.pallas_call(
        functools.partial(expert_kernel, experts, steps),
        out_shape=[far(shape, bf16) for shape in outs] + [far((slots, LANES), f32)],
        in_specs=[pl.BlockSpec(memory_space=pltpu.SMEM), vmem_ref] + [any_ref] * 5,
        out_specs=[any_ref] * 6,
        scratch_shapes=[pltpu.VMEM(slab, f32)]
        + [
            pltpu.VMEM(shape, bf16)
            for shape in (
                (width, wide), (slots, width), (width, units), (units, width),
                (slots, units), (slots, units), (slots, units),
            )
        ]
        + [pltpu.VMEM(shape, bf16) for shape in outs]
        + [
            pltpu.VMEM((slots, LANES), f32),
            pltpu.SemaphoreType.DMA((2 + 3 * steps,)),
            pltpu.SemaphoreType.DMA((6,)),
        ],
        **parameters(52, 18),
    )
    return lambda me, recv, *rest: call(me, recv, *[place(Far(a)) for a in rest])


def shards(
    count,
    inputs,
    segment_ids,
    routes,
    cotangent,
    gain_attn,
    gain_ffn,
    bias_table,
    w_query,
    w_key,
    w_value,
    w_output,
    w_router,
    w_in,
    w_out,
):
    tokens, width = inputs.shape
    experts = w_router.shape[1]
    rows_local = w_query.shape[0]
    entries = bias_table.shape[0]
    hidden_units = w_in.shape[2]
    capacity = max(2, 5 * tokens // (4 * experts))
    slots = experts * capacity
    blocks = width // LANES
    half = width // 2
    wide = -(-(experts + 1) // LANES) * LANES
    me = lax.axis_index("seq").astype(jnp.int32).reshape(1)
    vmem = pl.BlockSpec(memory_space=pltpu.VMEM)

    groups = bit_groups(count)
    levels = list(reversed(groups[1:]))
    columns = PAIRS * BLOCK
    piece, tail = flat_call(
        functools.partial(pack_kernel, experts),
        [near((rows_local, columns + LANES), bf16), near((rows_local, width + wide), bf16)],
        us=1,
    )(
        *map(Far, (gain_attn[None, :], gain_ffn[None, :], bias_table[None, :])),
        *map(Far, (w_query, w_key, w_value, w_output, w_router)),
    )

    def reach(values, low_bit, bits):
        return [swap(values, m << low_bit, count) for m in range(1, 1 << bits)]

    order = np.asarray(relative_order(count), np.int32)
    rel_row = jnp.asarray(np.repeat(order, rows_local)[None, :])
    off_row = jnp.asarray(np.tile(np.arange(rows_local, dtype=np.int32), count)[None, :])
    slab = (slots * blocks, LANES)
    slab_stage = pltpu.VMEM(slab, f32)
    perm, xperm, segrow, segcol, hmask, umask, dt, dm = flat_call(
        functools.partial(prepare_kernel, rows_local, entries, experts, capacity),
        [
            far((width, width), bf16),
            far((tokens, width), bf16),
            far((8, tokens), f32),
            far((tokens, LANES), f32),
            far((width, LANES), bf16),
            far((width, LANES), bf16),
            far((tokens, slots), bf16),
            far((slots, tokens), bf16),
        ],
        us=8,
    )(me, Far(rel_row), Far(off_row), Far(inputs), Far(segment_ids), Far(routes))
    cot_send = flat_call(dispatch_kernel, [far(slab, bf16)], us=3, scratch=[slab_stage])(
        Far(dm), Far(cotangent)
    )[0]

    moved = reach(piece, *levels[0])
    moved = lax.optimization_barrier((*moved, perm))[:-1]
    total = columns + LANES
    sizes = (columns // 2, total - columns // 2)
    starts = (0, sizes[0])
    rows = rows_local
    pieces = [piece, *moved]
    moves = [
        (i, 0, rows, starts[p], sizes[p], p, i * rows, 0) for i in range(len(pieces)) for p in range(2)
    ]
    rows *= len(pieces)
    parts = assemble(pieces, [near((rows, size), bf16) for size in sizes], moves)
    for k, (low_bit, _) in enumerate(levels[1:]):
        steps_of = ((2 << low_bit, 1 << low_bit), (1 << low_bit, 2 << low_bit))
        got = [swap(part, d[0], count) for part, d in zip(parts, steps_of)]
        tail_moved = reach(after(tail, *parts, cot_send), *levels[k])
        got = lax.optimization_barrier((*got, cot_send))[:-1]
        moves = [(p + 2 * i, 0, rows, 0, sizes[p], p, i * rows, 0) for i in range(2) for p in range(2)]
        parts = assemble(
            [*parts, *got], [near((2 * rows, size), bf16) for size in sizes], moves
        )
        got = [swap(part, d[1], count) for part, d in zip(parts, steps_of)]
        got = lax.optimization_barrier((*got, *tail_moved))[:2]
        tail = join(tail, tail_moved, near)
        final = k == len(levels) - 2
        order_of = (((0, 2), (1, 3)), ((0, 1), (2, 3)))
        moves = [
            (p + 2 * i, b * rows, rows, 0, sizes[p], 0 if final else p, order_of[p][i][b] * rows,
             starts[p] if final else 0)
            for i in range(2) for p in range(2) for b in range(2)
        ]
        outs = [far((4 * rows, total), bf16)] if final else [near((4 * rows, size), bf16) for size in sizes]
        parts = assemble([*parts, *got], outs, moves)
        rows *= 4
    piece = parts[0]
    other = swap(piece, 1, count)
    tail_moved = reach(after(tail, piece), *levels[-1])

    slab_split = (count, slots * blocks // count, LANES)

    def exchange(rows):
        return lax.all_to_all(
            rows.reshape(slab_split), "seq", split_axis=0, concat_axis=0, tiled=True
        ).reshape(slab)

    cot_recv = exchange(after(cot_send, other))

    def whole(shape):
        return pl.BlockSpec(shape, lambda i: (0,) * len(shape))

    pair_probs = pl.BlockSpec((2 * ABREAST, tokens, tokens), lambda i: (i, 0, 0))
    piece, other = Far(piece), Far(other)
    small_block = pl.BlockSpec((half, LANES), lambda i: (0, columns // LANES))
    pair_weights = pl.BlockSpec((half, ABREAST * BLOCK), lambda i: (0, i))
    qkv, probs, mixed, normed, gain_one = grid_call(
        attend_forward_kernel,
        [
            far((tokens, PAIRS * BLOCK), bf16),
            far((HEADS, tokens, tokens), bf16),
            near((tokens, width), bf16),
            far((tokens, width), bf16),
            far((8, width), f32),
        ],
        grid=(PAIRS // ABREAST,),
        in_specs=[whole((tokens, width))]
        + [pair_weights, pair_weights, small_block, small_block]
        + [whole(shape) for shape in ((width, LANES), (width, LANES), (8, tokens), (tokens, LANES))],
        out_specs=[
            pl.BlockSpec((tokens, ABREAST * BLOCK), lambda i: (0, i)),
            pair_probs,
            vmem,
            whole((tokens, width)),
            whole((8, width)),
        ],
        scratch=[
            pltpu.VMEM((16, 4 * LANES), f32),
            pltpu.VMEM((2 * ABREAST, tokens, tokens), f32),
            pltpu.VMEM((2 * ABREAST, LANES, 3 * LANES), f32),
        ],
        us=14,
    )(
        Far(after(xperm, tail)), piece, other, piece, other,
        *map(Far, (hmask, umask, segrow, segcol)),
    )
    tail_moved = lax.optimization_barrier((*tail_moved, mixed))[:-1]
    tail = join(tail, tail_moved, near)
    tail_other = swap(tail, 1, count)

    after_rows, low_two, row_send, gain_two, mixed_perm = flat_call(
        functools.partial(after_kernel, experts),
        [
            far((tokens, width), f32),
            far((tokens, width), bf16),
            far(slab, bf16),
            far((8, width), f32),
            far((tokens, width), bf16),
        ],
        us=6,
        scratch=[slab_stage],
    )(mixed, Far(perm), tail, tail_other, Far(inputs), Far(dm))
    row_recv = exchange(row_send)

    steps = 6
    units = hidden_units // steps
    weight_in = pl.BlockSpec((1, width, units), lambda i: (0, 0, i))
    weight_out = pl.BlockSpec((1, units, width), lambda i: (0, i, 0))

    low_in = pl.BlockSpec((1, width, units), lambda i: (i, 0, 0))
    low_out = pl.BlockSpec((units, width), lambda i: (i, 0))
    slot_units = pl.BlockSpec((1, slots, units), lambda i: (i, 0, 0))
    cot_rows, win_low, wout_low, grad_hidden = grid_call(
        early_expert_kernel,
        [
            far((slots, width), bf16),
            far((steps, width, units), bf16),
            far((hidden_units, width), bf16),
            far((steps, slots, units), bf16),
        ],
        grid=(steps,),
        in_specs=[whole(slab), weight_in, weight_out],
        out_specs=[whole((slots, width)), low_in, low_out, slot_units],
        us=13,
        scratch=[slab_stage],
    )(cot_recv, Far(w_in), Far(w_out))
    mixed_t, normed_t, output_w, router_w, query_t = flat_call(
        between_kernel,
        [
            far((width, tokens), bf16),
            far((width, tokens), bf16),
            far((width, width), bf16),
            far((width, wide), bf16),
            far((width, tokens), bf16),
        ],
        us=7,
    )(Far(mixed_perm), Far(normed), tail, tail_other, Far(perm), Far(qkv))
    back_send, made, x_rows, grad_rows, grad_logits, gates = expert_call(
        experts, steps, slots, width, hidden_units, wide
    )(me, row_recv, router_w, cot_rows, win_low, wout_low, grad_hidden)
    back_recv = exchange(back_send)
    grad_inner, grad_outer, grad_router, prod_send = grid_call(
        expert_weights_kernel,
        [
            far((1, width, hidden_units), f32),
            far((1, hidden_units, width), f32),
            far((width, wide), f32),
            far(slab, bf16),
        ],
        grid=(steps,),
        in_specs=[
            whole((slots, width)),
            whole((slots, width)),
            whole((slots, wide)),
            whole((slots, LANES)),
            whole((slots, width)),
            whole((width, width)),
            low_in,
            slot_units,
        ],
        out_specs=[weight_in, weight_out, whole((width, wide)), whole(slab)],
        us=19,
        scratch=[pltpu.VMEM((width, slots), bf16), slab_stage],
    )(*map(Far, (x_rows, grad_rows, grad_logits, gates, made, perm, win_low, grad_hidden)))
    prod_recv = exchange(prod_send)

    row_scratch = pltpu.VMEM((slots, width), bf16)
    grad_after, grad_mixed, keep_o, send_o = flat_call(
        functools.partial(norm_two_kernel, experts),
        [
            far((tokens, width), f32),
            near((tokens, width), bf16),
            near((half, width + wide), f32),
            near((half, width + wide), bf16),
        ],
        us=1,
        scratch=[slab_stage, row_scratch],
    )(
        back_recv,
        *map(Far, (dt, after_rows, gain_two, cotangent, output_w, mixed_t, perm, grad_router)),
    )

    def backward(run, ready):
        start, stop = RUNS[run], RUNS[run + 1]
        last = stop == PAIRS
        vec = before.get("vec")
        here = [Far(qkv), Far(query_t), Far(probs), after(grad_mixed, *ready), Far(normed_t)]
        specs = [
            pl.BlockSpec((tokens, BLOCK), lambda i: (0, i + start)),
            pl.BlockSpec((LANES, tokens), lambda i: (i + start, 0)),
            pl.BlockSpec((2, tokens, tokens), lambda i: (i + start, 0, 0)),
            vmem,
            whole((width, tokens)),
        ]
        if vec is not None:
            here.append(vec)
            specs.append(vmem)
        if last:
            here += [Far(hmask), Far(umask)]
            specs += [whole((width, LANES))] * 2
        pairs = stop - start
        cols = pairs * BLOCK + (LANES if last else 0)
        keep, send, vec, dq, dkv_t = grid_call(
            functools.partial(attend_backward_kernel, vec is not None, last),
            [
                near((half, cols), f32),
                near((half, cols), bf16),
                near((2 * stop, 4 * LANES), f32),
                far((tokens, pairs * LANES), bf16),
                far((2 * pairs * LANES, tokens), bf16),
            ],
            grid=(pairs,),
            in_specs=specs,
            out_specs=[
                vmem,
                vmem,
                vmem,
                pl.BlockSpec((tokens, LANES), lambda i: (0, i)),
                pl.BlockSpec((2 * LANES, tokens), lambda i: (i, 0)),
            ],
            scratch=[
                pltpu.VMEM((2, tokens, tokens), f32),
                pltpu.VMEM((2, tokens, tokens), bf16),
            ],
            us=(1, 4)[run],
            vmem=24,
        )(*here)
        before.update(vec=vec)
        born.append((keep, send))
        grads.append((dq, dkv_t))
        return keep

    def results(ready):
        return flat_call(
            functools.partial(output_kernel, experts),
            [far((tokens, width), bf16)],
            us=0.001,
            scratch=[slab_stage, row_scratch],
            vmem=20,
        )(after(prod_recv, *ready), *map(Far, (dt, low_two, router_w, routes, after_rows)))[0]

    def finish(ready):
        return flat_call(
            last_kernel,
            [far((tokens, width), bf16)],
            us=8,
            scratch=[pltpu.VMEM((tokens, columns), bf16)],
            vmem=32,
        )(
            piece, other, Far(after(xperm, *ready)),
            *map(Far, (gain_one, perm, grad_after)),
            *[Far(g[0]) for g in grads], *[Far(g[1]) for g in grads],
        )[0]

    before, born, grads = {}, [(keep_o, send_o)], []
    ups = groups[1:]
    core = (1, 2)
    first = (1 << ups[0][0], 1 << ups[0][1])
    direct = [(1 << low_bit, 1 << bits) for low_bit, bits in ups[1:]]
    halving = [(1 << (low_bit + b), 2) for low_bit, bits in ups[1:] for b in reversed(range(bits))]
    plans = {c: {c: core, c + 1: first} for c in range(3)}
    plans[2].update({4 + i: step for i, step in enumerate(direct)})
    plans[3] = {3 + i: step for i, step in enumerate(halving)}
    work = {run: [functools.partial(backward, run)] for run in range(2)}
    work.update({2: [finish], 3: [results]})
    own, going, flight, finished = {}, {}, {}, {}
    output = grad_inputs = None
    end = max(max(plan) for plan in plans.values())
    own[0], going[0] = born[0][0], [born[0][1]]
    for slot in range(end + 1):
        for c, plan in plans.items():
            if slot in plan:
                distance, parts = plan[slot]
                flight[c] = [swap(g, (m + 1) * distance, count) for m, g in enumerate(going[c])]
        ready = [own[c] for c in flight] + ([prod_recv] if slot == 2 else [])
        for step in work.get(slot, []):
            value = step(ready)
            ready = [value]
            if step is results:
                output = value
            if step is finish:
                grad_inputs = value
        if slot in work:
            for c in flight:
                flight[c] = list(lax.optimization_barrier((*flight[c], value))[:-1])
        folds, args, outs, cut = [], [], [], []

        def fold(members, following, name):
            parts = following[1]
            folds.append(([len(flight[c]) if c in flight else 0 for c in members], parts))
            rows = own[members[0]].shape[0] // parts
            cols = sum(own[c].shape[1] for c in members)
            for c in members:
                args.append(own[c])
                args.extend(flight.pop(c, []))
            outs.append(near((rows, cols), f32))
            outs.extend([near((rows, cols), bf16)] * (parts - 1))
            cut.append((name, parts))

        if slot == 2:
            fold([0, 1], plans[3][3], 3)
        for c in list(flight):
            following = plans[c].get(slot + 1)
            if following or c < 2:
                fold([c], following or (0, 1), c)
            else:
                finished[c] = [own[c], *flight.pop(c)]
        if folds:
            folded = list(
                flat_call(functools.partial(fold_kernel, folds), outs, us=1, vmem=16)(*args)
            )
            for c, parts in cut:
                own[c] = folded.pop(0)
                going[c] = [folded.pop(0) for _ in range(parts - 1)]
            if len(born) == slot + 2:
                own[slot + 1] = born[-1][0]
                going[slot + 1] = [after(born[-1][1], own[cut[0][0]])]

    def row(size):
        return far((1, size), f32)

    square = far((rows_local, width), f32)
    grad_wo, grad_wr, grad_gain_two, grad_q, grad_k, grad_v, grad_gain_one, grad_table = flat_call(
        functools.partial(finish_kernel, len(finished[3]) - 1),
        [square, far((rows_local, experts), f32), row(rows_local)]
        + [square, square, square, row(rows_local), row(entries)],
        us=2,
        vmem=16,
    )(
        *map(Far, (gain_attn[None, :], w_query, w_key, w_value)),
        finished[3][0], finished[2][0], *finished[3][1:], *finished[2][1:],
    )

    return (
        output,
        grad_inputs,
        grad_gain_one[0],
        grad_gain_two[0],
        grad_table[0],
        grad_q,
        grad_k,
        grad_v,
        grad_wo,
        grad_wr,
        grad_inner,
        grad_outer,
    )


def solution(mesh):
    row, flat, cube = P("seq", None), P("seq"), P("seq", None, None)
    in_specs = (row,) * 4 + (flat,) * 3 + (row,) * 5 + (cube,) * 2
    out_specs = (row,) * 2 + (flat,) * 3 + (row,) * 5 + (cube,) * 2
    return jax.shard_map(
        functools.partial(shards, mesh.shape["seq"]),
        mesh=mesh,
        in_specs=in_specs,
        out_specs=out_specs,
        check_vma=False,
    )
```

```python
import functools

import jax
import jax.numpy as jnp
import numpy as np
from jax import lax
from jax.experimental import pallas as pl
from jax.experimental.pallas import tpu as pltpu
from jax.sharding import PartitionSpec as P

HEADS = 12
HEAD_DIM = 64
BUCKETS = 32
PAIRS = HEADS // 2
RUNS = (0, 4, 6)
ABREAST = 1
LANES = 128
BLOCK = 3 * LANES

epsilon = 1e-06
bucket_edges = (1, 2, 3, 4, 5, 6, 7, 8, 12, 16, 23, 32, 46, 64, 91)
gelu_coef = 0.7978845608028654
cubic_coef = 0.044715

f32 = jnp.float32
bf16 = jnp.bfloat16


def bit_groups(count):
    bits = count.bit_length() - 1
    groups, low = [(0, 1)], 1
    while low < bits:
        width = min(2, bits - low)
        groups.append((low, width))
        low += width
    return groups


def relative_order(count):
    order = [0]
    for low, width in bit_groups(count):
        order = [base + (m << low) for base in order for m in range(1 << width)]
    return order


def swap(values, distance, count):
    return lax.ppermute(values, "seq", [(i, i ^ distance) for i in range(count)])


def after(values, *others):
    return lax.optimization_barrier((values, *others))[0]


def mm(left, right):
    return jnp.dot(left, right, preferred_element_type=f32)


def mm_nt(left, right):
    return lax.dot_general(left, right, (((1,), (1,)), ((), ())), preferred_element_type=f32)


def mm_tn(left, right):
    return lax.dot_general(left, right, (((0,), (0,)), ((), ())), preferred_element_type=f32)


def split_two(values):
    high = values.astype(bf16)
    return high, (values - high.astype(f32)).astype(bf16)


class Far:
    def __init__(self, values, turn=0):
        self.values, self.turn = values, turn


def near(shape, dtype):
    return pltpu.VMEM(shape, dtype)


def far(shape, dtype):
    return pltpu.HBM(shape, dtype)


class Fetched:
    def __init__(self, copy, ref, following=()):
        self.copy, self.ref, self.here, self.following = copy, ref, False, following

    def __call__(self):
        if not self.here:
            self.copy.wait()
            self.here = True
            while self.following:
                self.following.pop().start()
        return self.ref


class Stored:
    def __init__(self, copy, ref):
        self.copy, self.ref, self.sent = copy, ref, False

    def send(self):
        self.copy.start()
        self.sent = True


def place(a):
    if isinstance(a, Far):
        return pltpu.with_memory_space_constraint(a.values, pltpu.HBM)
    return a


def parameters(vmem, us):
    return dict(
        compiler_params=pltpu.CompilerParams(vmem_limit_bytes=vmem * 1024 * 1024),
        cost_estimate=pl.CostEstimate(
            flops=int(us * 10**9), bytes_accessed=int(us * 10**6), transcendentals=0
        ),
    )


def grid_call(body, outs, grid, in_specs, out_specs, us, scratch=(), vmem=40):
    call = pl.pallas_call(
        body,
        out_shape=list(outs),
        grid=grid,
        in_specs=in_specs,
        out_specs=out_specs,
        scratch_shapes=list(scratch),
        **parameters(vmem, us),
    )
    return lambda *args: call(*[place(a) for a in args])


def flat_call(body, outs, us, scratch=(), vmem=32):
    def run(*args):
        lazy = [isinstance(a, Far) for a in args]
        late = [o.memory_space == pltpu.HBM for o in outs]
        values = [a.values if f else a for a, f in zip(args, lazy)]
        n_in, n_out, n_scratch = len(args), len(outs), len(scratch)
        any_ref, vmem_ref, smem_ref = (
            pl.BlockSpec(memory_space=m) for m in (pl.ANY, pltpu.VMEM, pltpu.SMEM)
        )
        in_copies = [pltpu.VMEM(v.shape, v.dtype) for v, f in zip(values, lazy) if f]
        out_copies = [pltpu.VMEM(o.shape, o.dtype) for o, f in zip(outs, late) if f]

        def wrapped(*refs):
            ins, rest = refs[:n_in], refs[n_in:]
            results, rest = rest[:n_out], rest[n_out:]
            own, rest = rest[:n_scratch], rest[n_scratch:]
            fetched, rest = list(rest[: len(in_copies)]), rest[len(in_copies) :]
            stored, rest = list(rest[: len(out_copies)]), rest[len(out_copies) :]
            sems = list(rest)
            given, made = [], []
            turns = {}
            for ref, a, f in zip(ins, args, lazy):
                if f:
                    copy = pltpu.make_async_copy(ref, fetched[0], sems.pop())
                    if a.turn:
                        turns.setdefault(a.turn, []).append(copy)
                    else:
                        copy.start()
                    given.append(Fetched(copy, fetched.pop(0), turns.setdefault(a.turn + 1, [])))
                else:
                    given.append(ref)
            for ref, f in zip(results, late):
                if f:
                    made.append(
                        Stored(pltpu.make_async_copy(stored[0], ref, sems.pop()), stored[0])
                    )
                    stored.pop(0)
                else:
                    made.append(ref)
            body(*given, *made, *own)
            for item in given:
                if isinstance(item, Fetched):
                    item()
            for item in made:
                if isinstance(item, Stored):
                    if not item.sent:
                        item.send()
                    item.copy.wait()

        return pl.pallas_call(
            wrapped,
            out_shape=list(outs),
            in_specs=[
                any_ref if f else (smem_ref if v.size == 1 else vmem_ref)
                for v, f in zip(values, lazy)
            ],
            out_specs=[any_ref if f else vmem_ref for f in late],
            scratch_shapes=list(scratch)
            + in_copies
            + out_copies
            + [pltpu.SemaphoreType.DMA] * (len(in_copies) + len(out_copies)),
            **parameters(vmem, us),
        )(*[place(a) for a in args])

    return run


def to_slab(values, stage, out_ref):
    slots, width = values.shape
    blocks = width // LANES
    for c in range(blocks):
        stage[pl.ds(c, slots, stride=blocks), :] = values[:, c * LANES : (c + 1) * LANES]
    out_ref[...] = stage[...].astype(out_ref.dtype)


def from_slab(in_ref, stage, slots, put):
    stage[...] = in_ref[...].astype(f32)
    blocks = in_ref.shape[0] // slots
    for c in range(blocks):
        put(c, stage[pl.ds(c, slots, stride=blocks), :])


def to_column(row, width=LANES):
    return jnp.transpose(jnp.broadcast_to(row, (width, row.shape[1])))


def inverse_rms(values):
    return lax.rsqrt(jnp.mean(values * values, axis=-1, keepdims=True) + epsilon)


def buckets_of(offset):
    magnitude = jnp.abs(offset)
    bucket = jnp.zeros(offset.shape, jnp.int32)
    for edge in bucket_edges:
        bucket = bucket + (magnitude >= edge).astype(jnp.int32)
    return bucket + BUCKETS // 2 * (offset > 0).astype(jnp.int32)


def prepare_kernel(
    rows_local, entries, experts, capacity,
    me_ref, rel_ref, off_ref, x_get, seg_get, routes_get,
    perm_out, xperm_out, segrow_out, segcol_out, hmask_out, umask_out, dt_out, dm_out,
):
    perm_ref, xperm_ref, segrow_ref, segcol_ref, hmask_ref, umask_ref, dt_ref, dm_ref = (
        out.ref
        for out in (perm_out, xperm_out, segrow_out, segcol_out, hmask_out, umask_out, dt_out, dm_out)
    )
    x_ref, seg_ref, routes_ref = x_get(), seg_get(), routes_get()
    tokens, width = x_ref.shape
    slots = dm_ref.shape[0]
    me = me_ref[0]
    device_row = rel_ref()[...] ^ me
    off_row = off_ref()[...]
    true_row = device_row * rows_local + off_row
    perm = (lax.broadcasted_iota(jnp.int32, (width, width), 0) == true_row).astype(f32).astype(bf16)
    perm_ref[...] = perm
    perm_out.send()
    xperm_ref[...] = mm(x_ref[...], perm).astype(bf16)
    xperm_out.send()
    segments = seg_ref[...].astype(f32)
    segrow_ref[...] = jnp.broadcast_to(segments, segrow_ref.shape)
    segcol_ref[...] = to_column(segments)
    flat = device_row * entries + off_row
    bucket_row = ((flat.astype(f32) + 0.5) * (1.0 / HEADS)).astype(jnp.int32)
    head_row = jnp.where(off_row < entries, flat - bucket_row * HEADS, -1)
    bucket_col = to_column(bucket_row.astype(f32))
    head_col = to_column(head_row.astype(f32))
    lane = lax.broadcasted_iota(jnp.int32, (width, LANES), 1).astype(f32)
    hmask_ref[...] = (head_col == lane).astype(f32).astype(bf16)
    umask_ref[...] = (bucket_col == lane).astype(f32).astype(bf16)
    for out in (segrow_out, segcol_out, hmask_out, umask_out):
        out.send()
    routes = routes_ref[...]
    labels = lax.broadcasted_iota(jnp.int32, (tokens, experts), 1)
    picked = (routes == labels).astype(f32)
    earlier = (
        lax.broadcasted_iota(jnp.int32, (tokens, tokens), 1)
        <= lax.broadcasted_iota(jnp.int32, (tokens, tokens), 0)
    ).astype(f32).astype(bf16)
    counts = mm(earlier, picked.astype(bf16))
    position = jnp.sum(counts * picked, axis=1, keepdims=True) - 1.0
    slot_col = jnp.where(
        position < capacity, routes.astype(f32) * capacity + position, -1.0
    )
    slot_lane = lax.broadcasted_iota(jnp.int32, (tokens, slots), 1).astype(f32)
    dt_ref[...] = (slot_col == slot_lane).astype(f32).astype(bf16)
    dt_out.send()
    slot_row = jnp.transpose(jnp.broadcast_to(slot_col, (tokens, LANES)))[0:1, :]
    slot_sub = lax.broadcasted_iota(jnp.int32, (slots, tokens), 0).astype(f32)
    dm_ref[...] = (slot_sub == slot_row).astype(f32).astype(bf16)


def dispatch_kernel(dm_get, cot_get, send_out, stage):
    to_slab(mm(dm_get()[...], cot_get()[...]), stage, send_out.ref)


def pack_kernel(
    experts, gain_get, gain_two_get, table_get, wq_get, wk_get, wv_get, wo_get, router_get,
    piece, tail,
):
    gain_ref, gain_two_ref, table_ref = gain_get(), gain_two_get(), table_get()
    wq_ref, wk_ref, wv_ref, wo_ref, router_ref = (
        get() for get in (wq_get, wk_get, wv_get, wo_get, router_get)
    )
    rows, width = wq_ref.shape

    def column(ref):
        size = ref.shape[1]
        same = lax.broadcasted_iota(jnp.int32, (rows, size), 0) == lax.broadcasted_iota(
            jnp.int32, (rows, size), 1
        )
        return jnp.sum(jnp.where(same, ref[...], 0.0), axis=1, keepdims=True)

    for c in range(PAIRS):
        for k, w in enumerate((wq_ref, wk_ref, wv_ref)):
            at = c * BLOCK + k * LANES
            piece[:, at : at + LANES] = w[:, c * LANES : (c + 1) * LANES].astype(bf16)
    lane = lax.broadcasted_iota(jnp.int32, (rows, LANES), 1)
    small = jnp.where(lane == 0, column(gain_ref), jnp.where(lane == 1, column(table_ref), 0.0))
    piece[:, PAIRS * BLOCK :] = small.astype(bf16)
    tail[:, :width] = wo_ref[...].astype(bf16)
    lane = lax.broadcasted_iota(jnp.int32, (rows, tail.shape[1] - width), 1)
    tail[:, width:] = jnp.where(lane == experts, column(gain_two_ref), 0.0).astype(bf16)
    tail[:, width : width + experts] = router_ref[...].astype(bf16)


def attend_forward_kernel(
    xperm_ref, own_ref, oth_ref, own_small, oth_small, hmask_ref, umask_ref, segrow_ref, segcol_ref,
    qkv_ref, probs_ref, mixed_ref, normed_ref, gain_ref,
    vec_ref, score_ref, strip_ref,
):
    half = own_ref.shape[0]
    tokens = segcol_ref.shape[0]
    blocks = tokens // LANES
    pair = pl.program_id(0)

    @pl.when(pair == 0)
    def _():
        packed = jnp.concatenate([own_small[...].astype(f32), oth_small[...].astype(f32)], axis=0)
        gain = jnp.transpose(packed)[0:1, :]
        gain_ref[...] = jnp.broadcast_to(gain, gain_ref.shape)
        spread = (packed[:, 1:2] * hmask_ref[...].astype(f32)).astype(bf16)
        table = mm_tn(spread, umask_ref[...])[:16]
        offset = lax.broadcasted_iota(jnp.int32, (LANES, 4 * LANES), 1) - 255
        onehot = (
            lax.broadcasted_iota(jnp.int32, (LANES, 4 * LANES), 0) == buckets_of(offset)
        ).astype(f32).astype(bf16)
        vec_ref[...] = mm(table.astype(bf16), onehot)
        x = xperm_ref[...].astype(f32)
        normed_ref[...] = (x * inverse_rms(x) * gain).astype(bf16)

    low_half = lax.broadcasted_iota(jnp.int32, (tokens, LANES), 1) < HEAD_DIM
    left, right, vals = {}, {}, []
    for sub in range(ABREAST):
        cols = slice(sub * BLOCK, (sub + 1) * BLOCK)
        qkv = mm(normed_ref[:, :half], own_ref[:, cols]) + mm(normed_ref[:, half:], oth_ref[:, cols])
        query = (qkv[:, :LANES].astype(bf16) * HEAD_DIM ** (-0.5)).astype(bf16)
        keys = qkv[:, LANES : 2 * LANES].astype(bf16)
        vals.append(qkv[:, 2 * LANES :].astype(bf16))
        at = sub * BLOCK
        qkv_ref[:, at : at + LANES] = query
        qkv_ref[:, at + LANES : at + 2 * LANES] = keys
        qkv_ref[:, at + 2 * LANES : at + BLOCK] = vals[sub]
        for k in range(2):
            head = 2 * sub + k
            keep = low_half if k == 0 else jnp.logical_not(low_half)
            score_ref[head] = mm_nt(jnp.where(keep, query, jnp.zeros_like(query)), keys)
            row = vec_ref[pl.ds(pair * 2 * ABREAST + head, 1), :]
            left[head] = row[:, 0:1]
            right[head] = row[:, 510:511]
            rolled = pltpu.roll(
                jnp.broadcast_to(row, (LANES, 4 * LANES)), 3 * LANES + 1, 1, stride=1, stride_axis=0
            )
            strip_ref[head] = rolled[:, : 3 * LANES]
    for sub in range(ABREAST):
        for i in range(blocks):
            rows = slice(i * LANES, (i + 1) * LANES)
            same = segcol_ref[rows, 0:1] == segrow_ref[0:1, :]
            for head in (2 * sub, 2 * sub + 1):
                bias = []
                for j in range(blocks):
                    if j < i - 1:
                        bias.append(jnp.broadcast_to(left[head], (LANES, LANES)))
                    elif j > i + 1:
                        bias.append(jnp.broadcast_to(right[head], (LANES, LANES)))
                    else:
                        at = (j - i + 1) * LANES
                        bias.append(strip_ref[head, :, at : at + LANES])
                scores = score_ref[head, rows, :] + jnp.concatenate(bias, axis=1)
                scores = jnp.where(same, scores, -1000000000.0)
                top = jnp.max(scores, axis=-1, keepdims=True)
                weights = jnp.exp(scores - top)
                total = jnp.sum(weights, axis=-1, keepdims=True)
                probs_ref[head, rows, :] = (weights * (1.0 / total)).astype(bf16)
        mixed = [mm(probs_ref[2 * sub + k], vals[sub]) for k in range(2)]
        at = pl.multiple_of((pair * ABREAST + sub) * LANES, LANES)
        mixed_ref[:, pl.ds(at, LANES)] = jnp.where(low_half, mixed[0], mixed[1]).astype(bf16)


def after_kernel(
    experts, mixed_ref, perm_get, own_ref, oth_ref, x_get, dm_get,
    after_out, low_out, send_out, gain_out, mixed_out,
    stage,
):
    half = own_ref.shape[0]
    width = mixed_ref.shape[1]
    perm = perm_get()[...]
    mixed = mm(mixed_ref[...], perm).astype(bf16)
    mixed_out.ref[...] = mixed
    mixed_out.send()
    block = width + (experts // LANES) * LANES
    lanes = jnp.transpose(
        jnp.concatenate(
            [own_ref[:, block : block + LANES].astype(f32), oth_ref[:, block : block + LANES].astype(f32)],
            axis=0,
        )
    )
    at = experts % LANES
    gain = mm_nt(jnp.broadcast_to(lanes[at : at + 1, :], (8, width)).astype(bf16), perm)
    gain_out.ref[...] = gain
    gain_out.send()
    after = x_get()[...].astype(f32) + (
        mm(mixed[:, :half], own_ref[:, :width]) + mm(mixed[:, half:], oth_ref[:, :width])
    )
    after_out.ref[...] = after
    after_out.send()
    low = (after * inverse_rms(after) * gain[0:1, :]).astype(bf16)
    low_out.ref[...] = low
    low_out.send()
    to_slab(mm(dm_get()[...], low), stage, send_out.ref)


def between_kernel(
    mixed_get, normed_get, own_ref, oth_ref, perm_get, qkv_get,
    mixed_t_out, normed_t_out, wo_out, router_out, query_t_out,
):
    mixed_t_out.ref[...] = jnp.transpose(mixed_get()[...].astype(f32)).astype(bf16)
    mixed_t_out.send()
    normed_t_out.ref[...] = jnp.transpose(normed_get()[...].astype(f32)).astype(bf16)
    normed_t_out.send()
    half = own_ref.shape[0]
    perm = perm_get()[...]
    rest = (mm(perm[:, :half], own_ref[...]) + mm(perm[:, half:], oth_ref[...])).astype(bf16)
    width = wo_out.ref.shape[1]
    wo_out.ref[...] = rest[:, :width]
    router_out.ref[...] = rest[:, width:]
    wo_out.send()
    qkv_ref = qkv_get()
    for c in range(PAIRS):
        query = qkv_ref[:, c * BLOCK : c * BLOCK + LANES].astype(f32)
        query_t_out.ref[c * LANES : (c + 1) * LANES, :] = jnp.transpose(query).astype(bf16)


def early_expert_kernel(recv_ref, win_ref, wout_ref, cot_ref, win_low_ref, wout_low_ref, g_ref, stage):
    slots = cot_ref.shape[0]

    @pl.when(pl.program_id(0) == 0)
    def _():
        def put(c, values):
            cot_ref[:, c * LANES : (c + 1) * LANES] = values.astype(bf16)

        from_slab(recv_ref, stage, slots, put)

    win_low_ref[0] = win_ref[0].astype(bf16)
    wout = wout_ref[0].astype(bf16)
    wout_low_ref[...] = wout
    g_ref[0] = mm_nt(cot_ref[...], wout).astype(bf16)


def activate(pre):
    squared = pre * pre
    bent = jnp.tanh(pre * (gelu_coef + (gelu_coef * cubic_coef) * squared))
    rise = 0.5 + 0.5 * bent
    value = pre * rise
    slope = rise + (value - value * rise) * (
        2.0 * gelu_coef + (6.0 * gelu_coef * cubic_coef) * squared
    )
    return value, slope


def expert_kernel(
    experts, steps,
    me_ref, recv_ref, router_hbm, cot_hbm, win_hbm, wout_hbm, g_hbm,
    back_hbm, made_hbm, x_hbm, rows_hbm, glog_hbm, gate_hbm,
    stage, router_ref, cot_ref, win_ref, wout_ref, g_ref, hidden_ref, act_ref,
    back_ref, made_ref, x_ref, rows_ref, glog_ref, gate_ref, in_sems, out_sems,
):
    slots, width = x_ref.shape
    units = win_ref.shape[1] // steps
    parts = [slice(i * units, (i + 1) * units) for i in range(steps)]
    fetch = [(router_hbm, router_ref), (cot_hbm, cot_ref)]
    fetch += [(win_hbm.at[i], win_ref.at[:, p]) for i, p in enumerate(parts)]
    fetch += [(g_hbm.at[i], g_ref.at[:, p]) for i, p in enumerate(parts)]
    fetch += [(wout_hbm.at[p, :], wout_ref.at[p, :]) for p in parts]
    copies = [pltpu.make_async_copy(a, b, in_sems.at[i]) for i, (a, b) in enumerate(fetch)]
    stores = [
        pltpu.make_async_copy(a, b, out_sems.at[i])
        for i, (a, b) in enumerate(
            (
                (back_ref, back_hbm), (made_ref, made_hbm), (x_ref, x_hbm),
                (rows_ref, rows_hbm), (glog_ref, glog_hbm), (gate_ref, gate_hbm),
            )
        )
    ]
    sequence = [0, 2, 2 + steps, 3, 3 + steps]
    for i in sequence:
        copies[i].start()

    def put(c, values):
        x_ref[:, c * LANES : (c + 1) * LANES] = values.astype(bf16)

    from_slab(recv_ref, stage, slots, put)
    stores[2].start()
    copies[0].wait()
    router = router_ref[...]
    wide = router.shape[1]
    logits = mm(x_ref[...], router)
    for step, part in enumerate(parts):
        if step + 2 < steps:
            copies[4 + step].start()
            copies[4 + step + steps].start()
        else:
            for i in range(steps // 2):
                copies[2 + 2 * steps + (step + 2 - steps) * (steps // 2) + i].start()
        if step == steps - 1:
            copies[1].start()
        copies[2 + step].wait()
        copies[2 + step + steps].wait()
        value, slope = activate(mm(x_ref[...], win_ref[:, part]))
        hidden_ref[:, part] = value.astype(bf16)
        act_ref[:, part] = (g_ref[:, part].astype(f32) * slope).astype(bf16)
    for step in range(steps):
        copies[2 + 2 * steps + step].wait()
    produced = mm(hidden_ref[...], wout_ref[...]).astype(bf16)
    made_ref[...] = produced
    stores[1].start()
    lane = lax.broadcasted_iota(jnp.int32, (slots, wide), 1)
    logits = jnp.where(lane < experts, logits, -jnp.inf)
    weights = jnp.exp(logits - jnp.max(logits, axis=-1, keepdims=True))
    probs = weights / jnp.sum(weights, axis=-1, keepdims=True)
    own = (lane == me_ref[0]).astype(f32)
    gate = jnp.sum(probs * own, axis=-1, keepdims=True)
    gate_ref[...] = jnp.broadcast_to(gate, (slots, LANES))
    stores[5].start()
    copies[1].wait()
    cot = cot_ref[...].astype(f32)
    rows_ref[...] = (gate * cot).astype(bf16)
    stores[3].start()
    grad_gate = jnp.sum(cot * produced.astype(f32), axis=-1, keepdims=True)
    grad_logits = (probs * (own - gate) * grad_gate).astype(bf16)
    glog_ref[...] = grad_logits
    stores[4].start()
    back = (gate * mm_nt(act_ref[...], win_ref[...])).astype(bf16).astype(f32)
    to_slab(back + mm_nt(grad_logits, router), stage, back_ref)
    stores[0].start()
    for copy in stores:
        copy.wait()


def expert_weights_kernel(
    x_ref, rows_ref, glog_ref, gate_ref, made_ref, perm_ref, win_ref, g_ref,
    gin_ref, gout_ref, grouter_ref, prod_ref,
    xt, stage,
):
    @pl.when(pl.program_id(0) == 0)
    def _():
        to_slab(made_ref[...].astype(f32), stage, prod_ref)
        x = x_ref[...]
        xt[...] = jnp.transpose(gate_ref[:, 0:1] * x.astype(f32)).astype(bf16)
        moved = mm(x, perm_ref[...]).astype(bf16)
        grouter_ref[...] = mm_tn(moved, glog_ref[...])

    value, slope = activate(mm(x_ref[...], win_ref[0]))
    act = (g_ref[0].astype(f32) * slope).astype(bf16)
    gout_ref[0] = mm_tn(value.astype(bf16), rows_ref[...])
    gin_ref[0] = mm(xt[...], act)


def output_kernel(experts, recv_ref, dt_get, low_get, router_get, routes_get, after_get, out_out, stage, rows):
    def put(c, values):
        rows[:, c * LANES : (c + 1) * LANES] = values.astype(bf16)

    dt = dt_get()[...]
    from_slab(recv_ref, stage, dt.shape[1], put)
    produced = mm(dt, rows[...])
    logits = mm(low_get()[...], router_get()[...])
    lane = lax.broadcasted_iota(jnp.int32, logits.shape, 1)
    logits = jnp.where(lane < experts, logits, -jnp.inf)
    weights = jnp.exp(logits - jnp.max(logits, axis=-1, keepdims=True))
    own = (lane == routes_get()[...]).astype(f32)
    gate = jnp.sum(weights * own, axis=-1, keepdims=True) / jnp.sum(weights, axis=-1, keepdims=True)
    out_out.ref[...] = (after_get()[...] + gate * produced).astype(bf16)


def norm_two_kernel(
    experts,
    recv_ref, dt_get, after_get, gain_get, cot_get, wo_get, mixed_t_get, perm_get, grouter_get,
    grad_after_out, grad_mixed_ref, keep_ref, send_ref,
    stage, rows,
):
    def put(c, values):
        rows[:, c * LANES : (c + 1) * LANES] = values.astype(bf16)

    slots = recv_ref.shape[0] * LANES // grad_mixed_ref.shape[1]
    from_slab(recv_ref, stage, slots, put)
    grad = mm(dt_get()[...], rows[...])
    after = after_get()[...]
    inverse = inverse_rms(after)
    unit = after * inverse
    scaled = grad * gain_get()[0:1, :]
    back = inverse * (scaled - unit * jnp.mean(scaled * unit, axis=-1, keepdims=True))
    grad_after = cot_get()[...].astype(f32) + back
    grad_after_out.ref[...] = grad_after
    grad_after_out.send()
    low = grad_after.astype(bf16)
    grad_mixed_ref[...] = mm_nt(low, wo_get()[...]).astype(bf16)
    half = keep_ref.shape[0]
    width = low.shape[1]
    mixed_t_ref = mixed_t_get()
    keep_ref[:, :width] = mm(mixed_t_ref[:half, :], low)
    send_ref[:, :width] = mm(mixed_t_ref[half:, :], low).astype(bf16)
    gain_row = jnp.sum(grad * unit, axis=0, keepdims=True)
    high, rest = split_two(jnp.broadcast_to(gain_row, (8, width)))
    perm = perm_get()[...]
    gain_row = (mm(high, perm) + mm(rest, perm))[0:1, :]
    grouter = grouter_get()[...]
    lane = lax.broadcasted_iota(jnp.int32, grouter.shape, 1)
    packed = jnp.where(
        lane < experts, grouter, jnp.where(lane == experts, to_column(gain_row, grouter.shape[1]), 0.0)
    )
    keep_ref[:, width:] = packed[:half]
    send_ref[:, width:] = packed[half:].astype(bf16)


def unskew(skewed):
    span = 4 * LANES
    total = None
    for g in range(LANES // 8):
        moved = pltpu.roll(skewed[8 * g : 8 * g + 8, :], (LANES - 1 - 8 * g) % span, 1)
        total = moved if total is None else total + moved
    turned = jnp.concatenate([total[7 - s : 8 - s, :] for s in range(8)], axis=0)
    turned = pltpu.roll(turned, span - 7, 1, stride=1, stride_axis=0)
    return jnp.sum(turned, axis=0, keepdims=True)


def attend_backward_kernel(
    before, last, qkv_ref, query_t_ref, probs_ref, gm_ref, normed_t_ref, *refs
):
    refs = list(refs)
    vec_in = refs.pop(0) if before else None
    if last:
        hmask_ref, umask_ref = refs.pop(0), refs.pop(0)
    keep_ref, send_ref, dvec_ref, dq_ref, dkv_ref, dp_ref, ds_ref = refs
    pairs_before = 0 if vec_in is None else vec_in.shape[0] // 2
    pair = pl.program_id(0)
    tokens = qkv_ref.shape[0]
    blocks = tokens // LANES
    low_half = lax.broadcasted_iota(jnp.int32, (tokens, LANES), 1) < HEAD_DIM
    lane = lax.broadcasted_iota(jnp.int32, (1, 4 * LANES), 1)
    keys, vals = (qkv_ref[:, k * LANES : (k + 1) * LANES] for k in (1, 2))
    grad = gm_ref[:, pl.ds(pl.multiple_of((pair + pairs_before) * LANES, LANES), LANES)]
    grad_t = jnp.transpose(grad.astype(f32)).astype(bf16)
    dq = []
    for k in range(2):
        keep = low_half if k == 0 else jnp.logical_not(low_half)
        dp_ref[k] = mm_nt(jnp.where(keep, grad, jnp.zeros_like(grad)), vals)
    for k in range(2):
        strip = [None] * 3
        far_left = far_right = None
        for i in range(blocks):
            rows = slice(i * LANES, (i + 1) * LANES)
            dp = dp_ref[k, rows, :]
            probs = probs_ref[k, rows, :].astype(f32)
            delta = jnp.sum(probs * dp, axis=-1, keepdims=True)
            ds = (probs * (dp - delta)).astype(bf16)
            ds_ref[k, rows, :] = ds
            wide = ds.astype(f32)
            for j in range(blocks):
                piece = wide[:, j * LANES : (j + 1) * LANES]
                if j < i - 1:
                    far_left = piece if far_left is None else far_left + piece
                elif j > i + 1:
                    far_right = piece if far_right is None else far_right + piece
                else:
                    at = j - i + 1
                    strip[at] = piece if strip[at] is None else strip[at] + piece
        part = slice(k * HEAD_DIM, (k + 1) * HEAD_DIM)
        dq.append(mm(ds_ref[k], keys))
        dkv_ref[part, :] = mm(query_t_ref[part, :], ds_ref[k]).astype(bf16)
        low_part = slice(LANES + k * HEAD_DIM, LANES + (k + 1) * HEAD_DIM)
        dkv_ref[low_part, :] = mm(grad_t[part, :], probs_ref[k]).astype(bf16)
        vec = unskew(jnp.concatenate(strip + [jnp.zeros((LANES, LANES), f32)], axis=1))
        left = jnp.sum(jnp.sum(far_left, axis=0, keepdims=True), axis=1, keepdims=True)
        right = jnp.sum(jnp.sum(far_right, axis=0, keepdims=True), axis=1, keepdims=True)
        vec = vec + jnp.where(lane == 0, left, 0.0) + jnp.where(lane == 510, right, 0.0)
        dvec_ref[pl.ds((pair + pairs_before) * 2 + k, 1), :] = vec
    dq_ref[...] = (jnp.where(low_half, dq[0], dq[1]) * HEAD_DIM ** (-0.5)).astype(bf16)
    half = keep_ref.shape[0]
    start = pl.multiple_of(pair * BLOCK, LANES)
    queries, rest = pl.ds(start, LANES), pl.ds(start + LANES, 2 * LANES)
    send_ref[:, queries] = mm(normed_t_ref[half:, :], dq_ref[...]).astype(bf16)
    send_ref[:, rest] = mm_nt(normed_t_ref[half:, :], dkv_ref[...]).astype(bf16)
    keep_ref[:, queries] = mm(normed_t_ref[:half, :], dq_ref[...])
    keep_ref[:, rest] = mm_nt(normed_t_ref[:half, :], dkv_ref[...])

    if vec_in is not None:

        @pl.when(pair == 0)
        def _():
            dvec_ref[: 2 * pairs_before, :] = vec_in[...]

    if not last:
        return

    @pl.when(pair == pl.num_programs(0) - 1)
    def _():
        table_col = table_column(
            jnp.concatenate([dvec_ref[...], jnp.zeros((16 - HEADS, 4 * LANES), f32)], axis=0),
            hmask_ref,
            umask_ref,
        )
        lane = lax.broadcasted_iota(jnp.int32, (2 * half, LANES), 1)
        packed = jnp.where(lane == 0, table_col, 0.0)
        end = keep_ref.shape[1] - LANES
        keep_ref[:, end:] = packed[:half]
        send_ref[:, end:] = packed[half:].astype(bf16)


def split_three(values):
    one, rest = split_two(values)
    two, three = split_two(values - one.astype(f32))
    return one, two, three


def table_column(vec, hmask_ref, umask_ref):
    offset = lax.broadcasted_iota(jnp.int32, (LANES, 4 * LANES), 1) - 255
    onehot = (
        lax.broadcasted_iota(jnp.int32, (LANES, 4 * LANES), 0) == buckets_of(offset)
    ).astype(f32).astype(bf16)
    one, two, three = split_three(vec)
    table = mm_nt(one, onehot) + (mm_nt(two, onehot) + mm_nt(three, onehot))
    heads = hmask_ref[:, :16]
    one, two, three = split_three(table)
    spread = mm(heads, one) + (mm(heads, two) + mm(heads, three))
    return jnp.sum(spread * umask_ref[...].astype(f32), axis=1, keepdims=True)


def last_kernel(own_get, oth_get, xperm_get, gain_get, perm_get, after_get, *refs):
    *gets, out_out, grads_ref = refs
    runs = len(gets) // 2
    at = 0
    for dq_get, dkv_get in zip(gets[:runs], gets[runs:]):
        dq, dkv_t = dq_get()[...], dkv_get()
        for c in range(dq.shape[1] // LANES):
            grads_ref[:, at : at + LANES] = dq[:, c * LANES : (c + 1) * LANES]
            moved = jnp.transpose(dkv_t[2 * c * LANES : 2 * (c + 1) * LANES, :].astype(f32))
            grads_ref[:, at + LANES : at + BLOCK] = moved.astype(bf16)
            at += BLOCK
    grads = grads_ref[...]
    cols = slice(0, at)
    grad = jnp.concatenate(
        [mm_nt(grads, own_get()[:, cols]), mm_nt(grads, oth_get()[:, cols])], axis=1
    )
    x = xperm_get()[...].astype(f32)
    inverse = inverse_rms(x)
    unit = x * inverse
    scaled = grad * gain_get()[0:1, :]
    back = inverse * (scaled - unit * jnp.mean(scaled * unit, axis=-1, keepdims=True))
    high, rest = split_two(back)
    perm = perm_get()[...]
    out_out.ref[...] = (after_get()[...] + (mm_nt(high, perm) + mm_nt(rest, perm))).astype(bf16)


def fold_kernel(plan, *refs):
    refs = list(refs)
    total_in = sum(1 + n for members, _ in plan for n in members)
    ins, outs = refs[:total_in], refs[total_in:]
    for members, parts in plan:
        outs_here = [outs.pop(0) for _ in range(parts)]
        at = 0
        for arrived in members:
            total = ins.pop(0)[...]
            for _ in range(arrived):
                total = total + ins.pop(0)[...].astype(f32)
            rows = total.shape[0] // parts
            cols = slice(at, at + total.shape[1])
            at += total.shape[1]
            for m, out in enumerate(outs_here):
                out[:, cols] = total[m * rows : (m + 1) * rows].astype(out.dtype)


def summed(first_ref, moved):
    total = first_ref[...]
    for piece in moved:
        total = total + piece[...].astype(f32)
    return total


def as_row(column):
    size = column.shape[0]
    same = lax.broadcasted_iota(jnp.int32, (size, size), 0) == lax.broadcasted_iota(
        jnp.int32, (size, size), 1
    )
    return jnp.sum(jnp.where(same, column, 0.0), axis=0, keepdims=True)


def finish_kernel(moved_group, gain_get, wq_get, wk_get, wv_get, first_group, first_last, *refs):
    *moved, wo_out, router_out, gain_two_out, wq_out, wk_out, wv_out, gain_out, table_out = refs
    total = summed(first_group, moved[:moved_group])
    width, experts = wo_out.ref.shape[1], router_out.ref.shape[1]
    wo_out.ref[...] = total[:, :width]
    wo_out.send()
    router_out.ref[...] = total[:, width : width + experts]
    router_out.send()
    gain_two_out.ref[...] = as_row(total[:, width + experts : width + experts + 1])
    gain_two_out.send()
    early = RUNS[1]
    sources = [(total, total.shape[1] - early * BLOCK)]
    total = summed(first_last, moved[moved_group:])
    sources.append((total, -early * BLOCK))
    for c in range(PAIRS):
        source, base = sources[c >= early]
        for k, out in enumerate((wq_out, wk_out, wv_out)):
            at = base + c * BLOCK + k * LANES
            out.ref[:, c * LANES : (c + 1) * LANES] = source[:, at : at + LANES]
    for out in (wq_out, wk_out, wv_out):
        out.send()
    products = None
    for get, out in ((wq_get, wq_out), (wk_get, wk_out), (wv_get, wv_out)):
        part = get()[...].astype(bf16).astype(f32) * out.ref[...]
        products = part if products is None else products + part
    gain = gain_get()[...].astype(bf16).astype(f32)
    gain_out.ref[...] = as_row(jnp.sum(products, axis=1, keepdims=True)) / gain
    at = total.shape[1] - LANES
    entries = table_out.ref.shape[1]
    table_out.ref[...] = as_row(total[:, at : at + 1])[:, :entries]


def join_kernel(*refs):
    *pieces, out_ref, sems = refs
    rows = pieces[0].shape[0]
    copies = [
        pltpu.make_async_copy(p, out_ref.at[pl.ds(i * rows, rows), :], sems.at[i])
        for i, p in enumerate(pieces)
    ]
    for copy in copies:
        copy.start()
    for copy in copies:
        copy.wait()


def join(values, moved, space):
    pieces = [values, *moved]
    if values.shape[0] % 8:
        return jnp.concatenate(pieces, axis=0)
    shape = (len(pieces) * values.shape[0], values.shape[1])
    any_ref = pl.BlockSpec(memory_space=pl.ANY)
    return pl.pallas_call(
        join_kernel,
        out_shape=space(shape, values.dtype),
        in_specs=[any_ref] * len(pieces),
        out_specs=any_ref,
        scratch_shapes=[pltpu.SemaphoreType.DMA((len(pieces),))],
        **parameters(4, 1),
    )(*pieces)


def assemble_kernel(moves, count, *refs):
    sources, outs, sems = refs[:count], refs[count:-1], refs[-1]
    copies = []
    for i, (source, row, rows, col, cols, out, to_row, to_col) in enumerate(moves):
        copies.append(
            pltpu.make_async_copy(
                sources[source].at[pl.ds(row, rows), pl.ds(col, cols)],
                outs[out].at[pl.ds(to_row, rows), pl.ds(to_col, cols)],
                sems.at[i],
            )
        )
    for copy in copies:
        copy.start()
    for copy in copies:
        copy.wait()


def assemble(arrays, outs, moves):
    if any(m[i] % 8 for m in moves for i in (1, 2, 6)):
        made = [jnp.zeros(o.shape, o.dtype) for o in outs]
        for a, row, rows, col, cols, out, to_row, to_col in moves:
            block = arrays[a][row : row + rows, col : col + cols]
            made[out] = lax.dynamic_update_slice(made[out], block, (to_row, to_col))
        return made
    any_ref = pl.BlockSpec(memory_space=pl.ANY)
    return pl.pallas_call(
        functools.partial(assemble_kernel, moves, len(arrays)),
        out_shape=list(outs),
        in_specs=[any_ref] * len(arrays),
        out_specs=[any_ref] * len(outs),
        scratch_shapes=[pltpu.SemaphoreType.DMA((len(moves),))],
        **parameters(4, 1),
    )(*arrays)


def expert_call(experts, steps, slots, width, units, wide):
    slab = (slots * width // LANES, LANES)
    any_ref, vmem_ref = (pl.BlockSpec(memory_space=m) for m in (pl.ANY, pltpu.VMEM))
    outs = [slab, (slots, width), (slots, width), (slots, width), (slots, wide)]
    call = pl.pallas_call(
        functools.partial(expert_kernel, experts, steps),
        out_shape=[far(shape, bf16) for shape in outs] + [far((slots, LANES), f32)],
        in_specs=[pl.BlockSpec(memory_space=pltpu.SMEM), vmem_ref] + [any_ref] * 5,
        out_specs=[any_ref] * 6,
        scratch_shapes=[pltpu.VMEM(slab, f32)]
        + [
            pltpu.VMEM(shape, bf16)
            for shape in (
                (width, wide), (slots, width), (width, units), (units, width),
                (slots, units), (slots, units), (slots, units),
            )
        ]
        + [pltpu.VMEM(shape, bf16) for shape in outs]
        + [
            pltpu.VMEM((slots, LANES), f32),
            pltpu.SemaphoreType.DMA((2 + 3 * steps,)),
            pltpu.SemaphoreType.DMA((6,)),
        ],
        **parameters(52, 18),
    )
    return lambda me, recv, *rest: call(me, recv, *[place(Far(a)) for a in rest])


def shards(
    count,
    inputs,
    segment_ids,
    routes,
    cotangent,
    gain_attn,
    gain_ffn,
    bias_table,
    w_query,
    w_key,
    w_value,
    w_output,
    w_router,
    w_in,
    w_out,
):
    tokens, width = inputs.shape
    experts = w_router.shape[1]
    rows_local = w_query.shape[0]
    entries = bias_table.shape[0]
    hidden_units = w_in.shape[2]
    capacity = max(2, 5 * tokens // (4 * experts))
    slots = experts * capacity
    blocks = width // LANES
    half = width // 2
    wide = -(-(experts + 1) // LANES) * LANES
    me = lax.axis_index("seq").astype(jnp.int32).reshape(1)
    vmem = pl.BlockSpec(memory_space=pltpu.VMEM)

    groups = bit_groups(count)
    levels = list(reversed(groups[1:]))
    columns = PAIRS * BLOCK
    piece, tail = flat_call(
        functools.partial(pack_kernel, experts),
        [near((rows_local, columns + LANES), bf16), near((rows_local, width + wide), bf16)],
        us=1,
    )(
        *map(Far, (gain_attn[None, :], gain_ffn[None, :], bias_table[None, :])),
        *map(Far, (w_query, w_key, w_value, w_output, w_router)),
    )

    def reach(values, low_bit, bits):
        return [swap(values, m << low_bit, count) for m in range(1, 1 << bits)]

    order = np.asarray(relative_order(count), np.int32)
    rel_row = jnp.asarray(np.repeat(order, rows_local)[None, :])
    off_row = jnp.asarray(np.tile(np.arange(rows_local, dtype=np.int32), count)[None, :])
    slab = (slots * blocks, LANES)
    slab_stage = pltpu.VMEM(slab, f32)
    perm, xperm, segrow, segcol, hmask, umask, dt, dm = flat_call(
        functools.partial(prepare_kernel, rows_local, entries, experts, capacity),
        [
            far((width, width), bf16),
            far((tokens, width), bf16),
            far((8, tokens), f32),
            far((tokens, LANES), f32),
            far((width, LANES), bf16),
            far((width, LANES), bf16),
            far((tokens, slots), bf16),
            far((slots, tokens), bf16),
        ],
        us=8,
    )(me, Far(rel_row), Far(off_row), Far(inputs), Far(segment_ids), Far(routes))
    cot_send = flat_call(dispatch_kernel, [far(slab, bf16)], us=3, scratch=[slab_stage])(
        Far(dm), Far(cotangent)
    )[0]

    moved = reach(piece, *levels[0])
    moved = lax.optimization_barrier((*moved, perm))[:-1]
    total = columns + LANES
    sizes = (columns // 2, total - columns // 2)
    starts = (0, sizes[0])
    rows = rows_local
    pieces = [piece, *moved]
    moves = [
        (i, 0, rows, starts[p], sizes[p], p, i * rows, 0) for i in range(len(pieces)) for p in range(2)
    ]
    rows *= len(pieces)
    parts = assemble(pieces, [near((rows, size), bf16) for size in sizes], moves)
    for k, (low_bit, _) in enumerate(levels[1:]):
        steps_of = ((2 << low_bit, 1 << low_bit), (1 << low_bit, 2 << low_bit))
        got = [swap(part, d[0], count) for part, d in zip(parts, steps_of)]
        tail_moved = reach(after(tail, *parts, cot_send), *levels[k])
        got = lax.optimization_barrier((*got, cot_send))[:-1]
        moves = [(p + 2 * i, 0, rows, 0, sizes[p], p, i * rows, 0) for i in range(2) for p in range(2)]
        parts = assemble(
            [*parts, *got], [near((2 * rows, size), bf16) for size in sizes], moves
        )
        got = [swap(part, d[1], count) for part, d in zip(parts, steps_of)]
        got = lax.optimization_barrier((*got, *tail_moved))[:2]
        tail = join(tail, tail_moved, near)
        final = k == len(levels) - 2
        order_of = (((0, 2), (1, 3)), ((0, 1), (2, 3)))
        moves = [
            (p + 2 * i, b * rows, rows, 0, sizes[p], 0 if final else p, order_of[p][i][b] * rows,
             starts[p] if final else 0)
            for i in range(2) for p in range(2) for b in range(2)
        ]
        outs = [far((4 * rows, total), bf16)] if final else [near((4 * rows, size), bf16) for size in sizes]
        parts = assemble([*parts, *got], outs, moves)
        rows *= 4
    piece = parts[0]
    other = swap(piece, 1, count)
    tail_moved = reach(after(tail, piece), *levels[-1])

    slab_split = (count, slots * blocks // count, LANES)

    def exchange(rows):
        return lax.all_to_all(
            rows.reshape(slab_split), "seq", split_axis=0, concat_axis=0, tiled=True
        ).reshape(slab)

    cot_recv = exchange(after(cot_send, other))

    def whole(shape):
        return pl.BlockSpec(shape, lambda i: (0,) * len(shape))

    pair_probs = pl.BlockSpec((2 * ABREAST, tokens, tokens), lambda i: (i, 0, 0))
    piece, other = Far(piece), Far(other)
    small_block = pl.BlockSpec((half, LANES), lambda i: (0, columns // LANES))
    pair_weights = pl.BlockSpec((half, ABREAST * BLOCK), lambda i: (0, i))
    qkv, probs, mixed, normed, gain_one = grid_call(
        attend_forward_kernel,
        [
            far((tokens, PAIRS * BLOCK), bf16),
            far((HEADS, tokens, tokens), bf16),
            near((tokens, width), bf16),
            far((tokens, width), bf16),
            far((8, width), f32),
        ],
        grid=(PAIRS // ABREAST,),
        in_specs=[whole((tokens, width))]
        + [pair_weights, pair_weights, small_block, small_block]
        + [whole(shape) for shape in ((width, LANES), (width, LANES), (8, tokens), (tokens, LANES))],
        out_specs=[
            pl.BlockSpec((tokens, ABREAST * BLOCK), lambda i: (0, i)),
            pair_probs,
            vmem,
            whole((tokens, width)),
            whole((8, width)),
        ],
        scratch=[
            pltpu.VMEM((16, 4 * LANES), f32),
            pltpu.VMEM((2 * ABREAST, tokens, tokens), f32),
            pltpu.VMEM((2 * ABREAST, LANES, 3 * LANES), f32),
        ],
        us=14,
    )(
        Far(after(xperm, tail)), piece, other, piece, other,
        *map(Far, (hmask, umask, segrow, segcol)),
    )
    tail_moved = lax.optimization_barrier((*tail_moved, mixed))[:-1]
    tail = join(tail, tail_moved, near)
    tail_other = swap(tail, 1, count)

    after_rows, low_two, row_send, gain_two, mixed_perm = flat_call(
        functools.partial(after_kernel, experts),
        [
            far((tokens, width), f32),
            far((tokens, width), bf16),
            far(slab, bf16),
            far((8, width), f32),
            far((tokens, width), bf16),
        ],
        us=6,
        scratch=[slab_stage],
    )(mixed, Far(perm), tail, tail_other, Far(inputs), Far(dm))
    row_recv = exchange(row_send)

    steps = 6
    units = hidden_units // steps
    weight_in = pl.BlockSpec((1, width, units), lambda i: (0, 0, i))
    weight_out = pl.BlockSpec((1, units, width), lambda i: (0, i, 0))

    low_in = pl.BlockSpec((1, width, units), lambda i: (i, 0, 0))
    low_out = pl.BlockSpec((units, width), lambda i: (i, 0))
    slot_units = pl.BlockSpec((1, slots, units), lambda i: (i, 0, 0))
    cot_rows, win_low, wout_low, grad_hidden = grid_call(
        early_expert_kernel,
        [
            far((slots, width), bf16),
            far((steps, width, units), bf16),
            far((hidden_units, width), bf16),
            far((steps, slots, units), bf16),
        ],
        grid=(steps,),
        in_specs=[whole(slab), weight_in, weight_out],
        out_specs=[whole((slots, width)), low_in, low_out, slot_units],
        us=13,
        scratch=[slab_stage],
    )(cot_recv, Far(w_in), Far(w_out))
    mixed_t, normed_t, output_w, router_w, query_t = flat_call(
        between_kernel,
        [
            far((width, tokens), bf16),
            far((width, tokens), bf16),
            far((width, width), bf16),
            far((width, wide), bf16),
            far((width, tokens), bf16),
        ],
        us=7,
    )(Far(mixed_perm), Far(normed), tail, tail_other, Far(perm), Far(qkv))
    back_send, made, x_rows, grad_rows, grad_logits, gates = expert_call(
        experts, steps, slots, width, hidden_units, wide
    )(me, row_recv, router_w, cot_rows, win_low, wout_low, grad_hidden)
    back_recv = exchange(back_send)
    grad_inner, grad_outer, grad_router, prod_send = grid_call(
        expert_weights_kernel,
        [
            far((1, width, hidden_units), f32),
            far((1, hidden_units, width), f32),
            far((width, wide), f32),
            far(slab, bf16),
        ],
        grid=(steps,),
        in_specs=[
            whole((slots, width)),
            whole((slots, width)),
            whole((slots, wide)),
            whole((slots, LANES)),
            whole((slots, width)),
            whole((width, width)),
            low_in,
            slot_units,
        ],
        out_specs=[weight_in, weight_out, whole((width, wide)), whole(slab)],
        us=19,
        scratch=[pltpu.VMEM((width, slots), bf16), slab_stage],
    )(*map(Far, (x_rows, grad_rows, grad_logits, gates, made, perm, win_low, grad_hidden)))
    prod_recv = exchange(prod_send)

    row_scratch = pltpu.VMEM((slots, width), bf16)
    grad_after, grad_mixed, keep_o, send_o = flat_call(
        functools.partial(norm_two_kernel, experts),
        [
            far((tokens, width), f32),
            near((tokens, width), bf16),
            near((half, width + wide), f32),
            near((half, width + wide), bf16),
        ],
        us=1,
        scratch=[slab_stage, row_scratch],
    )(
        back_recv,
        *map(Far, (dt, after_rows, gain_two, cotangent, output_w, mixed_t, perm, grad_router)),
    )

    def backward(run, ready):
        start, stop = RUNS[run], RUNS[run + 1]
        last = stop == PAIRS
        vec = before.get("vec")
        here = [Far(qkv), Far(query_t), Far(probs), after(grad_mixed, *ready), Far(normed_t)]
        specs = [
            pl.BlockSpec((tokens, BLOCK), lambda i: (0, i + start)),
            pl.BlockSpec((LANES, tokens), lambda i: (i + start, 0)),
            pl.BlockSpec((2, tokens, tokens), lambda i: (i + start, 0, 0)),
            vmem,
            whole((width, tokens)),
        ]
        if vec is not None:
            here.append(vec)
            specs.append(vmem)
        if last:
            here += [Far(hmask), Far(umask)]
            specs += [whole((width, LANES))] * 2
        pairs = stop - start
        cols = pairs * BLOCK + (LANES if last else 0)
        keep, send, vec, dq, dkv_t = grid_call(
            functools.partial(attend_backward_kernel, vec is not None, last),
            [
                near((half, cols), f32),
                near((half, cols), bf16),
                near((2 * stop, 4 * LANES), f32),
                far((tokens, pairs * LANES), bf16),
                far((2 * pairs * LANES, tokens), bf16),
            ],
            grid=(pairs,),
            in_specs=specs,
            out_specs=[
                vmem,
                vmem,
                vmem,
                pl.BlockSpec((tokens, LANES), lambda i: (0, i)),
                pl.BlockSpec((2 * LANES, tokens), lambda i: (i, 0)),
            ],
            scratch=[
                pltpu.VMEM((2, tokens, tokens), f32),
                pltpu.VMEM((2, tokens, tokens), bf16),
            ],
            us=(1, 4)[run],
            vmem=24,
        )(*here)
        before.update(vec=vec)
        born.append((keep, send))
        grads.append((dq, dkv_t))
        return keep

    def results(ready):
        return flat_call(
            functools.partial(output_kernel, experts),
            [far((tokens, width), bf16)],
            us=0.001,
            scratch=[slab_stage, row_scratch],
            vmem=20,
        )(after(prod_recv, *ready), *map(Far, (dt, low_two, router_w, routes, after_rows)))[0]

    def finish(ready):
        return flat_call(
            last_kernel,
            [far((tokens, width), bf16)],
            us=8,
            scratch=[pltpu.VMEM((tokens, columns), bf16)],
            vmem=32,
        )(
            piece, other, Far(after(xperm, *ready)),
            *map(Far, (gain_one, perm, grad_after)),
            *[Far(g[0]) for g in grads], *[Far(g[1]) for g in grads],
        )[0]

    before, born, grads = {}, [(keep_o, send_o)], []
    ups = groups[1:]
    core = (1, 2)
    first = (1 << ups[0][0], 1 << ups[0][1])
    direct = [(1 << low_bit, 1 << bits) for low_bit, bits in ups[1:]]
    halving = [(1 << (low_bit + b), 2) for low_bit, bits in ups[1:] for b in reversed(range(bits))]
    plans = {c: {c: core, c + 1: first} for c in range(3)}
    plans[2].update({4 + i: step for i, step in enumerate(direct)})
    plans[3] = {3 + i: step for i, step in enumerate(halving)}
    work = {run: [functools.partial(backward, run)] for run in range(2)}
    work.update({2: [results], 3: [finish]})
    own, going, flight, finished = {}, {}, {}, {}
    output = grad_inputs = None
    end = max(max(plan) for plan in plans.values())
    own[0], going[0] = born[0][0], [born[0][1]]
    for slot in range(end + 1):
        for c, plan in plans.items():
            if slot in plan:
                distance, parts = plan[slot]
                flight[c] = [swap(g, (m + 1) * distance, count) for m, g in enumerate(going[c])]
        ready = [own[c] for c in flight] + ([prod_recv] if slot == 2 else [])
        for step in work.get(slot, []):
            value = step(ready)
            ready = [value]
            if step is results:
                output = value
            if step is finish:
                grad_inputs = value
        if slot in work:
            for c in flight:
                flight[c] = list(lax.optimization_barrier((*flight[c], value))[:-1])
        folds, args, outs, cut = [], [], [], []

        def fold(members, following, name):
            parts = following[1]
            folds.append(([len(flight[c]) if c in flight else 0 for c in members], parts))
            rows = own[members[0]].shape[0] // parts
            cols = sum(own[c].shape[1] for c in members)
            for c in members:
                args.append(own[c])
                args.extend(flight.pop(c, []))
            outs.append(near((rows, cols), f32))
            outs.extend([near((rows, cols), bf16)] * (parts - 1))
            cut.append((name, parts))

        if slot == 2:
            fold([0, 1], plans[3][3], 3)
        for c in list(flight):
            following = plans[c].get(slot + 1)
            if following or c < 2:
                fold([c], following or (0, 1), c)
            else:
                finished[c] = [own[c], *flight.pop(c)]
        if folds:
            folded = list(
                flat_call(functools.partial(fold_kernel, folds), outs, us=1, vmem=16)(*args)
            )
            for c, parts in cut:
                own[c] = folded.pop(0)
                going[c] = [folded.pop(0) for _ in range(parts - 1)]
            if len(born) == slot + 2:
                own[slot + 1] = born[-1][0]
                going[slot + 1] = [after(born[-1][1], own[cut[0][0]])]

    def row(size):
        return far((1, size), f32)

    square = far((rows_local, width), f32)
    grad_wo, grad_wr, grad_gain_two, grad_q, grad_k, grad_v, grad_gain_one, grad_table = flat_call(
        functools.partial(finish_kernel, len(finished[3]) - 1),
        [square, far((rows_local, experts), f32), row(rows_local)]
        + [square, square, square, row(rows_local), row(entries)],
        us=2,
        vmem=16,
    )(
        *map(Far, (gain_attn[None, :], w_query, w_key, w_value)),
        finished[3][0], finished[2][0], *finished[3][1:], *finished[2][1:],
    )

    return (
        output,
        grad_inputs,
        grad_gain_one[0],
        grad_gain_two[0],
        grad_table[0],
        grad_q,
        grad_k,
        grad_v,
        grad_wo,
        grad_wr,
        grad_inner,
        grad_outer,
    )


def solution(mesh):
    row, flat, cube = P("seq", None), P("seq"), P("seq", None, None)
    in_specs = (row,) * 4 + (flat,) * 3 + (row,) * 5 + (cube,) * 2
    out_specs = (row,) * 2 + (flat,) * 3 + (row,) * 5 + (cube,) * 2
    return jax.shard_map(
        functools.partial(shards, mesh.shape["seq"]),
        mesh=mesh,
        in_specs=in_specs,
        out_specs=out_specs,
        check_vma=False,
    )
```
